32 devices in a mesh: dp: 8 (over z, y), tensor: 4 (over x, core).
Axes of the slice: x: 2, y: 2, z: 4, core: 2. Of those that a mesh axis runs over, the one named last changes fastest.
Arguments:
- tokens: bfloat16 [24, 4, 128, 1024], P(None, 'tensor', 'dp'), may hold values from -6 to 6
- cotangent: bfloat16 [24, 4, 128, 1024], P(None, 'tensor', 'dp'), may hold values from -6 to 6
- lengths: int32 [24], replicated, may hold values from 1 to 512, 10752 in all
- order: int32 [24], replicated, may hold values from 0 to 23, each once
- triple_weight: bfloat16 [3, 1024, 1024], P(None, 'dp', 'tensor'), may hold values from -0.1875 to 0.1875
- output_weight: bfloat16 [1024, 1024], P(None, 'dp'), may hold values from -2 to 2
- expand_weight: bfloat16 [1024, 4096], P('dp', 'tensor'), may hold values from -0.1875 to 0.1875
- shrink_weight: bfloat16 [4096, 1024], P('tensor', 'dp'), may hold values from -0.09375 to 0.09375
- biases: bfloat16 [6, 1024], P(None, 'dp'), may hold values from -3 to 3
- gains: bfloat16 [2, 1024], P(None, 'dp'), may hold values from 0.25 to 1.75
- expand_bias: bfloat16 [4096], P('dp'), may hold values from -3 to 3
Outputs:
- mixed: bfloat16 [24, 4, 128, 1024], P(None, 'tensor', 'dp')
- input_grad: bfloat16 [24, 4, 128, 1024], P(None, 'tensor', 'dp')
- triple_grad: float32 [3, 1024, 1024], P(None, 'dp', 'tensor')
- output_grad: float32 [1024, 1024], P('tensor', 'dp')
- expand_grad: float32 [1024, 4096], P('dp', 'tensor')
- shrink_grad: float32 [4096, 1024], P('tensor', 'dp')
- biases_grad: float32 [6, 1024], P(None, 'dp')
- gains_grad: float32 [2, 1024], P(None, 'dp')
- expand_bias_grad: float32 [4096], P('dp')
The draws below stay inside these ranges and needn't reach their ends.
Inputs may be any that keep to these rules, and one draw needn't show every extreme that they name: lengths[i] counts the valid leading positions of sequence i; the longest is exactly 512. `order`: a permutation of the sequence numbers.
All inputs are finite; a program needn't handle non-finite values.
Results may differ from the reference program's by a relative error of at most 0.02.
Values may be sent and summed in bfloat16 or wider, within the bound.
A program may use at most 128 MiB of HBM per device.

```python
import math
import jax
import jax.numpy as jnp
import numpy as np
from jax import lax

D = 1024
HEADS = 16
HEAD_DIM = 64
FF = 4096
SEQ_LEN = 512
NSEQ = 24
QUARTER = 128
N_TENSOR = 4


def level_of(rng, dims, shards, smallest, high):
    factor_of = 1.0
    for dim, shards_of in shards:
        heights = jax.random.uniform(jax.random.fold_in(jax.random.fold_in(rng, 6), dim), (shards_of,), jnp.float32, smallest / len(shards), high / len(shards))
        factor_of = factor_of * jnp.repeat(jnp.exp(heights), dims[dim] // shards_of).reshape((-1,) + (1,) * (len(dims) - 1 - dim))
    return factor_of


def length_profile(number_of, total, reach, lean):
    loads = [(1 << 20) // math.isqrt(grade ** lean) + 1 for grade in range(2, number_of + 1)]
    spare, holding = total - reach - (number_of - 1), [1] * (number_of - 1)
    while spare > 0:
        candidates = [i for i in range(number_of - 1) if holding[i] < reach]
        whole, budget = sum([loads[i] for i in candidates]), spare
        for i in candidates:
            more = min(reach - holding[i], max(1, budget * loads[i] // whole), spare)
            holding[i] = holding[i] + more
            spare = spare - more
    return np.array([reach] + holding)


def ragged(key, amount, total, most, lean):
    if amount == 2:
        one = jax.random.randint(key, (), max(1, total - most), min(most, total - 1) + 1)
        return jnp.stack([one, total - one])
    sizes = jnp.asarray(length_profile(amount, total, most, lean), jnp.int32)
    pairs = (amount - 1) // 2
    giver, taker = sizes[1:1 + 2 * pairs:2], sizes[2:2 + 2 * pairs:2]
    room = jnp.minimum(giver - 1, most - taker)
    shifted = jax.random.randint(jax.random.fold_in(key, 1), (pairs,), 0, 1 << 20) % (room + 1)
    sizes = sizes.at[1:1 + 2 * pairs:2].set(giver - shifted).at[2:2 + 2 * pairs:2].set(taker + shifted)
    return sizes[jax.random.permutation(jax.random.fold_in(key, 2), amount)]


def gaussian(stream_key, dims, scale, limit, shards=(), held_as=jnp.bfloat16):
    entries = jax.random.normal(stream_key, dims, jnp.float32) * scale
    if len(shards) > 0:
        entries = level_of(stream_key, dims, shards, -0.22, 0.18) * entries
    return jnp.clip(entries, min=-limit, max=limit).astype(held_as)


def setup_inputs(seed: int = 0) -> dict:
    streams_of = jax.random.split(jax.random.key(seed), 12)
    tokens = gaussian(streams_of[0], (NSEQ, N_TENSOR, QUARTER, D), 1.0, 6.0, ((1, 4), (2, 8)))
    cotangent = gaussian(streams_of[1], (NSEQ, N_TENSOR, QUARTER, D), 1.0, 6.0, ((1, 4), (2, 8)))
    lengths = ragged(streams_of[2], NSEQ, NSEQ * SEQ_LEN * 7 // 8, SEQ_LEN, 0).astype(jnp.int32)
    order = jax.random.permutation(streams_of[3], NSEQ).astype(jnp.int32)
    triple_weight = gaussian(streams_of[4], (3, D, D), D ** -0.5, 0.1875, ((1, 8), (2, 4)))
    output_weight = gaussian(streams_of[5], (D, D), (max(D // 128, 2)) ** -0.5, 2.0, ((1, 8),))
    expand_weight = gaussian(streams_of[6], (D, FF), D ** -0.5, 0.1875, ((0, 8), (1, 4)))
    shrink_weight = gaussian(streams_of[7], (FF, D), FF ** -0.5, 0.09375, ((0, 4), (1, 8)))
    biases = gaussian(streams_of[8], (6, D), 0.5, 3.0, ((1, 8),))
    gains = jnp.clip(1.0 + 0.15 * jax.random.normal(streams_of[9], (2, D), jnp.float32), 0.25, 1.75).astype(jnp.bfloat16)
    expand_bias = gaussian(streams_of[10], (FF,), 0.5, 3.0, ((0, 8),))
    return dict(tokens=tokens, cotangent=cotangent, lengths=lengths, order=order, triple_weight=triple_weight, output_weight=output_weight, expand_weight=expand_weight, shrink_weight=shrink_weight, biases=biases, gains=gains, expand_bias=expand_bias)


@jax.custom_vjp
def low(v):
    return lax.optimization_barrier(v.astype(jnp.bfloat16)).astype(jnp.float32)

@jax.custom_vjp
def low_back(v):
    return v

def low_keep(v):
    return (low(v), None)

def low_pass(kept, grad):
    return (grad,)

def back_keep(v):
    return (v, None)

def back_low(kept, grad):
    return (low(grad),)
low.defvjp(low_keep, low_pass)
low_back.defvjp(back_keep, back_low)
EPSILON = 1e-12
MASKED = -1e+30
HIGHEST = lax.Precision.HIGHEST

def layer_norm(values, gain, shift):
    center = values - lax.optimization_barrier(jnp.mean(values, axis=-1, keepdims=True))
    spread = lax.optimization_barrier(jnp.mean(center * center, axis=-1, keepdims=True))
    return center * lax.rsqrt(spread + EPSILON) * gain + shift

def gelu_exact(values):
    return 0.5 * values * (1.0 + jax.scipy.special.erf(values / math.sqrt(2.0)))

def single_sequence(seq_item, weights):
    sequence, seq_length = seq_item
    query_key_value_proj, out_weight, widen_projection, shrink, bias_rows, gain_rows, exp_bias = weights
    queries = low_back(low(jnp.dot(sequence, query_key_value_proj[0], precision=HIGHEST) + bias_rows[0]))
    key_rows = low_back(low(jnp.dot(sequence, query_key_value_proj[1], precision=HIGHEST)))
    value_rows = low_back(low(jnp.dot(sequence, query_key_value_proj[2], precision=HIGHEST) + bias_rows[1]))
    shaped = (SEQ_LEN, HEADS, HEAD_DIM)
    raw_scores = jnp.einsum('qhe,khe->hqk', queries.reshape(shaped), key_rows.reshape(shaped), precision=HIGHEST)
    scores = low_back(raw_scores * (1.0 / math.sqrt(HEAD_DIM)))
    visible = jnp.arange(SEQ_LEN) < seq_length
    soft_weights = jax.nn.softmax(jnp.where(visible[None, None, :], scores, MASKED), axis=-1)
    blended = jnp.einsum('hqk,khe->qhe', low(soft_weights), value_rows.reshape(shaped), precision=HIGHEST)
    attended = low_back(low(blended.reshape(SEQ_LEN, D)))
    branch = low_back(jnp.dot(attended, out_weight, precision=HIGHEST)) + bias_rows[2]
    normed = layer_norm(sequence + branch, gain_rows[0], bias_rows[3])
    pre_act = low_back(jnp.dot(low(normed), widen_projection, precision=HIGHEST) + exp_bias)
    hidden = low(gelu_exact(pre_act))
    ff_out = low_back(jnp.dot(hidden, shrink, precision=HIGHEST)) + bias_rows[4]
    return layer_norm(normed + ff_out, gain_rows[1], bias_rows[5])

def reference(tokens, cotangent, lengths, order, triple_weight, output_weight, expand_weight, shrink_weight, biases, gains, expand_bias):
    inverse = jnp.zeros((NSEQ,), jnp.int32).at[order].set(jnp.arange(NSEQ, dtype=jnp.int32))
    inputs = tokens.astype(jnp.float32).reshape(NSEQ, SEQ_LEN, D)[inverse]
    valid = (jnp.arange(SEQ_LEN)[None, :] < lengths[:, None]).astype(jnp.float32)
    seed_grad = cotangent.astype(jnp.float32).reshape(NSEQ, SEQ_LEN, D) * valid[:, :, None]
    params = tuple((weight_arg.astype(jnp.float32) for weight_arg in (triple_weight, output_weight, expand_weight, shrink_weight, biases, gains, expand_bias)))

    def forward(inputs_all, params_all):
        stepper = jax.checkpoint(single_sequence)
        return lax.map(lambda seq_item: stepper(seq_item, params_all), (inputs_all, lengths))
    outputs, pull_back = jax.vjp(forward, inputs, params)
    input_grad, param_grads = pull_back(seed_grad)
    shape_out = (NSEQ, N_TENSOR, QUARTER, D)
    mixed = outputs.reshape(shape_out).astype(jnp.bfloat16)
    back_rows = input_grad[order].reshape(shape_out).astype(jnp.bfloat16)
    return (mixed, back_rows, param_grads[0], param_grads[1], param_grads[2], param_grads[3], param_grads[4], param_grads[5], param_grads[6])
```

```python
import functools
import math
import types

import jax
import jax.numpy as jnp
from jax import lax
from jax.experimental import pallas as pl
from jax.experimental.pallas import tpu as pltpu
from jax.sharding import PartitionSpec as P

HEAD_DIM = 64


EPSILON = 1e-12
MASKED = -1e30


def normalize(values, gain, shift):
    center = values - jnp.mean(values, axis=-1, keepdims=True)
    spread = jnp.mean(center * center, axis=-1, keepdims=True)
    inv_std = lax.rsqrt(spread + EPSILON)
    scaled = center * inv_std
    return (scaled * gain + shift, scaled, inv_std)


def normalize_back(grad_rows, scaled, inv_std, gain):
    pushed = grad_rows * gain
    first = jnp.mean(pushed, axis=-1, keepdims=True)
    second = jnp.mean(pushed * scaled, axis=-1, keepdims=True)
    return inv_std * (pushed - first - scaled * second)


def gelu_exact(values):
    return 0.5 * values * (1.0 + jax.scipy.special.erf(values / math.sqrt(2.0)))


def gelu_slope(values):
    return 0.5 * (1.0 + jax.scipy.special.erf(values / math.sqrt(2.0))) + values * jnp.exp(
        -0.5 * values * values
    ) / math.sqrt(2.0 * math.pi)


def split_heads(rows):
    return rows.reshape(rows.shape[0], rows.shape[1] // HEAD_DIM, HEAD_DIM)


def score_block(queries, key_rows, seq_length):
    raw_scores = jnp.einsum("qhe,khe->hqk", queries, key_rows, preferred_element_type=jnp.float32)
    scores = raw_scores * (1.0 / math.sqrt(HEAD_DIM))
    visible = jnp.arange(key_rows.shape[0]) < seq_length
    return jnp.where(visible[None, None, :], scores, MASKED)


def attend(seq_item):
    queries, key_rows, value_rows, seq_length = seq_item
    queries = split_heads(queries)
    key_rows = split_heads(key_rows)
    value_rows = split_heads(value_rows)
    masked = score_block(queries, key_rows, seq_length)
    highest = jnp.max(masked, axis=-1, keepdims=True)
    totals = jnp.sum(jnp.exp(masked - highest), axis=-1, keepdims=True)
    log_totals = highest + jnp.log(totals)
    probs = jnp.exp(masked - log_totals).astype(jnp.bfloat16)
    blended = jnp.einsum("hqk,khe->qhe", probs, value_rows, preferred_element_type=jnp.float32)
    return (blended.astype(jnp.bfloat16).reshape(queries.shape[0], -1), log_totals[..., 0])


def attend_back(seq_item):
    queries, key_rows, value_rows, grad_rows, log_totals, seq_length = seq_item
    queries = split_heads(queries)
    key_rows = split_heads(key_rows)
    value_rows = split_heads(value_rows)
    grad_heads = split_heads(grad_rows)
    masked = score_block(queries, key_rows, seq_length)
    probs = jnp.exp(masked - log_totals[..., None])
    grad_probs = jnp.einsum(
        "qhe,khe->hqk", grad_heads, value_rows, preferred_element_type=jnp.float32
    )
    inner = jnp.sum(probs * grad_probs, axis=-1, keepdims=True)
    grad_scores = (probs * (grad_probs - inner)).astype(jnp.bfloat16)
    score_scale = 1.0 / math.sqrt(HEAD_DIM)
    grad_query = (
        jnp.einsum("hqk,khe->qhe", grad_scores, key_rows, preferred_element_type=jnp.float32)
        * score_scale
    )
    grad_key = (
        jnp.einsum("hqk,qhe->khe", grad_scores, queries, preferred_element_type=jnp.float32)
        * score_scale
    )
    grad_value = jnp.einsum(
        "hqk,qhe->khe", probs.astype(jnp.bfloat16), grad_heads, preferred_element_type=jnp.float32
    )
    row_count = queries.shape[0]
    return (
        grad_query.astype(jnp.bfloat16).reshape(row_count, -1),
        grad_key.astype(jnp.bfloat16).reshape(row_count, -1),
        grad_value.astype(jnp.bfloat16).reshape(row_count, -1),
    )


def plain_body(
    tokens,
    cotangent,
    lengths,
    order,
    triple_weight,
    output_weight,
    expand_weight,
    shrink_weight,
    biases,
    gains,
    expand_bias,
):
    seq_count = order.shape[0]
    per_group = seq_count // lax.axis_size("dp")
    tensor_size = lax.axis_size("tensor")
    member = lax.axis_index("dp")
    my_rank = lax.axis_index("tensor")
    slot_ids = jnp.arange(seq_count, dtype=jnp.int32)
    inverse = jnp.zeros((seq_count,), jnp.int32).at[order].set(slot_ids)
    local_x, local_dy = (
        lax.all_to_all(tokens[inverse], "dp", split_axis=0, concat_axis=2, tiled=True),
        lax.all_to_all(cotangent, "dp", split_axis=0, concat_axis=2, tiled=True),
    )
    quarter = local_x.shape[2]
    model_width = local_x.shape[3]
    full_length = quarter * tensor_size
    my_lengths = lax.dynamic_slice_in_dim(lengths, member * per_group, per_group)
    gathered = (
        lax.all_gather(triple_weight, "dp", axis=1, tiled=True),
        lax.all_gather(output_weight, "dp", axis=1, tiled=True),
        lax.all_gather(expand_weight, "dp", axis=0, tiled=True),
        lax.all_gather(shrink_weight, "dp", axis=1, tiled=True),
        lax.all_gather(biases, "dp", axis=1, tiled=True),
        lax.all_gather(gains, "dp", axis=1, tiled=True),
        lax.all_gather(expand_bias, "dp", axis=0, tiled=True),
    )
    query_key_value_proj, out_weight, widen_projection, shrink, bias_rows, gain_rows, exp_bias = (
        gathered
    )
    head_width = query_key_value_proj.shape[2]
    hidden_width = widen_projection.shape[1]
    out_heads = lax.dynamic_slice_in_dim(out_weight, my_rank * head_width, head_width, 0)
    bias_query = lax.dynamic_slice_in_dim(bias_rows[0], my_rank * head_width, head_width).astype(
        jnp.float32
    )
    bias_value = lax.dynamic_slice_in_dim(bias_rows[1], my_rank * head_width, head_width).astype(
        jnp.float32
    )
    bias_hidden = lax.dynamic_slice_in_dim(exp_bias, my_rank * hidden_width, hidden_width).astype(
        jnp.float32
    )
    bias_stack = jnp.stack([bias_query, jnp.zeros_like(bias_query), bias_value])
    gain_first = gain_rows[0].astype(jnp.float32)
    gain_second = gain_rows[1].astype(jnp.float32)
    full_shape = (per_group, tensor_size, quarter, model_width)
    token_all_rows = lax.all_gather(local_x, "tensor", axis=1, tiled=True).reshape(
        per_group, full_length, model_width
    )
    projected = (
        jnp.einsum(
            "jah,rhu->rjau",
            token_all_rows,
            query_key_value_proj,
            preferred_element_type=jnp.float32,
        )
        + bias_stack[:, None, None, :]
    ).astype(jnp.bfloat16)
    attended, log_totals = lax.map(attend, (projected[0], projected[1], projected[2], my_lengths))
    attn_terms = jnp.einsum(
        "sle,em->slm", attended, out_heads, preferred_element_type=jnp.float32
    ).reshape(full_shape)
    attn_sum = lax.psum_scatter(attn_terms, "tensor", scatter_dimension=1, tiled=True)
    hidden_in = local_x.astype(jnp.float32) + (attn_sum + bias_rows[2].astype(jnp.float32))
    normed, normed_scaled, normed_inv = normalize(
        hidden_in, gain_first, bias_rows[3].astype(jnp.float32)
    )
    normalized_all_rows = lax.all_gather(
        normed.astype(jnp.bfloat16), "tensor", axis=1, tiled=True
    ).reshape(per_group, full_length, model_width)
    pre_act = (
        jnp.einsum(
            "uqj,jt->uqt", normalized_all_rows, widen_projection, preferred_element_type=jnp.float32
        )
        + bias_hidden
    )
    hidden = gelu_exact(pre_act).astype(jnp.bfloat16)
    ffn_terms = jnp.einsum(
        "slf,fm->slm", hidden, shrink, preferred_element_type=jnp.float32
    ).reshape(full_shape)
    ffn_sum = lax.psum_scatter(
        ffn_terms.astype(jnp.bfloat16), "tensor", scatter_dimension=1, tiled=True
    ).astype(jnp.float32)
    total_rows = normed + (ffn_sum + bias_rows[4].astype(jnp.float32))
    output, out_scaled, out_inv = normalize(
        total_rows, gain_second, bias_rows[5].astype(jnp.float32)
    )
    positions = my_rank * quarter + jnp.arange(quarter)
    valid = (positions[None, :] < my_lengths[:, None]).astype(jnp.float32)
    grad_out = local_dy.astype(jnp.float32) * valid[:, None, :, None]
    row_axes = (0, 1, 2)
    gain_grad_second = jnp.sum(grad_out * out_scaled, axis=row_axes)
    shift_grad_second = jnp.sum(grad_out, axis=row_axes)
    grad_total = normalize_back(grad_out, out_scaled, out_inv, gain_second)
    branch_bias_grad = jnp.sum(grad_total, axis=row_axes)
    grad_branch = lax.all_gather(
        grad_total.astype(jnp.bfloat16), "tensor", axis=1, tiled=True
    ).reshape(per_group, full_length, model_width)
    shrink_grad = jnp.einsum("slf,slm->fm", hidden, grad_branch, preferred_element_type=jnp.float32)
    grad_hidden = jnp.einsum("slm,fm->slf", grad_branch, shrink, preferred_element_type=jnp.float32)
    preactivation_grad = (grad_hidden * gelu_slope(pre_act)).astype(jnp.bfloat16)
    hidden_bias_grad = jnp.sum(preactivation_grad, axis=(0, 1), dtype=jnp.float32)
    expand_grad = jnp.einsum(
        "mgc,mga->ca", normalized_all_rows, preactivation_grad, preferred_element_type=jnp.float32
    )
    normed_terms = jnp.einsum(
        "cpk,rk->cpr", preactivation_grad, widen_projection, preferred_element_type=jnp.float32
    ).reshape(full_shape)
    grad_normed = grad_total + lax.psum_scatter(
        normed_terms.astype(jnp.bfloat16), "tensor", scatter_dimension=1, tiled=True
    ).astype(jnp.float32)
    first_norm_gain_grad = jnp.sum(grad_normed * normed_scaled, axis=row_axes)
    shift_grad_first = jnp.sum(grad_normed, axis=row_axes)
    grad_hidden_in = normalize_back(grad_normed, normed_scaled, normed_inv, gain_first)
    out_bias_grad = jnp.sum(grad_hidden_in, axis=row_axes)
    grad_attn = lax.all_gather(
        grad_hidden_in.astype(jnp.bfloat16), "tensor", axis=1, tiled=True
    ).reshape(per_group, full_length, model_width)
    output_grad = jnp.einsum("sle,slm->em", attended, grad_attn, preferred_element_type=jnp.float32)
    grad_blended = jnp.einsum(
        "slm,em->sle", grad_attn, out_heads, preferred_element_type=jnp.float32
    ).astype(jnp.bfloat16)
    grad_query, grad_key, grad_value = lax.map(
        attend_back,
        (projected[0], projected[1], projected[2], grad_blended, log_totals, my_lengths),
    )
    projection_output_grad = jnp.stack([grad_query, grad_key, grad_value])
    query_bias_grad = jnp.sum(grad_query, axis=(0, 1), dtype=jnp.float32)
    value_bias_grad = jnp.sum(grad_value, axis=(0, 1), dtype=jnp.float32)
    triple_grad = jnp.einsum(
        "xyt,vxyu->vtu", token_all_rows, projection_output_grad, preferred_element_type=jnp.float32
    )
    token_terms = jnp.einsum(
        "atpi,aki->tpk",
        projection_output_grad,
        query_key_value_proj,
        preferred_element_type=jnp.float32,
    ).reshape(full_shape)
    grad_tokens = grad_hidden_in + lax.psum_scatter(
        token_terms.astype(jnp.bfloat16), "tensor", scatter_dimension=1, tiled=True
    ).astype(jnp.float32)
    zero_row = jnp.zeros((model_width,), jnp.float32)
    query_full = lax.dynamic_update_slice_in_dim(zero_row, query_bias_grad, my_rank * head_width, 0)
    value_full = lax.dynamic_update_slice_in_dim(zero_row, value_bias_grad, my_rank * head_width, 0)
    bias_grad = jnp.stack(
        [
            query_full,
            value_full,
            out_bias_grad,
            shift_grad_first,
            branch_bias_grad,
            shift_grad_second,
        ]
    )
    gain_grad = jnp.stack([first_norm_gain_grad, gain_grad_second])
    hidden_full = lax.dynamic_update_slice_in_dim(
        jnp.zeros((exp_bias.shape[0],), jnp.float32), hidden_bias_grad, my_rank * hidden_width, 0
    )
    bias_grad, gain_grad, hidden_full = (
        lax.psum(bias_grad.astype(jnp.bfloat16), "tensor").astype(jnp.float32),
        lax.psum(gain_grad.astype(jnp.bfloat16), "tensor").astype(jnp.float32),
        lax.psum(hidden_full.astype(jnp.bfloat16), "tensor").astype(jnp.float32),
    )
    shards = (
        lax.psum_scatter(triple_grad, "dp", scatter_dimension=1, tiled=True),
        lax.psum_scatter(output_grad, "dp", scatter_dimension=1, tiled=True),
        lax.psum_scatter(expand_grad, "dp", scatter_dimension=0, tiled=True),
        lax.psum_scatter(shrink_grad, "dp", scatter_dimension=1, tiled=True),
        lax.psum_scatter(bias_grad, "dp", scatter_dimension=1, tiled=True),
        lax.psum_scatter(gain_grad, "dp", scatter_dimension=1, tiled=True),
        lax.psum_scatter(hidden_full, "dp", scatter_dimension=0, tiled=True),
    )
    mixed_rows, back_rows = (
        lax.all_to_all(output.astype(jnp.bfloat16), "dp", split_axis=2, concat_axis=0, tiled=True),
        lax.all_to_all(
            grad_tokens.astype(jnp.bfloat16), "dp", split_axis=2, concat_axis=0, tiled=True
        ),
    )
    return (
        mixed_rows,
        back_rows[order],
        shards[0],
        shards[1],
        shards[2],
        shards[3],
        shards[4],
        shards[5],
        shards[6],
    )


BF = jnp.bfloat16
F32 = jnp.float32
MESH = pl.DeviceIdType.MESH
LOG2E = math.log2(math.e)
N_SEM = 320
VMEM_BYTES = 64 * 1024 * 1024


def mm(a, b):
    return lax.dot_general(a, b, (((1,), (0,)), ((), ())), preferred_element_type=F32)


def mm_t(a, b):
    return lax.dot_general(a, b, (((1,), (1,)), ((), ())), preferred_element_type=F32)


def t_mm(a, b):
    return lax.dot_general(a, b, (((0,), (0,)), ((), ())), preferred_element_type=F32)


class Links:
    def __init__(self, send_sems, recv_sems, local_sems):
        self.send_sems = send_sems
        self.recv_sems = recv_sems
        self.local_sems = local_sems
        self.slots = {}
        self.flying = {}
        self.local_count = 0

    def slot(self, name):
        return self.slots.setdefault(name, len(self.slots))

    def send(self, name, src, dst, where):
        i = self.slot(name)
        copy = pltpu.make_async_remote_copy(
            src_ref=src,
            dst_ref=dst,
            send_sem=self.send_sems.at[i],
            recv_sem=self.recv_sems.at[i],
            device_id=where,
            device_id_type=MESH,
        )
        copy.start()
        self.flying[name] = copy

    def sent(self, name):
        self.flying.pop(name).wait_send()

    def arrived(self, name, dst, where):
        i = self.slot(name)
        pltpu.make_async_remote_copy(
            src_ref=dst,
            dst_ref=dst,
            send_sem=self.send_sems.at[i],
            recv_sem=self.recv_sems.at[i],
            device_id=where,
            device_id_type=MESH,
        ).wait_recv()

    def local(self, src, dst):
        copy = pltpu.make_async_copy(src, dst, self.local_sems.at[self.local_count])
        self.local_count += 1
        copy.start()
        return copy


def layer_kernel(g, *refs):
    (order_s, inverse_s, lengths_s, tok, cot, w3, wo, we, ws, pack) = refs[:10]
    (out_mixed, out_back, out_g3, out_go, out_ge, out_gs, out_small) = refs[10:17]
    s = types.SimpleNamespace(**dict(zip(g.scratch_names, refs[17:])))
    n_seq, quarter, width = g.n_seq, g.quarter, g.width
    n_dp, n_y, n_t = g.n_dp, g.n_y, g.n_t
    n_z = n_dp // n_y
    full = n_t * quarter
    half = full // 2
    rows = quarter // n_dp
    hw, fw = g.head_width, g.hidden_width
    heads = hw // HEAD_DIM
    dw = width // n_dp
    tile = 256
    ebias_rows = g.ebias_rows
    owners = n_dp // n_t

    d = lax.axis_index("dp")
    t = lax.axis_index("tensor")
    z, y = d // n_y, d % n_y
    x, c = t // 2, t % 2
    t_core = x * 2 + (1 - c)
    t_far = (1 - x) * 2 + c
    t_diag = (1 - x) * 2 + (1 - c)

    def dp_to(o):
        return (d + o) % n_dp

    def dp_from(o):
        return (d + n_dp - o) % n_dp

    def z_to(k):
        return ((z + k) % n_z) * n_y + y

    def z_from(k):
        return ((z + n_z - k) % n_z) * n_y + y

    y_peer = z * n_y + (1 - y)
    link = Links(s.send_sems, s.recv_sems, s.local_sems)

    barrier = pltpu.get_barrier_semaphore()
    for o in range(1, n_dp):
        pl.semaphore_signal(barrier, inc=1, device_id={"dp": dp_to(o)}, device_id_type=MESH)
    for peer in (t_core, t_far, t_diag):
        pl.semaphore_signal(barrier, inc=1, device_id={"tensor": peer}, device_id_type=MESH)

    stage, x_all, cots = s.stage, s.x_all, s.cots
    w3_all, wo_all, we_all, ws_all = s.w3_all, s.wo_all, s.we_all, s.ws_all
    pack_all, vec, ebias = s.pack_all, s.vec, s.ebias
    qkv, att, lse, part = s.qkv, s.att, s.lse, s.part
    r_a, r_b, r_x = s.r_a, s.r_b, s.r_x
    n1, inv1, u_all, hid, slope = s.n1, s.inv1, s.u_all, s.hid, s.slope
    dz, dh, dy, dqkv = s.dz, s.dh, s.dy, s.dqkv
    acc, hacc, qacc = s.acc, s.hacc, s.qacc
    kt, ot, dk_acc, dv_acc, da = s.kt, s.ot, s.dk_acc, s.dv_acc, s.da
    mixed_send, back_send, back_recv = s.mixed_send, s.back_send, s.back_recv

    def al(v, m):
        return pl.multiple_of(v, m)

    def seq_rows(j, start, n):
        return pl.ds(al(j * full + start, 16), n)

    def mine(j):
        return seq_rows(j, t * quarter, quarter)


    def permute(k, carry):
        stage[k] = tok[inverse_s[k]]
        return carry

    lax.fori_loop(0, n_dp * n_seq, permute, 0)
    acc[...] = jnp.zeros_like(acc)
    hacc[...] = jnp.zeros_like(hacc)
    qacc[...] = jnp.zeros_like(qacc)
    pl.semaphore_wait(barrier, n_dp - 1 + 3)

    def x_block(j, src):
        return x_all.at[seq_rows(j, t * quarter + src * rows, rows)]

    def tokens_start(j):
        for o in range(1, n_dp):
            e = dp_to(o)
            link.send(("tok", j, o), stage.at[e * n_seq + j], x_block(j, d), {"dp": e})
        x_all[seq_rows(j, t * quarter + d * rows, rows), :] = stage[d * n_seq + j]

    def tokens_finish(j):
        for o in range(1, n_dp):
            link.arrived(("tok", j, o), x_block(j, dp_from(o)), {"dp": dp_from(o)})
            link.sent(("tok", j, o))

    def cot_block(src):
        return cots.at[:, pl.ds(al(src * rows, 16), rows), :]

    def cot_start():
        for o in range(1, n_dp):
            e = dp_to(o)
            link.send(("cot", o), cot.at[pl.ds(e * n_seq, n_seq)], cot_block(d), {"dp": e})
        own = link.local(cot.at[pl.ds(d * n_seq, n_seq)], cot_block(d))
        return own

    def cot_finish(own):
        own.wait()
        for o in range(1, n_dp):
            link.arrived(("cot", o), cot_block(dp_from(o)), {"dp": dp_from(o)})
            link.sent(("cot", o))

    def cols(ref, e):
        return ref.at[:, pl.ds(al(e * dw, 128), dw)]

    def row_block(ref, e):
        return ref.at[pl.ds(al(e * dw, 16), dw), :]

    gathers = {
        "pack": (pack, lambda e: cols(pack_all, e)),
        "w3": (w3, lambda e: row_block(w3_all, e)),
        "wo": (wo.at[pl.ds(al(t * hw, 16), hw), :], lambda e: cols(wo_all, e)),
        "we": (we, lambda e: row_block(we_all, e)),
        "ws": (ws, lambda e: cols(ws_all, e)),
    }
    own_copies = {}

    def gather_start(name):
        src, block = gathers[name]
        for k in range(1, n_z):
            link.send((name, "z", k), src, block(d), {"dp": z_to(k)})
        link.send((name, "y", 0), src, block(d), {"dp": y_peer})
        own_copies[name] = link.local(src, block(d))

    def gather_forward(name, k):
        _, block = gathers[name]
        e = z_from(k)
        link.arrived((name, "z", k), block(e), {"dp": e})
        link.send((name, "y", k), block(e), block(e), {"dp": y_peer})

    def gather_finish(name):
        _, block = gathers[name]
        own_copies.pop(name).wait()
        for k in range(n_z):
            e = ((z + n_z - k) % n_z) * n_y + (1 - y)
            link.arrived((name, "y", k), block(e), {"dp": y_peer})
        for k in range(1, n_z):
            link.sent((name, "z", k))
        for k in range(n_z):
            link.sent((name, "y", k))


    def t_rows(j, who):
        return seq_rows(j, who * quarter, quarter)

    def ag_start(buf, tag, j):
        own = buf.at[t_rows(j, t)]
        link.send((tag, "far", j), own, own, {"tensor": t_far})
        link.send((tag, "core", j), own, own, {"tensor": t_core})

    def ag_forward(buf, tag, j):
        got = buf.at[t_rows(j, t_far)]
        link.arrived((tag, "far", j), got, {"tensor": t_far})
        link.send((tag, "fwd", j), got, got, {"tensor": t_core})

    def ag_finish(buf, tag, j):
        link.arrived((tag, "core", j), buf.at[t_rows(j, t_core)], {"tensor": t_core})
        link.arrived((tag, "fwd", j), buf.at[t_rows(j, t_diag)], {"tensor": t_core})
        for what in ("far", "core", "fwd"):
            link.sent((tag, what, j))

    def q_rows(j):
        return pl.ds(j * quarter, quarter)

    def rs_start_far(tag, j):
        link.send((tag, "b", j), part.at[t_rows(j, t_diag)], r_b.at[q_rows(j)], {"tensor": t_core})

    def rs_start_near(tag, j):
        link.send((tag, "a", j), part.at[t_rows(j, t_core)], r_a.at[q_rows(j)], {"tensor": t_core})

    def rs_forward(tag, j):
        link.arrived((tag, "b", j), r_b.at[q_rows(j)], {"tensor": t_core})
        far = t_rows(j, t_far)
        both = part[far, :].astype(F32) + r_b[q_rows(j), :].astype(F32)
        part[far, :] = both.astype(BF)
        link.send((tag, "x", j), part.at[far], r_x.at[q_rows(j)], {"tensor": t_far})

    def rs_finish(tag, j):
        link.arrived((tag, "a", j), r_a.at[q_rows(j)], {"tensor": t_core})
        link.arrived((tag, "x", j), r_x.at[q_rows(j)], {"tensor": t_far})
        for what in ("a", "b", "x"):
            link.sent((tag, what, j))

    chunk = 32

    def row_loop(fn):
        lax.fori_loop(0, quarter // chunk, lambda i, carry: fn(i * chunk) or carry, 0)

    def summed(j, r):
        loc = seq_rows(j, t * quarter + r, chunk)
        buf = pl.ds(al(j * quarter + r, 16), chunk)
        return (
            part[loc, :].astype(F32)
            + r_a[buf, :].astype(F32)
            + r_x[buf, :].astype(F32)
        )

    def add_sum(row, value):
        acc[row : row + 1, :] += jnp.sum(value, axis=0, keepdims=True)

    def two_halves(tag, j, fn):
        fn(al(j * full + (1 - x) * half, 16))
        rs_start_far(tag, j)
        fn(al(j * full + x * half, 16))
        rs_start_near(tag, j)

    def by_tiles(n, fn):
        lax.fori_loop(0, n // tile, lambda i, carry: fn(al(i * tile, tile)) or carry, 0)


    def spread_vectors():
        vec[...] = pack_all[...].astype(F32)
        for i in range(owners):
            e = t * owners + i
            for r in range(ebias_rows):
                ebias[0:1, (i * ebias_rows + r) * dw : (i * ebias_rows + r + 1) * dw] = vec[
                    8 + r : 9 + r, pl.ds(al(e * dw, 128), dw)
                ]


    def project(j):
        at = pl.ds(j * full, full)
        for w in range(3):
            span = slice(w * hw, (w + 1) * hw)
            value = mm(x_all[at, :], w3_all[:, span])
            if w == 0:
                value = value + vec[0:1, pl.ds(al(t * hw, 128), hw)]
            if w == 2:
                value = value + vec[1:2, pl.ds(al(t * hw, 128), hw)]
            qkv[at, span] = value.astype(BF)

    lane_head = lax.broadcasted_iota(jnp.int32, (full, hw), 1) // HEAD_DIM
    scale2 = LOG2E / math.sqrt(HEAD_DIM)

    def head_scores(j, h, at):
        q_head = jnp.where(lane_head == h, qkv[at, 0:hw], jnp.zeros((), BF))
        raw = mm_t(qkv[at, hw : 2 * hw], q_head)
        key_row = lax.broadcasted_iota(jnp.int32, (full, 1), 0)
        visible = key_row < lengths_s[d * n_seq + j]
        return q_head, jnp.where(visible, raw * scale2, MASKED)

    def attention(j):
        at = pl.ds(j * full, full)
        kt[...] = jnp.transpose(qkv[at, 2 * hw : 3 * hw])

        def head(h, carry):
            span = pl.ds(al(h * HEAD_DIM, HEAD_DIM), HEAD_DIM)
            _, scores = head_scores(j, h, at)
            top = jnp.max(scores, axis=0, keepdims=True)
            e = jnp.exp2(scores - top)
            total = jnp.sum(e, axis=0, keepdims=True)
            o = mm(kt[span, :], e.astype(BF))
            ot[span, :] = o * (1.0 / total)
            lse[j, pl.ds(h, 1), :] = top + jnp.log2(total)
            return carry

        lax.fori_loop(0, heads, head, 0)
        att[at, :] = jnp.transpose(ot[...]).astype(BF)

    def project_out(j):
        def part_rows(start):
            def go(n):
                part[pl.ds(start, half), pl.ds(n, tile)] = mm(
                    att[pl.ds(start, half), :], wo_all[:, pl.ds(n, tile)]
                ).astype(BF)

            by_tiles(width, go)

        two_halves("r1", j, part_rows)

    def norm_first(j):
        def go(r):
            loc = seq_rows(j, t * quarter + r, chunk)
            buf = pl.ds(al(j * quarter + r, 16), chunk)
            h = x_all[loc, :].astype(F32) + (summed(j, r) + vec[2:3, :])
            center = h - jnp.mean(h, axis=-1, keepdims=True)
            inv = lax.rsqrt(jnp.mean(center * center, axis=-1, keepdims=True) + EPSILON)
            scaled = center * inv
            n1[buf, :] = scaled
            inv1[buf, :] = jnp.broadcast_to(inv, (chunk, 128))
            u_all[loc, :] = (scaled * vec[6:7, :] + vec[3:4, :]).astype(BF)

        row_loop(go)

    def widen(j):
        at = pl.ds(j * full, full)

        def go(n):
            f = mm(u_all[at, :], we_all[:, pl.ds(n, tile)]) + ebias[0:1, pl.ds(n, tile)]
            cdf = 0.5 + 0.5 * lax.erf(f * (1.0 / math.sqrt(2.0)))
            hid[at, pl.ds(n, tile)] = (f * cdf).astype(BF)
            bell = jnp.exp2((f * f) * (-0.5 * LOG2E)) * (1.0 / math.sqrt(2.0 * math.pi))
            slope[at, pl.ds(n, tile)] = (cdf + f * bell).astype(BF)

        by_tiles(fw, go)

    def shrink_rows(j):
        def part_rows(start):
            def go(n):
                part[pl.ds(start, half), pl.ds(n, tile)] = mm(
                    hid[pl.ds(start, half), :], ws_all[:, pl.ds(n, tile)]
                ).astype(BF)

            by_tiles(width, go)

        two_halves("r2", j, part_rows)

    def norm_second(j):
        length = lengths_s[d * n_seq + j]

        def go(r):
            loc = seq_rows(j, t * quarter + r, chunk)
            buf = pl.ds(al(j * quarter + r, 16), chunk)
            u = n1[buf, :] * vec[6:7, :] + vec[3:4, :]
            total = u + (summed(j, r) + vec[4:5, :])
            center = total - jnp.mean(total, axis=-1, keepdims=True)
            inv = lax.rsqrt(jnp.mean(center * center, axis=-1, keepdims=True) + EPSILON)
            scaled = center * inv
            mixed_send[buf, :] = (scaled * vec[7:8, :] + vec[5:6, :]).astype(BF)
            place = t * quarter + r + lax.broadcasted_iota(jnp.int32, (chunk, 1), 0)
            valid = (place < length).astype(F32)
            e = cots[j, pl.ds(al(r, 16), chunk), :].astype(F32) * valid
            add_sum(5, e)
            add_sum(7, e * scaled)
            pushed = e * vec[7:8, :]
            first = jnp.mean(pushed, axis=-1, keepdims=True)
            second = jnp.mean(pushed * scaled, axis=-1, keepdims=True)
            grad = inv * (pushed - first - scaled * second)
            add_sum(4, grad)
            dy[buf, :] = grad
            dz[loc, :] = grad.astype(BF)

        row_loop(go)

    def rows_out(tag, j, src, dst):
        for o in range(1, n_dp):
            e = dp_to(o)
            link.send(
                (tag, j, o),
                src.at[pl.ds(al(j * quarter + e * rows, 16), rows)],
                dst.at[d * n_seq + j],
                {"dp": e},
            )
        return link.local(
            src.at[pl.ds(al(j * quarter + d * rows, 16), rows)], dst.at[d * n_seq + j]
        )

    def rows_in(tag, j, dst, own):
        own.wait()
        for o in range(1, n_dp):
            e = dp_from(o)
            link.arrived((tag, j, o), dst.at[e * n_seq + j], {"dp": e})
            link.sent((tag, j, o))


    def widen_back(j):
        at = pl.ds(j * full, full)

        def go(n):
            spread = mm_t(dz[at, :], ws_all[pl.ds(n, tile), :])
            grad = (spread * slope[at, pl.ds(n, tile)].astype(F32)).astype(BF)
            slope[at, pl.ds(n, tile)] = grad
            hacc[0:1, pl.ds(n, tile)] += jnp.sum(grad.astype(F32), axis=0, keepdims=True)

        by_tiles(fw, go)

    def normed_rows(j):
        def part_rows(start):
            def go(n):
                part[pl.ds(start, half), pl.ds(n, tile)] = mm_t(
                    slope[pl.ds(start, half), :], we_all[pl.ds(n, tile), :]
                ).astype(BF)

            by_tiles(width, go)

        two_halves("r3", j, part_rows)

    def norm_first_back(j):
        def go(r):
            loc = seq_rows(j, t * quarter + r, chunk)
            buf = pl.ds(al(j * quarter + r, 16), chunk)
            du = dy[buf, :] + summed(j, r)
            scaled = n1[buf, :]
            add_sum(3, du)
            add_sum(6, du * scaled)
            pushed = du * vec[6:7, :]
            first = jnp.mean(pushed, axis=-1, keepdims=True)
            second = jnp.mean(pushed * scaled, axis=-1, keepdims=True)
            grad = inv1[buf, 0:1] * (pushed - first - scaled * second)
            add_sum(2, grad)
            dy[buf, :] = grad
            dh[loc, :] = grad.astype(BF)

        row_loop(go)

    def attention_back(j, between=None):
        at = pl.ds(j * full, full)
        da[...] = mm_t(dh[at, :], wo_all[...]).astype(BF)
        kt[...] = jnp.transpose(qkv[at, hw : 2 * hw])
        dk_acc[...] = jnp.zeros_like(dk_acc)
        dv_acc[...] = jnp.zeros_like(dv_acc)

        def head(h, carry):
            span = pl.ds(al(h * HEAD_DIM, HEAD_DIM), HEAD_DIM)
            q_head, scores = head_scores(j, h, at)
            da_head = jnp.where(lane_head == h, da[...], jnp.zeros((), BF))
            p = jnp.exp2(scores - lse[j, pl.ds(h, 1), :])
            dp = mm_t(qkv[at, 2 * hw : 3 * hw], da_head)
            inner = jnp.sum(p * dp, axis=0, keepdims=True)
            ds = (p * (dp - inner)).astype(BF)
            dv_acc[...] += mm(p.astype(BF), da_head)
            dk_acc[...] += mm(ds, q_head)
            ot[span, :] = mm(kt[span, :], ds)
            return carry

        lax.fori_loop(0, heads, head, 0)
        scale = 1.0 / math.sqrt(HEAD_DIM)
        grad_q = (jnp.transpose(ot[...]) * scale).astype(BF)
        grad_k = (dk_acc[...] * scale).astype(BF)
        grad_v = dv_acc[...].astype(BF)
        dqkv[at, 0:hw] = grad_q
        dqkv[at, hw : 2 * hw] = grad_k
        dqkv[at, 2 * hw : 3 * hw] = grad_v
        qacc[0:1, :] += jnp.sum(grad_q.astype(F32), axis=0, keepdims=True)
        qacc[1:2, :] += jnp.sum(grad_v.astype(F32), axis=0, keepdims=True)

    def token_rows(j):
        def part_rows(start):
            def go(n):
                part[pl.ds(start, half), pl.ds(n, tile)] = mm_t(
                    dqkv[pl.ds(start, half), :], w3_all[pl.ds(n, tile), :]
                ).astype(BF)

            by_tiles(width, go)

        two_halves("r4", j, part_rows)

    def finish_rows(j):
        def go(r):
            buf = pl.ds(al(j * quarter + r, 16), chunk)
            back_send[buf, :] = (dy[buf, :] + summed(j, r)).astype(BF)

        row_loop(go)


    def weight_grad(dst, left, right):
        n = dst.shape[0]

        def go(m):
            dst[pl.ds(m, tile), :] = t_mm(left[:, pl.ds(m, tile)], right[...]).astype(BF)

        by_tiles(n, go)

    grads = {
        "gs": (s.gs, s.gs_y, s.gs_z, False, out_gs),
        "ge": (s.ge, s.ge_y, s.ge_z, True, out_ge),
        "go": (s.go, s.go_y, s.go_z, False, out_go),
        "g3": (s.g3, s.g3_y, s.g3_z, True, out_g3),
    }

    def part_of(ref, by_rows, i):
        if by_rows:
            return (pl.ds(al(i * dw, 16), dw), slice(None))
        return (slice(None), pl.ds(al(i * dw, 128), dw))

    def grad_start(name):
        whole, from_y, _, by_rows, _ = grads[name]
        for k in list(range(1, n_z)) + [0]:
            owner = ((z + k) % n_z) * n_y + (1 - y)
            link.send(
                (name, "y", k),
                whole.at[part_of(whole, by_rows, owner)],
                from_y.at[part_of(from_y, by_rows, k)],
                {"dp": y_peer},
            )

    def grad_forward(name):
        whole, from_y, from_z, by_rows, _ = grads[name]
        for k in list(range(1, n_z)) + [0]:
            mid = part_of(from_y, by_rows, k)
            link.arrived((name, "y", k), from_y.at[mid], {"dp": y_peer})
            owner = ((z + k) % n_z) * n_y + y
            both = whole[part_of(whole, by_rows, owner)].astype(F32) + from_y[mid].astype(F32)
            from_y[mid] = both.astype(BF)
            if k:
                link.send(
                    (name, "z", k),
                    from_y.at[mid],
                    from_z.at[part_of(from_z, by_rows, k - 1)],
                    {"dp": z_to(k)},
                )

    def grad_finish(name):
        _, from_y, from_z, by_rows, out = grads[name]
        total = from_y[part_of(from_y, by_rows, 0)].astype(F32)
        for k in range(1, n_z):
            at = part_of(from_z, by_rows, k - 1)
            link.arrived((name, "z", k), from_z.at[at], {"dp": z_from(k)})
            total = total + from_z[at].astype(F32)
        out[...] = total
        for k in range(1, n_z):
            link.sent((name, "z", k))
        for k in range(n_z):
            link.sent((name, "y", k))

    small_send, small_recv, small_t = s.small_send, s.small_recv, s.small_t

    def small_start():
        small_send[...] = jnp.zeros_like(small_send)
        for e in range(n_dp):
            small_send[e, 2:8, :] = acc[2:8, e * dw : (e + 1) * dw]
        for i in range(owners):
            e = t * owners + i
            small_send[e, 0:2, :] = qacc[0:2, i * dw : (i + 1) * dw]
            for r in range(ebias_rows):
                at = (i * ebias_rows + r) * dw
                small_send[e, 8 + r : 9 + r, :] = hacc[0:1, at : at + dw]
        for o in range(1, n_dp):
            e = dp_to(o)
            link.send(("small", o), small_send.at[e], small_recv.at[o], {"dp": e})

    def small_forward():
        total = small_send[d]
        for o in range(1, n_dp):
            link.arrived(("small", o), small_recv.at[o], {"dp": dp_from(o)})
            total = total + small_recv[o]
            link.sent(("small", o))
        small_t[t] = total
        for what, peer in (("c", t_core), ("f", t_far), ("g", t_diag)):
            link.send(("small_t", what), small_t.at[t], small_t.at[t], {"tensor": peer})

    def small_finish():
        for what, peer in (("c", t_core), ("f", t_far), ("g", t_diag)):
            link.arrived(("small_t", what), small_t.at[peer], {"tensor": peer})
            link.sent(("small_t", what))
        total = small_t[0]
        for i in range(1, n_t):
            total = total + small_t[i]
        out_small[...] = total


    def reduce_pair(tag, j):
        rs_finish(tag, j)

    seqs = range(n_seq)
    last = n_seq - 1
    tokens_start(0)
    gather_start("pack")
    gather_start("w3")
    for j in seqs[1:]:
        tokens_start(j)
    gather_start("wo")
    tokens_finish(0)
    ag_start(x_all, "x", 0)
    for k in range(1, n_z):
        gather_forward("pack", k)
        gather_forward("w3", k)
    for j in seqs[1:]:
        tokens_finish(j)
        ag_start(x_all, "x", j)
    for k in range(1, n_z):
        gather_forward("wo", k)
    for j in seqs:
        ag_forward(x_all, "x", j)
    gather_finish("pack")
    spread_vectors()
    gather_finish("w3")
    gather_start("we")
    gather_start("ws")
    ag_finish(x_all, "x", 0)
    project(0)
    attention(0)
    for k in range(1, n_z):
        gather_forward("we", k)
    gather_finish("wo")
    project_out(0)
    ag_finish(x_all, "x", 1)
    project(1)
    rs_forward("r1", 0)
    attention(1)
    for k in range(1, n_z):
        gather_forward("ws", k)
    cot_own = cot_start()
    project_out(1)
    rs_finish("r1", 0)
    norm_first(0)
    ag_start(u_all, "u", 0)
    ag_finish(x_all, "x", 2)
    project(2)
    rs_forward("r1", 1)
    attention(2)
    ag_forward(u_all, "u", 0)
    project_out(2)
    rs_finish("r1", 1)
    norm_first(1)
    ag_start(u_all, "u", 1)
    gather_finish("we")
    ag_finish(u_all, "u", 0)
    rs_forward("r1", 2)
    widen(0)
    ag_forward(u_all, "u", 1)
    gather_finish("ws")
    shrink_rows(0)
    rs_finish("r1", 2)
    norm_first(2)
    ag_start(u_all, "u", 2)
    ag_finish(u_all, "u", 1)
    rs_forward("r2", 0)
    widen(1)
    ag_forward(u_all, "u", 2)
    cot_finish(cot_own)
    shrink_rows(1)
    mixed_own = []
    rs_finish("r2", 0)
    norm_second(0)
    ag_start(dz, "z", 0)
    ag_finish(u_all, "u", 2)
    rs_forward("r2", 1)
    widen(2)
    ag_forward(dz, "z", 0)
    shrink_rows(2)
    rs_finish("r2", 1)
    norm_second(1)
    ag_start(dz, "z", 1)
    ag_finish(dz, "z", 0)
    rs_forward("r2", 2)
    widen_back(0)
    ag_forward(dz, "z", 1)
    normed_rows(0)
    rs_finish("r2", 2)
    norm_second(2)
    ag_start(dz, "z", 2)
    for j in seqs:
        mixed_own.append(rows_out("mix", j, mixed_send, out_mixed))
    ag_finish(dz, "z", 1)
    rs_forward("r3", 0)
    widen_back(1)
    ag_forward(dz, "z", 2)
    normed_rows(1)
    rs_finish("r3", 0)
    norm_first_back(0)
    ag_start(dh, "h", 0)
    ag_finish(dz, "z", 2)
    rs_forward("r3", 1)
    widen_back(2)
    ag_forward(dh, "h", 0)
    normed_rows(2)
    rs_finish("r3", 1)
    norm_first_back(1)
    ag_start(dh, "h", 1)
    weight_grad(s.gs, hid, dz)
    grad_start("gs")
    rs_forward("r3", 2)
    ag_forward(dh, "h", 1)
    ag_finish(dh, "h", 0)
    attention_back(0)
    rs_finish("r3", 2)
    norm_first_back(2)
    ag_start(dh, "h", 2)
    token_rows(0)
    grad_forward("gs")
    weight_grad(s.ge, u_all, slope)
    grad_start("ge")
    rs_forward("r4", 0)
    ag_forward(dh, "h", 2)
    ag_finish(dh, "h", 1)
    attention_back(1)
    rs_finish("r4", 0)
    finish_rows(0)
    back_own = [rows_out("back", 0, back_send, back_recv)]
    token_rows(1)
    grad_forward("ge")
    ag_finish(dh, "h", 2)
    rs_forward("r4", 1)
    attention_back(2)
    weight_grad(s.g3, x_all, dqkv)
    grad_start("g3")
    token_rows(2)
    rs_finish("r4", 1)
    finish_rows(1)
    back_own.append(rows_out("back", 1, back_send, back_recv))
    rs_forward("r4", 2)
    grad_forward("g3")
    small_start()
    weight_grad(s.go, att, dh)
    grad_start("go")
    rs_finish("r4", 2)
    finish_rows(2)
    back_own.append(rows_out("back", 2, back_send, back_recv))
    grad_finish("gs")
    grad_finish("ge")
    for j in seqs:
        rows_in("mix", j, out_mixed, mixed_own[j])
    small_forward()
    grad_forward("go")
    grad_finish("g3")
    small_finish()
    grad_finish("go")
    for j in seqs:
        rows_in("back", j, back_recv, back_own[j])

    def restore(k, carry):
        out_back[k] = back_recv[order_s[k]]
        return carry

    lax.fori_loop(0, n_dp * n_seq, restore, 0)


def body(
    tokens,
    cotangent,
    lengths,
    order,
    triple_weight,
    output_weight,
    expand_weight,
    shrink_weight,
    biases,
    gains,
    expand_bias,
):
    n_dp, n_t = lax.axis_size("dp"), lax.axis_size("tensor")
    slots, _, rows, width = tokens.shape
    n_seq = slots // n_dp
    quarter = rows * n_dp
    full = quarter * n_t
    dw = triple_weight.shape[1]
    hw = triple_weight.shape[2]
    fw = expand_weight.shape[1]
    fits = (
        n_t == 4
        and n_dp % 4 == 0
        and rows % 16 == 0
        and dw % 128 == 0
        and hw % 128 == 0
        and n_seq == 3
        and expand_bias.shape[0] % dw == 0
        and n_dp % n_t == 0
    )
    if not fits:
        return plain_body(
            tokens,
            cotangent,
            lengths,
            order,
            triple_weight,
            output_weight,
            expand_weight,
            shrink_weight,
            biases,
            gains,
            expand_bias,
        )
    n_y = 2
    n_z = n_dp // n_y
    ebias_rows = expand_bias.shape[0] // dw
    ids = jnp.arange(slots, dtype=jnp.int32)
    inverse = jnp.sum(jnp.where(order[None, :] == ids[:, None], ids[None, :], 0), axis=1)
    pack_rows = 16
    pack = jnp.concatenate(
        [
            biases,
            gains,
            expand_bias.reshape(ebias_rows, dw),
            jnp.zeros((pack_rows - 8 - ebias_rows, dw), BF),
        ]
    )
    w3 = jnp.concatenate([triple_weight[0], triple_weight[1], triple_weight[2]], axis=1)
    all_rows = n_seq * full
    own_rows = n_seq * quarter
    vm = pltpu.VMEM
    scratch = dict(
        stage=vm((slots, rows, width), BF),
        x_all=vm((all_rows, width), BF),
        cots=vm((n_seq, quarter, width), BF),
        w3_all=vm((width, 3 * hw), BF),
        wo_all=vm((hw, width), BF),
        we_all=vm((width, fw), BF),
        ws_all=vm((fw, width), BF),
        pack_all=vm((pack_rows, width), BF),
        vec=vm((pack_rows, width), F32),
        ebias=vm((8, fw), F32),
        qkv=vm((all_rows, 3 * hw), BF),
        att=vm((all_rows, hw), BF),
        lse=vm((n_seq, 8, full), F32),
        part=vm((all_rows, width), BF),
        r_a=vm((own_rows, width), BF),
        r_b=vm((own_rows, width), BF),
        r_x=vm((own_rows, width), BF),
        n1=vm((own_rows, width), F32),
        inv1=vm((own_rows, 128), F32),
        u_all=vm((all_rows, width), BF),
        hid=vm((all_rows, fw), BF),
        slope=vm((all_rows, fw), BF),
        dz=vm((all_rows, width), BF),
        dh=vm((all_rows, width), BF),
        dy=vm((own_rows, width), F32),
        dqkv=vm((all_rows, 3 * hw), BF),
        acc=vm((8, width), F32),
        hacc=vm((8, fw), F32),
        qacc=vm((8, hw), F32),
        kt=vm((hw, full), BF),
        ot=vm((hw, full), F32),
        dk_acc=vm((full, hw), F32),
        dv_acc=vm((full, hw), F32),
        da=vm((full, hw), BF),
        mixed_send=vm((own_rows, width), BF),
        back_send=vm((own_rows, width), BF),
        back_recv=vm((slots, rows, width), BF),
        gs=vm((fw, width), BF),
        gs_y=vm((fw, n_z * dw), BF),
        gs_z=vm((fw, (n_z - 1) * dw), BF),
        ge=vm((width, fw), BF),
        ge_y=vm((n_z * dw, fw), BF),
        ge_z=vm(((n_z - 1) * dw, fw), BF),
        go=vm((hw, width), BF),
        go_y=vm((hw, n_z * dw), BF),
        go_z=vm((hw, (n_z - 1) * dw), BF),
        g3=vm((width, 3 * hw), BF),
        g3_y=vm((n_z * dw, 3 * hw), BF),
        g3_z=vm(((n_z - 1) * dw, 3 * hw), BF),
        small_send=vm((n_dp, 16, dw), F32),
        small_recv=vm((n_dp, 16, dw), F32),
        small_t=vm((n_t, 16, dw), F32),
        send_sems=pltpu.SemaphoreType.DMA((N_SEM,)),
        recv_sems=pltpu.SemaphoreType.DMA((N_SEM,)),
        local_sems=pltpu.SemaphoreType.DMA((24,)),
    )
    g = types.SimpleNamespace(
        n_seq=n_seq,
        quarter=quarter,
        width=width,
        n_dp=n_dp,
        n_y=n_y,
        n_t=n_t,
        head_width=hw,
        hidden_width=fw,
        ebias_rows=ebias_rows,
        scratch_names=tuple(scratch),
    )
    smem = pl.BlockSpec(memory_space=pltpu.SMEM)
    vmem = pl.BlockSpec(memory_space=pltpu.VMEM)
    anywhere = pl.BlockSpec(memory_space=pl.ANY)
    sds = jax.ShapeDtypeStruct
    flops = 2 * all_rows * (3 * width * 3 * hw + 3 * width * hw + 6 * width * fw + 7 * full * hw)
    mixed, back, g3, go, ge, gs, small = pl.pallas_call(
        functools.partial(layer_kernel, g),
        out_shape=(
            sds(tokens.shape[:1] + (rows, width), BF),
            sds(tokens.shape[:1] + (rows, width), BF),
            sds((dw, 3 * hw), F32),
            sds((hw, dw), F32),
            sds((dw, fw), F32),
            sds((fw, dw), F32),
            sds((16, dw), F32),
        ),
        in_specs=[smem] * 3 + [vmem] + [anywhere] * 6,
        out_specs=[anywhere] + [vmem] * 6,
        scratch_shapes=list(scratch.values()),
        compiler_params=pltpu.CompilerParams(
            collective_id=0,
            has_side_effects=True,
            vmem_limit_bytes=VMEM_BYTES,
        ),
        cost_estimate=pl.CostEstimate(flops=flops, bytes_accessed=1 << 24, transcendentals=0),
    )(
        order,
        inverse,
        lengths,
        tokens.reshape(slots, rows, width),
        cotangent.reshape(slots, rows, width),
        w3,
        output_weight,
        expand_weight,
        shrink_weight,
        pack,
    )
    return (
        mixed.reshape(tokens.shape),
        back.reshape(tokens.shape),
        jnp.stack([g3[:, i * hw : (i + 1) * hw] for i in range(3)]),
        go,
        ge,
        gs,
        small[0:6],
        small[6:8],
        small[8 : 8 + ebias_rows].reshape(expand_bias.shape),
    )


def solution(mesh):
    return jax.shard_map(
        body,
        mesh=mesh,
        in_specs=(
            P(None, "tensor", "dp", None),
            P(None, "tensor", "dp", None),
            P(),
            P(),
            P(None, "dp", "tensor"),
            P(None, "dp"),
            P("dp", "tensor"),
            P("tensor", "dp"),
            P(None, "dp"),
            P(None, "dp"),
            P("dp"),
        ),
        out_specs=(
            P(None, "tensor", "dp", None),
            P(None, "tensor", "dp", None),
            P(None, "dp", "tensor"),
            P("tensor", "dp"),
            P("dp", "tensor"),
            P("tensor", "dp"),
            P(None, "dp"),
            P(None, "dp"),
            P("dp"),
        ),
        check_vma=False,
    )
```

```python
import functools
import math
import types

import jax
import jax.numpy as jnp
from jax import lax
from jax.experimental import pallas as pl
from jax.experimental.pallas import tpu as pltpu
from jax.sharding import PartitionSpec as P

HEAD_DIM = 64


EPSILON = 1e-12
MASKED = -1e30


def normalize(values, gain, shift):
    center = values - jnp.mean(values, axis=-1, keepdims=True)
    spread = jnp.mean(center * center, axis=-1, keepdims=True)
    inv_std = lax.rsqrt(spread + EPSILON)
    scaled = center * inv_std
    return (scaled * gain + shift, scaled, inv_std)


def normalize_back(grad_rows, scaled, inv_std, gain):
    pushed = grad_rows * gain
    first = jnp.mean(pushed, axis=-1, keepdims=True)
    second = jnp.mean(pushed * scaled, axis=-1, keepdims=True)
    return inv_std * (pushed - first - scaled * second)


def gelu_exact(values):
    return 0.5 * values * (1.0 + jax.scipy.special.erf(values / math.sqrt(2.0)))


def gelu_slope(values):
    return 0.5 * (1.0 + jax.scipy.special.erf(values / math.sqrt(2.0))) + values * jnp.exp(
        -0.5 * values * values
    ) / math.sqrt(2.0 * math.pi)


def split_heads(rows):
    return rows.reshape(rows.shape[0], rows.shape[1] // HEAD_DIM, HEAD_DIM)


def score_block(queries, key_rows, seq_length):
    raw_scores = jnp.einsum("qhe,khe->hqk", queries, key_rows, preferred_element_type=jnp.float32)
    scores = raw_scores * (1.0 / math.sqrt(HEAD_DIM))
    visible = jnp.arange(key_rows.shape[0]) < seq_length
    return jnp.where(visible[None, None, :], scores, MASKED)


def attend(seq_item):
    queries, key_rows, value_rows, seq_length = seq_item
    queries = split_heads(queries)
    key_rows = split_heads(key_rows)
    value_rows = split_heads(value_rows)
    masked = score_block(queries, key_rows, seq_length)
    highest = jnp.max(masked, axis=-1, keepdims=True)
    totals = jnp.sum(jnp.exp(masked - highest), axis=-1, keepdims=True)
    log_totals = highest + jnp.log(totals)
    probs = jnp.exp(masked - log_totals).astype(jnp.bfloat16)
    blended = jnp.einsum("hqk,khe->qhe", probs, value_rows, preferred_element_type=jnp.float32)
    return (blended.astype(jnp.bfloat16).reshape(queries.shape[0], -1), log_totals[..., 0])


def attend_back(seq_item):
    queries, key_rows, value_rows, grad_rows, log_totals, seq_length = seq_item
    queries = split_heads(queries)
    key_rows = split_heads(key_rows)
    value_rows = split_heads(value_rows)
    grad_heads = split_heads(grad_rows)
    masked = score_block(queries, key_rows, seq_length)
    probs = jnp.exp(masked - log_totals[..., None])
    grad_probs = jnp.einsum(
        "qhe,khe->hqk", grad_heads, value_rows, preferred_element_type=jnp.float32
    )
    inner = jnp.sum(probs * grad_probs, axis=-1, keepdims=True)
    grad_scores = (probs * (grad_probs - inner)).astype(jnp.bfloat16)
    score_scale = 1.0 / math.sqrt(HEAD_DIM)
    grad_query = (
        jnp.einsum("hqk,khe->qhe", grad_scores, key_rows, preferred_element_type=jnp.float32)
        * score_scale
    )
    grad_key = (
        jnp.einsum("hqk,qhe->khe", grad_scores, queries, preferred_element_type=jnp.float32)
        * score_scale
    )
    grad_value = jnp.einsum(
        "hqk,qhe->khe", probs.astype(jnp.bfloat16), grad_heads, preferred_element_type=jnp.float32
    )
    row_count = queries.shape[0]
    return (
        grad_query.astype(jnp.bfloat16).reshape(row_count, -1),
        grad_key.astype(jnp.bfloat16).reshape(row_count, -1),
        grad_value.astype(jnp.bfloat16).reshape(row_count, -1),
    )


def plain_body(
    tokens,
    cotangent,
    lengths,
    order,
    triple_weight,
    output_weight,
    expand_weight,
    shrink_weight,
    biases,
    gains,
    expand_bias,
):
    seq_count = order.shape[0]
    per_group = seq_count // lax.axis_size("dp")
    tensor_size = lax.axis_size("tensor")
    member = lax.axis_index("dp")
    my_rank = lax.axis_index("tensor")
    slot_ids = jnp.arange(seq_count, dtype=jnp.int32)
    inverse = jnp.zeros((seq_count,), jnp.int32).at[order].set(slot_ids)
    local_x, local_dy = (
        lax.all_to_all(tokens[inverse], "dp", split_axis=0, concat_axis=2, tiled=True),
        lax.all_to_all(cotangent, "dp", split_axis=0, concat_axis=2, tiled=True),
    )
    quarter = local_x.shape[2]
    model_width = local_x.shape[3]
    full_length = quarter * tensor_size
    my_lengths = lax.dynamic_slice_in_dim(lengths, member * per_group, per_group)
    gathered = (
        lax.all_gather(triple_weight, "dp", axis=1, tiled=True),
        lax.all_gather(output_weight, "dp", axis=1, tiled=True),
        lax.all_gather(expand_weight, "dp", axis=0, tiled=True),
        lax.all_gather(shrink_weight, "dp", axis=1, tiled=True),
        lax.all_gather(biases, "dp", axis=1, tiled=True),
        lax.all_gather(gains, "dp", axis=1, tiled=True),
        lax.all_gather(expand_bias, "dp", axis=0, tiled=True),
    )
    query_key_value_proj, out_weight, widen_projection, shrink, bias_rows, gain_rows, exp_bias = (
        gathered
    )
    head_width = query_key_value_proj.shape[2]
    hidden_width = widen_projection.shape[1]
    out_heads = lax.dynamic_slice_in_dim(out_weight, my_rank * head_width, head_width, 0)
    bias_query = lax.dynamic_slice_in_dim(bias_rows[0], my_rank * head_width, head_width).astype(
        jnp.float32
    )
    bias_value = lax.dynamic_slice_in_dim(bias_rows[1], my_rank * head_width, head_width).astype(
        jnp.float32
    )
    bias_hidden = lax.dynamic_slice_in_dim(exp_bias, my_rank * hidden_width, hidden_width).astype(
        jnp.float32
    )
    bias_stack = jnp.stack([bias_query, jnp.zeros_like(bias_query), bias_value])
    gain_first = gain_rows[0].astype(jnp.float32)
    gain_second = gain_rows[1].astype(jnp.float32)
    full_shape = (per_group, tensor_size, quarter, model_width)
    token_all_rows = lax.all_gather(local_x, "tensor", axis=1, tiled=True).reshape(
        per_group, full_length, model_width
    )
    projected = (
        jnp.einsum(
            "jah,rhu->rjau",
            token_all_rows,
            query_key_value_proj,
            preferred_element_type=jnp.float32,
        )
        + bias_stack[:, None, None, :]
    ).astype(jnp.bfloat16)
    attended, log_totals = lax.map(attend, (projected[0], projected[1], projected[2], my_lengths))
    attn_terms = jnp.einsum(
        "sle,em->slm", attended, out_heads, preferred_element_type=jnp.float32
    ).reshape(full_shape)
    attn_sum = lax.psum_scatter(attn_terms, "tensor", scatter_dimension=1, tiled=True)
    hidden_in = local_x.astype(jnp.float32) + (attn_sum + bias_rows[2].astype(jnp.float32))
    normed, normed_scaled, normed_inv = normalize(
        hidden_in, gain_first, bias_rows[3].astype(jnp.float32)
    )
    normalized_all_rows = lax.all_gather(
        normed.astype(jnp.bfloat16), "tensor", axis=1, tiled=True
    ).reshape(per_group, full_length, model_width)
    pre_act = (
        jnp.einsum(
            "uqj,jt->uqt", normalized_all_rows, widen_projection, preferred_element_type=jnp.float32
        )
        + bias_hidden
    )
    hidden = gelu_exact(pre_act).astype(jnp.bfloat16)
    ffn_terms = jnp.einsum(
        "slf,fm->slm", hidden, shrink, preferred_element_type=jnp.float32
    ).reshape(full_shape)
    ffn_sum = lax.psum_scatter(
        ffn_terms.astype(jnp.bfloat16), "tensor", scatter_dimension=1, tiled=True
    ).astype(jnp.float32)
    total_rows = normed + (ffn_sum + bias_rows[4].astype(jnp.float32))
    output, out_scaled, out_inv = normalize(
        total_rows, gain_second, bias_rows[5].astype(jnp.float32)
    )
    positions = my_rank * quarter + jnp.arange(quarter)
    valid = (positions[None, :] < my_lengths[:, None]).astype(jnp.float32)
    grad_out = local_dy.astype(jnp.float32) * valid[:, None, :, None]
    row_axes = (0, 1, 2)
    gain_grad_second = jnp.sum(grad_out * out_scaled, axis=row_axes)
    shift_grad_second = jnp.sum(grad_out, axis=row_axes)
    grad_total = normalize_back(grad_out, out_scaled, out_inv, gain_second)
    branch_bias_grad = jnp.sum(grad_total, axis=row_axes)
    grad_branch = lax.all_gather(
        grad_total.astype(jnp.bfloat16), "tensor", axis=1, tiled=True
    ).reshape(per_group, full_length, model_width)
    shrink_grad = jnp.einsum("slf,slm->fm", hidden, grad_branch, preferred_element_type=jnp.float32)
    grad_hidden = jnp.einsum("slm,fm->slf", grad_branch, shrink, preferred_element_type=jnp.float32)
    preactivation_grad = (grad_hidden * gelu_slope(pre_act)).astype(jnp.bfloat16)
    hidden_bias_grad = jnp.sum(preactivation_grad, axis=(0, 1), dtype=jnp.float32)
    expand_grad = jnp.einsum(
        "mgc,mga->ca", normalized_all_rows, preactivation_grad, preferred_element_type=jnp.float32
    )
    normed_terms = jnp.einsum(
        "cpk,rk->cpr", preactivation_grad, widen_projection, preferred_element_type=jnp.float32
    ).reshape(full_shape)
    grad_normed = grad_total + lax.psum_scatter(
        normed_terms.astype(jnp.bfloat16), "tensor", scatter_dimension=1, tiled=True
    ).astype(jnp.float32)
    first_norm_gain_grad = jnp.sum(grad_normed * normed_scaled, axis=row_axes)
    shift_grad_first = jnp.sum(grad_normed, axis=row_axes)
    grad_hidden_in = normalize_back(grad_normed, normed_scaled, normed_inv, gain_first)
    out_bias_grad = jnp.sum(grad_hidden_in, axis=row_axes)
    grad_attn = lax.all_gather(
        grad_hidden_in.astype(jnp.bfloat16), "tensor", axis=1, tiled=True
    ).reshape(per_group, full_length, model_width)
    output_grad = jnp.einsum("sle,slm->em", attended, grad_attn, preferred_element_type=jnp.float32)
    grad_blended = jnp.einsum(
        "slm,em->sle", grad_attn, out_heads, preferred_element_type=jnp.float32
    ).astype(jnp.bfloat16)
    grad_query, grad_key, grad_value = lax.map(
        attend_back,
        (projected[0], projected[1], projected[2], grad_blended, log_totals, my_lengths),
    )
    projection_output_grad = jnp.stack([grad_query, grad_key, grad_value])
    query_bias_grad = jnp.sum(grad_query, axis=(0, 1), dtype=jnp.float32)
    value_bias_grad = jnp.sum(grad_value, axis=(0, 1), dtype=jnp.float32)
    triple_grad = jnp.einsum(
        "xyt,vxyu->vtu", token_all_rows, projection_output_grad, preferred_element_type=jnp.float32
    )
    token_terms = jnp.einsum(
        "atpi,aki->tpk",
        projection_output_grad,
        query_key_value_proj,
        preferred_element_type=jnp.float32,
    ).reshape(full_shape)
    grad_tokens = grad_hidden_in + lax.psum_scatter(
        token_terms.astype(jnp.bfloat16), "tensor", scatter_dimension=1, tiled=True
    ).astype(jnp.float32)
    zero_row = jnp.zeros((model_width,), jnp.float32)
    query_full = lax.dynamic_update_slice_in_dim(zero_row, query_bias_grad, my_rank * head_width, 0)
    value_full = lax.dynamic_update_slice_in_dim(zero_row, value_bias_grad, my_rank * head_width, 0)
    bias_grad = jnp.stack(
        [
            query_full,
            value_full,
            out_bias_grad,
            shift_grad_first,
            branch_bias_grad,
            shift_grad_second,
        ]
    )
    gain_grad = jnp.stack([first_norm_gain_grad, gain_grad_second])
    hidden_full = lax.dynamic_update_slice_in_dim(
        jnp.zeros((exp_bias.shape[0],), jnp.float32), hidden_bias_grad, my_rank * hidden_width, 0
    )
    bias_grad, gain_grad, hidden_full = (
        lax.psum(bias_grad.astype(jnp.bfloat16), "tensor").astype(jnp.float32),
        lax.psum(gain_grad.astype(jnp.bfloat16), "tensor").astype(jnp.float32),
        lax.psum(hidden_full.astype(jnp.bfloat16), "tensor").astype(jnp.float32),
    )
    shards = (
        lax.psum_scatter(triple_grad, "dp", scatter_dimension=1, tiled=True),
        lax.psum_scatter(output_grad, "dp", scatter_dimension=1, tiled=True),
        lax.psum_scatter(expand_grad, "dp", scatter_dimension=0, tiled=True),
        lax.psum_scatter(shrink_grad, "dp", scatter_dimension=1, tiled=True),
        lax.psum_scatter(bias_grad, "dp", scatter_dimension=1, tiled=True),
        lax.psum_scatter(gain_grad, "dp", scatter_dimension=1, tiled=True),
        lax.psum_scatter(hidden_full, "dp", scatter_dimension=0, tiled=True),
    )
    mixed_rows, back_rows = (
        lax.all_to_all(output.astype(jnp.bfloat16), "dp", split_axis=2, concat_axis=0, tiled=True),
        lax.all_to_all(
            grad_tokens.astype(jnp.bfloat16), "dp", split_axis=2, concat_axis=0, tiled=True
        ),
    )
    return (
        mixed_rows,
        back_rows[order],
        shards[0],
        shards[1],
        shards[2],
        shards[3],
        shards[4],
        shards[5],
        shards[6],
    )


BF = jnp.bfloat16
F32 = jnp.float32
MESH = pl.DeviceIdType.MESH
LOG2E = math.log2(math.e)
N_SEM = 147
PACK, W3, WO, WE, WS = range(5)
GS, GE, G3, GO = range(10, 14)
TX, TU, TZ, TH, R1, R2, R3, R4 = range(20, 28)
TOK, COT, MIX, BACK, SMALL, SMALL_T = range(30, 36)
RIGHT, LEFT, OVER_Y, OVER_Z, FAR, NEAR, NEAR_ON = range(40, 47)
VMEM_BYTES = 64 * 1024 * 1024


def mm(a, b):
    return lax.dot_general(a, b, (((1,), (0,)), ((), ())), preferred_element_type=F32)


def mm_t(a, b):
    return lax.dot_general(a, b, (((1,), (1,)), ((), ())), preferred_element_type=F32)


def t_mm(a, b):
    return lax.dot_general(a, b, (((0,), (0,)), ((), ())), preferred_element_type=F32)


class Links:
    def __init__(self, send_sems, recv_sems, local_sems):
        self.send_sems = send_sems
        self.recv_sems = recv_sems
        self.local_sems = local_sems
        self.slots = {}
        self.flying = {}
        self.local_count = 0

    def slot(self, name):
        if TX <= name[0] <= TH:
            name = (TX,) + name[1:]
        if R1 <= name[0] <= R4:
            name = (R1,) + name[1:]
        return self.slots.setdefault(name, len(self.slots))

    def send(self, name, src, dst, where):
        i = self.slot(name)
        if i in self.flying:
            self.sent(name)
        copy = pltpu.make_async_remote_copy(
            src_ref=src,
            dst_ref=dst,
            send_sem=self.send_sems.at[i],
            recv_sem=self.recv_sems.at[i],
            device_id=where,
            device_id_type=MESH,
        )
        copy.start()
        self.flying[i] = copy

    def sent(self, name):
        self.flying.pop(self.slot(name)).wait_send()

    def arrived(self, name, dst, where):
        i = self.slot(name)
        pltpu.make_async_remote_copy(
            src_ref=dst,
            dst_ref=dst,
            send_sem=self.send_sems.at[i],
            recv_sem=self.recv_sems.at[i],
            device_id=where,
            device_id_type=MESH,
        ).wait_recv()

    def drain(self):
        for copy in self.flying.values():
            copy.wait_send()

    def local(self, src, dst):
        copy = pltpu.make_async_copy(src, dst, self.local_sems.at[self.local_count])
        self.local_count += 1
        copy.start()
        return copy


def layer_kernel(g, *refs):
    (order_s, lengths_s, tok, cot, w3, wo, we, ws, bias_in, gain_in, hidden_in) = refs[:11]
    (out_mixed, back_recv, out_g3, out_go, out_ge, out_gs, out_small) = refs[11:18]
    s = types.SimpleNamespace(**dict(zip(g.scratch_names, refs[18:])))
    n_seq, quarter, width = g.n_seq, g.quarter, g.width
    n_dp, n_y, n_t = g.n_dp, g.n_y, g.n_t
    n_z = n_dp // n_y
    full = n_t * quarter
    half = full // 2
    rows = quarter // n_dp
    hw, fw = g.head_width, g.hidden_width
    heads = hw // HEAD_DIM
    dw = width // n_dp
    tile = 256
    ebias_rows = g.ebias_rows
    owners = n_dp // n_t

    d = lax.axis_index("dp")
    t = lax.axis_index("tensor")
    z, y = d // n_y, d % n_y
    x, c = t // 2, t % 2
    t_core = x * 2 + (1 - c)
    t_far = (1 - x) * 2 + c
    t_diag = (1 - x) * 2 + (1 - c)

    def dp_to(o):
        return (d + o) % n_dp

    def dp_from(o):
        return (d + n_dp - o) % n_dp

    def z_to(k):
        return ((z + k) % n_z) * n_y + y

    def z_from(k):
        return ((z + n_z - k) % n_z) * n_y + y

    y_peer = z * n_y + (1 - y)
    ring = (1 - y) * z + y * (n_dp - 1 - z)

    def ring_at(k):
        r = (ring + n_dp + k) % n_dp
        back = r // n_z
        return ((1 - back) * r + back * (n_dp - 1 - r)) * n_y + back

    link = Links(s.send_sems, s.recv_sems, s.local_sems)

    barrier = pltpu.get_barrier_semaphore()
    for o in range(1, n_dp):
        pl.semaphore_signal(barrier, inc=1, device_id={"dp": dp_to(o)}, device_id_type=MESH)
    for peer in (t_core, t_far, t_diag):
        pl.semaphore_signal(barrier, inc=1, device_id={"tensor": peer}, device_id_type=MESH)

    stage, x_all, cots = s.stage, s.x_all, s.cots
    w3_all, wo_all, we_all, ws_all = s.w3_all, s.wo_all, s.we_all, s.ws_all
    pack_own, vec, ebias = s.pack_own, s.vec, s.ebias
    qkv, att, lse, part = s.qkv, s.att, s.lse, s.part
    r_a, r_b, r_x = s.r_a, s.r_b, s.r_x
    n1, inv1, u_all, hid, slope = s.n1, s.inv1, s.u_all, s.hid, s.slope
    dz, dh, dy, dqkv = s.dz, s.dh, s.dy, s.dqkv
    acc, hacc, qacc = s.acc, s.hacc, s.qacc
    kt, ot, dk_acc, dv_acc, da = s.kt, s.ot, s.dk_acc, s.dv_acc, s.da
    mixed_send, back_send = s.mixed_send, s.back_send

    def al(v, m):
        return pl.multiple_of(v, m)

    def seq_rows(j, start, n):
        return pl.ds(al(j * full + start, 16), n)

    def mine(j):
        return seq_rows(j, t * quarter, quarter)


    def permute(k, carry):
        arrival = jnp.int32(0)
        for i in range(n_dp * n_seq):
            arrival = jnp.where(order_s[i] == k, i, arrival)
        stage[k] = tok[arrival]
        return carry

    lax.fori_loop(0, n_dp * n_seq, permute, 0)
    pack_own[0:6, :] = bias_in[...].astype(F32)
    pack_own[6:8, :] = gain_in[...].astype(F32)
    pack_own[8 : 8 + ebias_rows, :] = hidden_in[...].astype(F32)
    pack_own[8 + ebias_rows :, :] = jnp.zeros((16 - 8 - ebias_rows, dw), F32)
    acc[...] = jnp.zeros_like(acc)
    hacc[...] = jnp.zeros_like(hacc)
    qacc[...] = jnp.zeros_like(qacc)
    pl.semaphore_wait(barrier, n_dp - 1 + 3)

    def x_block(j, src):
        return x_all.at[seq_rows(j, t * quarter + src * rows, rows)]

    def tokens_start(j):
        for o in range(1, n_dp):
            e = dp_to(o)
            link.send((TOK, j, o), stage.at[e * n_seq + j], x_block(j, d), {"dp": e})
        x_all[seq_rows(j, t * quarter + d * rows, rows), :] = stage[d * n_seq + j]

    def tokens_finish(j):
        for o in range(1, n_dp):
            link.arrived((TOK, j, o), x_block(j, dp_from(o)), {"dp": dp_from(o)})

    def cot_block(src):
        return cots.at[:, pl.ds(al(src * rows, 16), rows), :]

    own_copies = {}

    def cot_start():
        for o in range(1, n_dp):
            e = dp_to(o)
            link.send((COT, o), cot.at[pl.ds(e * n_seq, n_seq)], cot_block(d), {"dp": e})
        own_copies[COT] = link.local(cot.at[pl.ds(d * n_seq, n_seq)], cot_block(d))

    def cot_finish():
        own_copies.pop(COT).wait()
        for o in range(1, n_dp):
            link.arrived((COT, o), cot_block(dp_from(o)), {"dp": dp_from(o)})

    def cols(ref, e):
        return ref.at[:, pl.ds(al(e * dw, 128), dw)]

    def row_block(ref, e):
        return ref.at[pl.ds(al(e * dw, 16), dw), :]

    def w3_block(e):
        return w3_all.at[:, pl.ds(al(e * dw, 16), dw), :]

    gathers = {
        PACK: (pack_own, lambda e: cols(vec, e), n_dp // 2),
        W3: (w3, w3_block, n_dp // 2),
        WO: (
            wo.at[pl.ds(al(t * hw, 16), hw), :],
            lambda e: cols(wo_all, e),
            n_dp // 2 - 1,
        ),
        WE: (we, lambda e: row_block(we_all, e), n_dp // 2),
        WS: (ws, lambda e: cols(ws_all, e), n_dp // 2 - 1),
    }

    def gather_start(name):
        src, block, _ = gathers[name]
        link.send((name, RIGHT, 1), src, block(d), {"dp": ring_at(1)})
        link.send((name, LEFT, 1), src, block(d), {"dp": ring_at(-1)})
        own_copies[name] = link.local(src, block(d))

    def gather_step(name, way, k):
        _, block, right = gathers[name]
        steps, sign = (right, -1) if way == RIGHT else (n_dp - 1 - right, 1)
        got = block(ring_at(sign * k))
        link.arrived((name, way, k), got, {"dp": ring_at(sign)})
        if k < steps:
            link.send((name, way, k + 1), got, got, {"dp": ring_at(-sign)})

    def gather_ready(name):
        own_copies.pop(name).wait()


    def t_rows(j, who):
        return seq_rows(j, who * quarter, quarter)

    def ag_start(buf, tag, j):
        own = buf.at[t_rows(j, t)]
        link.send((tag, FAR, j), own, own, {"tensor": t_far})
        link.send((tag, NEAR, j), own, own, {"tensor": t_core})

    def ag_forward(buf, tag, j):
        got = buf.at[t_rows(j, t_far)]
        link.arrived((tag, FAR, j), got, {"tensor": t_far})
        link.send((tag, NEAR_ON, j), got, got, {"tensor": t_core})

    def ag_finish(buf, tag, j):
        link.arrived((tag, NEAR, j), buf.at[t_rows(j, t_core)], {"tensor": t_core})
        link.arrived((tag, NEAR_ON, j), buf.at[t_rows(j, t_diag)], {"tensor": t_core})

    def q_rows(j):
        return pl.ds(j * quarter, quarter)

    def rs_start_far(tag, j):
        link.send((tag, NEAR_ON, j), part.at[t_rows(j, t_diag)], r_b.at[q_rows(j)], {"tensor": t_core})

    def rs_start_near(tag, j):
        link.send((tag, NEAR, j), part.at[t_rows(j, t_core)], r_a.at[q_rows(j)], {"tensor": t_core})

    def rs_forward(tag, j):
        link.arrived((tag, NEAR_ON, j), r_b.at[q_rows(j)], {"tensor": t_core})
        far = t_rows(j, t_far)
        both = part[far, :].astype(F32) + r_b[q_rows(j), :].astype(F32)
        part[far, :] = both.astype(BF)
        link.send((tag, FAR, j), part.at[far], r_x.at[q_rows(j)], {"tensor": t_far})

    def rs_finish(tag, j):
        link.arrived((tag, NEAR, j), r_a.at[q_rows(j)], {"tensor": t_core})
        link.arrived((tag, FAR, j), r_x.at[q_rows(j)], {"tensor": t_far})

    chunk = 32

    def row_loop(fn):
        lax.fori_loop(0, quarter // chunk, lambda i, carry: fn(i * chunk) or carry, 0)

    def summed(j, r):
        loc = seq_rows(j, t * quarter + r, chunk)
        buf = pl.ds(al(j * quarter + r, 16), chunk)
        return (
            part[loc, :].astype(F32)
            + r_a[buf, :].astype(F32)
            + r_x[buf, :].astype(F32)
        )

    def add_sum(row, value):
        acc[row : row + 1, :] += jnp.sum(value, axis=0, keepdims=True)

    def two_halves(tag, j, fn):
        if tag > R1:
            for what in (NEAR_ON, NEAR, FAR):
                link.sent((tag - 1, what, j))
        fn(al(j * full + (1 - x) * half, 16))
        rs_start_far(tag, j)
        fn(al(j * full + x * half, 16))
        rs_start_near(tag, j)

    def by_tiles(n, fn):
        lax.fori_loop(0, n // tile, lambda i, carry: fn(al(i * tile, tile)) or carry, 0)


    def spread_vectors():
        for i in range(owners):
            e = t * owners + i
            for r in range(ebias_rows):
                ebias[0:1, (i * ebias_rows + r) * dw : (i * ebias_rows + r + 1) * dw] = vec[
                    8 + r : 9 + r, pl.ds(al(e * dw, 128), dw)
                ]


    def project(j):
        at = pl.ds(j * full, full)
        for w in range(3):
            span = slice(w * hw, (w + 1) * hw)
            value = mm(x_all[at, :], w3_all[w])
            if w == 0:
                value = value + vec[0:1, pl.ds(al(t * hw, 128), hw)]
            if w == 2:
                value = value + vec[1:2, pl.ds(al(t * hw, 128), hw)]
            qkv[at, span] = value.astype(BF)

    lane_head = lax.broadcasted_iota(jnp.int32, (full, hw), 1) // HEAD_DIM
    scale2 = LOG2E / math.sqrt(HEAD_DIM)

    def head_scores(j, h, at):
        q_head = jnp.where(lane_head == h, qkv[at, 0:hw], jnp.zeros((), BF))
        raw = mm_t(qkv[at, hw : 2 * hw], q_head)
        key_row = lax.broadcasted_iota(jnp.int32, (full, 1), 0)
        visible = key_row < lengths_s[d * n_seq + j]
        return q_head, jnp.where(visible, raw * scale2, MASKED)

    def attention(j):
        at = pl.ds(j * full, full)
        kt[...] = jnp.transpose(qkv[at, 2 * hw : 3 * hw])

        def head(h, carry):
            span = pl.ds(al(h * HEAD_DIM, HEAD_DIM), HEAD_DIM)
            _, scores = head_scores(j, h, at)
            top = jnp.max(scores, axis=0, keepdims=True)
            e = jnp.exp2(scores - top)
            total = jnp.sum(e, axis=0, keepdims=True)
            o = mm(kt[span, :], e.astype(BF))
            ot[span, :] = o * (1.0 / total)
            lse[j, pl.ds(h, 1), :] = top + jnp.log2(total)
            return carry

        lax.fori_loop(0, heads, head, 0)
        att[at, :] = jnp.transpose(ot[...]).astype(BF)

    def project_out(j):
        def part_rows(start):
            def go(n):
                part[pl.ds(start, half), pl.ds(n, tile)] = mm(
                    att[pl.ds(start, half), :], wo_all[:, pl.ds(n, tile)]
                ).astype(BF)

            by_tiles(width, go)

        two_halves(R1, j, part_rows)

    def norm_first(j):
        def go(r):
            loc = seq_rows(j, t * quarter + r, chunk)
            buf = pl.ds(al(j * quarter + r, 16), chunk)
            h = x_all[loc, :].astype(F32) + (summed(j, r) + vec[2:3, :])
            center = h - jnp.mean(h, axis=-1, keepdims=True)
            inv = lax.rsqrt(jnp.mean(center * center, axis=-1, keepdims=True) + EPSILON)
            scaled = center * inv
            n1[buf, :] = scaled
            inv1[buf, :] = jnp.broadcast_to(inv, (chunk, 128))
            u_all[loc, :] = (scaled * vec[6:7, :] + vec[3:4, :]).astype(BF)

        row_loop(go)

    def widen(j):
        at = pl.ds(j * full, full)

        def go(n):
            f = mm(u_all[at, :], we_all[:, pl.ds(n, tile)]) + ebias[0:1, pl.ds(n, tile)]
            cdf = 0.5 + 0.5 * lax.erf(f * (1.0 / math.sqrt(2.0)))
            hid[at, pl.ds(n, tile)] = (f * cdf).astype(BF)
            bell = jnp.exp2((f * f) * (-0.5 * LOG2E)) * (1.0 / math.sqrt(2.0 * math.pi))
            slope[at, pl.ds(n, tile)] = (cdf + f * bell).astype(BF)

        by_tiles(fw, go)

    def shrink_rows(j):
        def part_rows(start):
            def go(n):
                part[pl.ds(start, half), pl.ds(n, tile)] = mm(
                    hid[pl.ds(start, half), :], ws_all[:, pl.ds(n, tile)]
                ).astype(BF)

            by_tiles(width, go)

        two_halves(R2, j, part_rows)

    def norm_second(j):
        length = lengths_s[d * n_seq + j]

        def go(r):
            loc = seq_rows(j, t * quarter + r, chunk)
            buf = pl.ds(al(j * quarter + r, 16), chunk)
            u = n1[buf, :] * vec[6:7, :] + vec[3:4, :]
            total = u + (summed(j, r) + vec[4:5, :])
            center = total - jnp.mean(total, axis=-1, keepdims=True)
            inv = lax.rsqrt(jnp.mean(center * center, axis=-1, keepdims=True) + EPSILON)
            scaled = center * inv
            mixed_send[j, pl.ds(al(r, 16), chunk), :] = (scaled * vec[7:8, :] + vec[5:6, :]).astype(BF)
            place = t * quarter + r + lax.broadcasted_iota(jnp.int32, (chunk, 1), 0)
            valid = (place < length).astype(F32)
            e = cots[j, pl.ds(al(r, 16), chunk), :].astype(F32) * valid
            add_sum(5, e)
            add_sum(7, e * scaled)
            pushed = e * vec[7:8, :]
            first = jnp.mean(pushed, axis=-1, keepdims=True)
            second = jnp.mean(pushed * scaled, axis=-1, keepdims=True)
            grad = inv * (pushed - first - scaled * second)
            add_sum(4, grad)
            dy[buf, :] = grad
            dz[loc, :] = grad.astype(BF)

        row_loop(go)

    def rows_out(tag, j, count, src, dst):
        for o in range(1, n_dp):
            e = dp_to(o)
            link.send(
                (tag, j, o),
                src.at[pl.ds(j, count), pl.ds(al(e * rows, 16), rows)],
                dst.at[pl.ds(d * n_seq + j, count)],
                {"dp": e},
            )
        own_copies[tag, j] = link.local(
            src.at[pl.ds(j, count), pl.ds(al(d * rows, 16), rows)],
            dst.at[pl.ds(d * n_seq + j, count)],
        )

    def rows_in(tag, j, count, dst):
        own_copies.pop((tag, j)).wait()
        for o in range(1, n_dp):
            e = dp_from(o)
            link.arrived((tag, j, o), dst.at[pl.ds(e * n_seq + j, count)], {"dp": e})


    def widen_back(j):
        at = pl.ds(j * full, full)

        def go(n):
            spread = mm_t(dz[at, :], ws_all[pl.ds(n, tile), :])
            grad = (spread * slope[at, pl.ds(n, tile)].astype(F32)).astype(BF)
            slope[at, pl.ds(n, tile)] = grad
            hacc[0:1, pl.ds(n, tile)] += jnp.sum(grad.astype(F32), axis=0, keepdims=True)

        by_tiles(fw, go)

    def normed_rows(j):
        def part_rows(start):
            def go(n):
                part[pl.ds(start, half), pl.ds(n, tile)] = mm_t(
                    slope[pl.ds(start, half), :], we_all[pl.ds(n, tile), :]
                ).astype(BF)

            by_tiles(width, go)

        two_halves(R3, j, part_rows)

    def norm_first_back(j):
        def go(r):
            loc = seq_rows(j, t * quarter + r, chunk)
            buf = pl.ds(al(j * quarter + r, 16), chunk)
            du = dy[buf, :] + summed(j, r)
            scaled = n1[buf, :]
            add_sum(3, du)
            add_sum(6, du * scaled)
            pushed = du * vec[6:7, :]
            first = jnp.mean(pushed, axis=-1, keepdims=True)
            second = jnp.mean(pushed * scaled, axis=-1, keepdims=True)
            grad = inv1[buf, 0:1] * (pushed - first - scaled * second)
            add_sum(2, grad)
            dy[buf, :] = grad
            dh[loc, :] = grad.astype(BF)

        row_loop(go)

    def attention_back(j, between=None):
        at = pl.ds(j * full, full)
        da[...] = mm_t(dh[at, :], wo_all[...]).astype(BF)
        kt[...] = jnp.transpose(qkv[at, hw : 2 * hw])
        dk_acc[...] = jnp.zeros_like(dk_acc)
        dv_acc[...] = jnp.zeros_like(dv_acc)

        def head(h, carry):
            span = pl.ds(al(h * HEAD_DIM, HEAD_DIM), HEAD_DIM)
            q_head, scores = head_scores(j, h, at)
            da_head = jnp.where(lane_head == h, da[...], jnp.zeros((), BF))
            p = jnp.exp2(scores - lse[j, pl.ds(h, 1), :])
            dp = mm_t(qkv[at, 2 * hw : 3 * hw], da_head)
            inner = jnp.sum(p * dp, axis=0, keepdims=True)
            ds = (p * (dp - inner)).astype(BF)
            dv_acc[...] += mm(p.astype(BF), da_head)
            dk_acc[...] += mm(ds, q_head)
            ot[span, :] = mm(kt[span, :], ds)
            return carry

        lax.fori_loop(0, heads, head, 0)
        scale = 1.0 / math.sqrt(HEAD_DIM)
        grad_q = (jnp.transpose(ot[...]) * scale).astype(BF)
        grad_k = (dk_acc[...] * scale).astype(BF)
        grad_v = dv_acc[...].astype(BF)
        dqkv[at, 0:hw] = grad_q
        dqkv[at, hw : 2 * hw] = grad_k
        dqkv[at, 2 * hw : 3 * hw] = grad_v
        qacc[0:1, :] += jnp.sum(grad_q.astype(F32), axis=0, keepdims=True)
        qacc[1:2, :] += jnp.sum(grad_v.astype(F32), axis=0, keepdims=True)

    def token_rows(j):
        def part_rows(start):
            def go(n):
                total = None
                for w in range(3):
                    term = mm_t(
                        dqkv[pl.ds(start, half), w * hw : (w + 1) * hw],
                        w3_all[w, pl.ds(n, tile), :],
                    )
                    total = term if total is None else total + term
                part[pl.ds(start, half), pl.ds(n, tile)] = total.astype(BF)

            by_tiles(width, go)

        two_halves(R4, j, part_rows)

    def finish_rows(j):
        def go(r):
            buf = pl.ds(al(j * quarter + r, 16), chunk)
            back_send[j, pl.ds(al(r, 16), chunk), :] = (dy[buf, :] + summed(j, r)).astype(BF)

        row_loop(go)


    grads = {
        GS: (dz, hid, s.gs, s.gs_y, s.gs_z, out_gs),
        GE: (u_all, slope, s.ge, s.ge_y, s.ge_z, out_ge),
        GO: (dh, att, s.go, s.go_y, s.go_z, out_go),
        G3: (x_all, dqkv, s.g3, s.g3_y, s.g3_z, out_g3),
    }

    def owned(i):
        return pl.ds(al(i * dw, 16), dw)

    def grad_tile(name, k):
        left, right, whole, from_y, _, _ = grads[name]
        first = ((z + k) % n_z) * n_y
        both = pl.ds(al(first * dw, n_y * dw), n_y * dw)
        whole[both, :] = t_mm(left[:, both], right[...]).astype(BF)
        link.send(
            (name, OVER_Y, k),
            whole.at[owned(first + (1 - y))],
            from_y.at[owned(k)],
            {"dp": y_peer},
        )

    def grad_forward(name, k):
        _, _, whole, from_y, from_z, _ = grads[name]
        mid = from_y.at[owned(k)]
        link.arrived((name, OVER_Y, k), mid, {"dp": y_peer})
        owner = ((z + k) % n_z) * n_y + y
        pair = whole[owned(owner), :].astype(F32) + from_y[owned(k), :].astype(F32)
        from_y[owned(k), :] = pair.astype(BF)
        if k:
            link.send((name, OVER_Z, k), mid, from_z.at[owned(k - 1)], {"dp": z_to(k)})

    def grad_finish(name):
        _, _, _, from_y, from_z, out = grads[name]
        total = from_y[owned(0), :].astype(F32)
        for k in range(1, n_z):
            link.arrived((name, OVER_Z, k), from_z.at[owned(k - 1)], {"dp": z_from(k)})
            total = total + from_z[owned(k - 1), :].astype(F32)
        out[...] = total

    small_send, small_recv, small_t = s.small_send, s.small_recv, s.small_t

    def small_start():
        small_send[...] = jnp.zeros_like(small_send)
        for e in range(n_dp):
            small_send[e, 2:8, :] = acc[2:8, e * dw : (e + 1) * dw]
        for i in range(owners):
            e = t * owners + i
            small_send[e, 0:2, :] = qacc[0:2, i * dw : (i + 1) * dw]
            for r in range(ebias_rows):
                at = (i * ebias_rows + r) * dw
                small_send[e, 8 + r : 9 + r, :] = hacc[0:1, at : at + dw]
        for o in range(1, n_dp):
            e = dp_to(o)
            link.send((SMALL, o), small_send.at[e], small_recv.at[o], {"dp": e})

    def small_forward():
        total = small_send[d]
        for o in range(1, n_dp):
            link.arrived((SMALL, o), small_recv.at[o], {"dp": dp_from(o)})
            total = total + small_recv[o]
        small_t[t] = total
        for what, peer in ((NEAR, t_core), (FAR, t_far), (NEAR_ON, t_diag)):
            link.send((SMALL_T, what), small_t.at[t], small_t.at[t], {"tensor": peer})

    def small_finish():
        for what, peer in ((NEAR, t_core), (FAR, t_far), (NEAR_ON, t_diag)):
            link.arrived((SMALL_T, what), small_t.at[peer], {"tensor": peer})
        total = small_t[0]
        for i in range(1, n_t):
            total = total + small_t[i]
        out_small[...] = total


    gather_start(W3)
    gather_start(PACK)
    tokens_start(2)
    gather_start(WO)
    gather_step(PACK, RIGHT, 1)
    gather_step(W3, RIGHT, 1)
    gather_step(W3, LEFT, 1)
    gather_step(PACK, RIGHT, 2)
    gather_step(PACK, LEFT, 1)
    tokens_finish(2)
    ag_start(x_all, TX, 2)
    gather_step(WO, LEFT, 1)
    tokens_start(1)
    gather_step(W3, RIGHT, 2)
    gather_step(PACK, LEFT, 2)
    tokens_start(0)
    gather_step(PACK, RIGHT, 3)
    gather_step(WO, LEFT, 2)
    tokens_finish(1)
    ag_start(x_all, TX, 1)
    gather_step(WO, RIGHT, 1)
    gather_step(W3, LEFT, 2)
    gather_step(W3, RIGHT, 3)
    ag_forward(x_all, TX, 2)
    gather_step(PACK, LEFT, 3)
    gather_step(PACK, RIGHT, 4)
    ag_finish(x_all, TX, 2)
    gather_step(WO, LEFT, 3)
    tokens_finish(0)
    ag_start(x_all, TX, 0)
    ag_forward(x_all, TX, 1)
    gather_step(WO, RIGHT, 2)
    gather_start(WE)
    ag_finish(x_all, TX, 1)
    gather_step(W3, LEFT, 3)
    gather_step(W3, RIGHT, 4)
    gather_ready(PACK)
    spread_vectors()
    gather_ready(W3)
    gather_step(WO, LEFT, 4)
    project(2)
    attention(2)
    gather_step(WO, RIGHT, 3)
    project(1)
    gather_start(WS)
    ag_forward(x_all, TX, 0)
    gather_ready(WO)
    project_out(2)
    gather_step(WE, RIGHT, 1)
    ag_finish(x_all, TX, 0)
    gather_step(WE, LEFT, 1)
    rs_forward(R1, 2)
    attention(1)
    project_out(1)
    rs_forward(R1, 1)
    gather_step(WS, LEFT, 1)
    project(0)
    gather_step(WS, RIGHT, 1)
    attention(0)
    gather_step(WE, LEFT, 2)
    rs_finish(R1, 2)
    norm_first(2)
    ag_start(u_all, TU, 2)
    gather_step(WE, RIGHT, 2)
    rs_finish(R1, 1)
    norm_first(1)
    ag_start(u_all, TU, 1)
    gather_step(WS, LEFT, 2)
    project_out(0)
    gather_step(WE, RIGHT, 3)
    gather_step(WE, LEFT, 3)
    ag_forward(u_all, TU, 2)
    rs_forward(R1, 0)
    ag_forward(u_all, TU, 1)
    ag_finish(u_all, TU, 1)
    gather_step(WS, LEFT, 3)
    gather_step(WS, RIGHT, 2)
    gather_step(WE, RIGHT, 4)
    gather_ready(WE)
    widen(1)
    ag_finish(u_all, TU, 2)
    rs_finish(R1, 0)
    norm_first(0)
    ag_start(u_all, TU, 0)
    widen(2)
    cot_start()
    gather_step(WS, RIGHT, 3)
    gather_step(WS, LEFT, 4)
    gather_ready(WS)
    shrink_rows(1)
    rs_forward(R2, 1)
    shrink_rows(2)
    ag_forward(u_all, TU, 0)
    rs_forward(R2, 2)
    ag_finish(u_all, TU, 0)
    widen(0)
    shrink_rows(0)
    rs_forward(R2, 0)
    cot_finish()
    rs_finish(R2, 2)
    norm_second(2)
    ag_start(dz, TZ, 2)
    rs_finish(R2, 0)
    norm_second(0)
    ag_start(dz, TZ, 0)
    ag_forward(dz, TZ, 2)
    rs_finish(R2, 1)
    norm_second(1)
    ag_start(dz, TZ, 1)
    rows_out(MIX, 0, n_seq, mixed_send, out_mixed)
    ag_finish(dz, TZ, 2)
    widen_back(2)
    ag_forward(dz, TZ, 0)
    normed_rows(2)
    rs_forward(R3, 2)
    ag_forward(dz, TZ, 1)
    ag_finish(dz, TZ, 1)
    ag_finish(dz, TZ, 0)
    grad_tile(GS, 1)
    widen_back(0)
    widen_back(1)
    rs_finish(R3, 2)
    norm_first_back(2)
    ag_start(dh, TH, 2)
    grad_tile(GS, 2)
    grad_forward(GS, 1)
    normed_rows(0)
    rs_forward(R3, 0)
    grad_tile(GS, 3)
    grad_forward(GS, 2)
    normed_rows(1)
    grad_tile(GE, 1)
    grad_forward(GS, 3)
    grad_tile(GE, 2)
    ag_forward(dh, TH, 2)
    rs_finish(R3, 0)
    norm_first_back(0)
    ag_start(dh, TH, 0)
    ag_finish(dh, TH, 2)
    rs_forward(R3, 1)
    attention_back(2)
    grad_forward(GE, 1)
    grad_tile(GS, 0)
    token_rows(2)
    ag_forward(dh, TH, 0)
    grad_tile(GE, 3)
    ag_finish(dh, TH, 0)
    rs_finish(R3, 1)
    norm_first_back(1)
    ag_start(dh, TH, 1)
    grad_forward(GE, 2)
    grad_forward(GS, 0)
    grad_tile(GE, 0)
    rs_forward(R4, 2)
    attention_back(0)
    grad_forward(GE, 3)
    ag_forward(dh, TH, 1)
    ag_finish(dh, TH, 1)
    grad_tile(GO, 1)
    token_rows(0)
    grad_tile(GO, 2)
    grad_tile(GO, 3)
    grad_finish(GS)
    rs_forward(R4, 0)
    rs_finish(R4, 2)
    finish_rows(2)
    rows_out(BACK, 2, 1, back_send, back_recv)
    rows_in(MIX, 0, n_seq, out_mixed)
    attention_back(1)
    grad_forward(GE, 0)
    grad_forward(GO, 3)
    grad_tile(GO, 0)
    grad_tile(G3, 1)
    grad_forward(GO, 2)
    grad_tile(G3, 2)
    small_start()
    rs_finish(R4, 0)
    finish_rows(0)
    rows_out(BACK, 0, 1, back_send, back_recv)
    small_forward()
    grad_forward(GO, 1)
    small_finish()
    grad_forward(G3, 1)
    grad_tile(G3, 3)
    token_rows(1)
    grad_forward(G3, 2)
    grad_forward(GO, 0)
    rs_forward(R4, 1)
    grad_forward(G3, 3)
    grad_finish(GO)
    rows_in(BACK, 2, 1, back_recv)
    rows_in(BACK, 0, 1, back_recv)
    grad_tile(G3, 0)
    grad_finish(GE)
    rs_finish(R4, 1)
    finish_rows(1)
    rows_out(BACK, 1, 1, back_send, back_recv)
    grad_forward(G3, 0)
    grad_finish(G3)
    rows_in(BACK, 1, 1, back_recv)
    link.drain()


def finish_kernel(
    ebias_rows,
    order_s,
    mixed,
    back,
    g3,
    go,
    ge,
    gs,
    small,
    out_mixed,
    out_back,
    out_g3,
    out_go,
    out_ge,
    out_gs,
    out_biases,
    out_gains,
    out_hidden,
):
    def move(k, carry):
        out_back[k] = back[order_s[k]]
        return carry

    lax.fori_loop(0, out_back.shape[0], move, 0)
    out_mixed[...] = mixed[...]
    width = out_g3.shape[2]
    for w in range(3):
        out_g3[w] = g3[:, w * width : (w + 1) * width]
    out_go[...] = jnp.transpose(go[...])
    out_gs[...] = jnp.transpose(gs[...])
    out_ge[...] = ge[...]
    out_biases[...] = small[0:6]
    out_gains[...] = small[6:8]
    out_hidden[...] = small[8 : 8 + ebias_rows]


def body(
    tokens,
    cotangent,
    lengths,
    order,
    triple_weight,
    output_weight,
    expand_weight,
    shrink_weight,
    biases,
    gains,
    expand_bias,
):
    n_dp, n_t = lax.axis_size("dp"), lax.axis_size("tensor")
    slots, _, rows, width = tokens.shape
    n_seq = slots // n_dp
    quarter = rows * n_dp
    full = quarter * n_t
    dw = triple_weight.shape[1]
    hw = triple_weight.shape[2]
    fw = expand_weight.shape[1]
    fits = (
        n_t == 4
        and n_dp % 4 == 0
        and rows % 16 == 0
        and dw % 128 == 0
        and hw % 128 == 0
        and n_seq == 3
        and expand_bias.shape[0] % dw == 0
        and n_dp % n_t == 0
    )
    if not fits:
        return plain_body(
            tokens,
            cotangent,
            lengths,
            order,
            triple_weight,
            output_weight,
            expand_weight,
            shrink_weight,
            biases,
            gains,
            expand_bias,
        )
    n_y = 2
    n_z = n_dp // n_y
    ebias_rows = expand_bias.shape[0] // dw
    all_rows = n_seq * full
    own_rows = n_seq * quarter
    vm = pltpu.VMEM
    scratch = dict(
        stage=vm((slots, rows, width), BF),
        x_all=vm((all_rows, width), BF),
        cots=vm((n_seq, quarter, width), BF),
        w3_all=vm((3, width, hw), BF),
        wo_all=vm((hw, width), BF),
        we_all=vm((width, fw), BF),
        ws_all=vm((fw, width), BF),
        pack_own=vm((16, dw), F32),
        vec=vm((16, width), F32),
        ebias=vm((8, fw), F32),
        qkv=vm((all_rows, 3 * hw), BF),
        att=vm((all_rows, hw), BF),
        lse=vm((n_seq, 8, full), F32),
        part=vm((all_rows, width), BF),
        r_a=vm((own_rows, width), BF),
        r_b=vm((own_rows, width), BF),
        r_x=vm((own_rows, width), BF),
        n1=vm((own_rows, width), F32),
        inv1=vm((own_rows, 128), F32),
        u_all=vm((all_rows, width), BF),
        hid=vm((all_rows, fw), BF),
        slope=vm((all_rows, fw), BF),
        dz=vm((all_rows, width), BF),
        dh=vm((all_rows, width), BF),
        dy=vm((own_rows, width), F32),
        dqkv=vm((all_rows, 3 * hw), BF),
        acc=vm((8, width), F32),
        hacc=vm((8, fw), F32),
        qacc=vm((8, hw), F32),
        kt=vm((hw, full), BF),
        ot=vm((hw, full), F32),
        dk_acc=vm((full, hw), F32),
        dv_acc=vm((full, hw), F32),
        da=vm((full, hw), BF),
        mixed_send=vm((n_seq, quarter, width), BF),
        back_send=vm((n_seq, quarter, width), BF),
        gs=vm((width, fw), BF),
        gs_y=vm((n_z * dw, fw), BF),
        gs_z=vm(((n_z - 1) * dw, fw), BF),
        ge=vm((width, fw), BF),
        ge_y=vm((n_z * dw, fw), BF),
        ge_z=vm(((n_z - 1) * dw, fw), BF),
        go=vm((width, hw), BF),
        go_y=vm((n_z * dw, hw), BF),
        go_z=vm(((n_z - 1) * dw, hw), BF),
        g3=vm((width, 3 * hw), BF),
        g3_y=vm((n_z * dw, 3 * hw), BF),
        g3_z=vm(((n_z - 1) * dw, 3 * hw), BF),
        small_send=vm((n_dp, 16, dw), F32),
        small_recv=vm((n_dp, 16, dw), F32),
        small_t=vm((n_t, 16, dw), F32),
        send_sems=pltpu.SemaphoreType.DMA((N_SEM,)),
        recv_sems=pltpu.SemaphoreType.DMA((N_SEM,)),
        local_sems=pltpu.SemaphoreType.DMA((24,)),
    )
    g = types.SimpleNamespace(
        n_seq=n_seq,
        quarter=quarter,
        width=width,
        n_dp=n_dp,
        n_y=n_y,
        n_t=n_t,
        head_width=hw,
        hidden_width=fw,
        ebias_rows=ebias_rows,
        scratch_names=tuple(scratch),
    )
    smem = pl.BlockSpec(memory_space=pltpu.SMEM)
    vmem = pl.BlockSpec(memory_space=pltpu.VMEM)
    anywhere = pl.BlockSpec(memory_space=pl.ANY)
    sds = jax.ShapeDtypeStruct
    flops = 2 * all_rows * (3 * width * 3 * hw + 3 * width * hw + 6 * width * fw + 7 * full * hw)
    mixed, back, g3, go, ge, gs, small = pl.pallas_call(
        functools.partial(layer_kernel, g),
        out_shape=(
            sds(tokens.shape[:1] + (rows, width), BF),
            sds(tokens.shape[:1] + (rows, width), BF),
            sds((dw, 3 * hw), F32),
            sds((dw, hw), F32),
            sds((dw, fw), F32),
            sds((dw, fw), F32),
            sds((16, dw), F32),
        ),
        in_specs=[smem] * 2 + [vmem] + [anywhere] * 5 + [vmem] * 3,
        out_specs=[anywhere] * 2 + [vmem] * 5,
        scratch_shapes=list(scratch.values()),
        compiler_params=pltpu.CompilerParams(
            collective_id=0,
            has_side_effects=True,
            vmem_limit_bytes=VMEM_BYTES,
        ),
        cost_estimate=pl.CostEstimate(flops=flops, bytes_accessed=1 << 24, transcendentals=0),
    )(
        order,
        lengths,
        tokens.reshape(slots, rows, width),
        cotangent.reshape(slots, rows, width),
        triple_weight,
        output_weight,
        expand_weight,
        shrink_weight,
        biases,
        gains,
        expand_bias.reshape(ebias_rows, dw),
    )
    finals = pl.pallas_call(
        functools.partial(finish_kernel, ebias_rows),
        out_shape=(
            sds(mixed.shape, BF),
            sds(back.shape, BF),
            sds((3, dw, hw), F32),
            sds((hw, dw), F32),
            sds((dw, fw), F32),
            sds((fw, dw), F32),
            sds((6, dw), F32),
            sds((2, dw), F32),
            sds((ebias_rows, dw), F32),
        ),
        in_specs=[smem] + [vmem] * 7,
        out_specs=[vmem] * 9,
        compiler_params=pltpu.CompilerParams(vmem_limit_bytes=VMEM_BYTES),
    )(order, mixed, back, g3, go, ge, gs, small)
    return (
        finals[0].reshape(tokens.shape),
        finals[1].reshape(tokens.shape),
        *finals[2:8],
        finals[8].reshape(expand_bias.shape),
    )


def solution(mesh):
    return jax.shard_map(
        body,
        mesh=mesh,
        in_specs=(
            P(None, "tensor", "dp", None),
            P(None, "tensor", "dp", None),
            P(),
            P(),
            P(None, "dp", "tensor"),
            P(None, "dp"),
            P("dp", "tensor"),
            P("tensor", "dp"),
            P(None, "dp"),
            P(None, "dp"),
            P("dp"),
        ),
        out_specs=(
            P(None, "tensor", "dp", None),
            P(None, "tensor", "dp", None),
            P(None, "dp", "tensor"),
            P("tensor", "dp"),
            P("dp", "tensor"),
            P("tensor", "dp"),
            P(None, "dp"),
            P(None, "dp"),
            P("dp"),
        ),
        check_vma=False,
    )
```

```python
import functools
import math
import types

import jax
import jax.numpy as jnp
from jax import lax
from jax.experimental import pallas as pl
from jax.experimental.pallas import tpu as pltpu
from jax.sharding import PartitionSpec as P

HEAD_DIM = 64


EPSILON = 1e-12
MASKED = -1e30


def normalize(values, gain, shift):
    center = values - jnp.mean(values, axis=-1, keepdims=True)
    spread = jnp.mean(center * center, axis=-1, keepdims=True)
    inv_std = lax.rsqrt(spread + EPSILON)
    scaled = center * inv_std
    return (scaled * gain + shift, scaled, inv_std)


def normalize_back(grad_rows, scaled, inv_std, gain):
    pushed = grad_rows * gain
    first = jnp.mean(pushed, axis=-1, keepdims=True)
    second = jnp.mean(pushed * scaled, axis=-1, keepdims=True)
    return inv_std * (pushed - first - scaled * second)


def gelu_exact(values):
    return 0.5 * values * (1.0 + jax.scipy.special.erf(values / math.sqrt(2.0)))


def gelu_slope(values):
    return 0.5 * (1.0 + jax.scipy.special.erf(values / math.sqrt(2.0))) + values * jnp.exp(
        -0.5 * values * values
    ) / math.sqrt(2.0 * math.pi)


def split_heads(rows):
    return rows.reshape(rows.shape[0], rows.shape[1] // HEAD_DIM, HEAD_DIM)


def score_block(queries, key_rows, seq_length):
    raw_scores = jnp.einsum("qhe,khe->hqk", queries, key_rows, preferred_element_type=jnp.float32)
    scores = raw_scores * (1.0 / math.sqrt(HEAD_DIM))
    visible = jnp.arange(key_rows.shape[0]) < seq_length
    return jnp.where(visible[None, None, :], scores, MASKED)


def attend(seq_item):
    queries, key_rows, value_rows, seq_length = seq_item
    queries = split_heads(queries)
    key_rows = split_heads(key_rows)
    value_rows = split_heads(value_rows)
    masked = score_block(queries, key_rows, seq_length)
    highest = jnp.max(masked, axis=-1, keepdims=True)
    totals = jnp.sum(jnp.exp(masked - highest), axis=-1, keepdims=True)
    log_totals = highest + jnp.log(totals)
    probs = jnp.exp(masked - log_totals).astype(jnp.bfloat16)
    blended = jnp.einsum("hqk,khe->qhe", probs, value_rows, preferred_element_type=jnp.float32)
    return (blended.astype(jnp.bfloat16).reshape(queries.shape[0], -1), log_totals[..., 0])


def attend_back(seq_item):
    queries, key_rows, value_rows, grad_rows, log_totals, seq_length = seq_item
    queries = split_heads(queries)
    key_rows = split_heads(key_rows)
    value_rows = split_heads(value_rows)
    grad_heads = split_heads(grad_rows)
    masked = score_block(queries, key_rows, seq_length)
    probs = jnp.exp(masked - log_totals[..., None])
    grad_probs = jnp.einsum(
        "qhe,khe->hqk", grad_heads, value_rows, preferred_element_type=jnp.float32
    )
    inner = jnp.sum(probs * grad_probs, axis=-1, keepdims=True)
    grad_scores = (probs * (grad_probs - inner)).astype(jnp.bfloat16)
    score_scale = 1.0 / math.sqrt(HEAD_DIM)
    grad_query = (
        jnp.einsum("hqk,khe->qhe", grad_scores, key_rows, preferred_element_type=jnp.float32)
        * score_scale
    )
    grad_key = (
        jnp.einsum("hqk,qhe->khe", grad_scores, queries, preferred_element_type=jnp.float32)
        * score_scale
    )
    grad_value = jnp.einsum(
        "hqk,qhe->khe", probs.astype(jnp.bfloat16), grad_heads, preferred_element_type=jnp.float32
    )
    row_count = queries.shape[0]
    return (
        grad_query.astype(jnp.bfloat16).reshape(row_count, -1),
        grad_key.astype(jnp.bfloat16).reshape(row_count, -1),
        grad_value.astype(jnp.bfloat16).reshape(row_count, -1),
    )


def plain_body(
    tokens,
    cotangent,
    lengths,
    order,
    triple_weight,
    output_weight,
    expand_weight,
    shrink_weight,
    biases,
    gains,
    expand_bias,
):
    seq_count = order.shape[0]
    per_group = seq_count // lax.axis_size("dp")
    tensor_size = lax.axis_size("tensor")
    member = lax.axis_index("dp")
    my_rank = lax.axis_index("tensor")
    slot_ids = jnp.arange(seq_count, dtype=jnp.int32)
    inverse = jnp.zeros((seq_count,), jnp.int32).at[order].set(slot_ids)
    local_x, local_dy = (
        lax.all_to_all(tokens[inverse], "dp", split_axis=0, concat_axis=2, tiled=True),
        lax.all_to_all(cotangent, "dp", split_axis=0, concat_axis=2, tiled=True),
    )
    quarter = local_x.shape[2]
    model_width = local_x.shape[3]
    full_length = quarter * tensor_size
    my_lengths = lax.dynamic_slice_in_dim(lengths, member * per_group, per_group)
    gathered = (
        lax.all_gather(triple_weight, "dp", axis=1, tiled=True),
        lax.all_gather(output_weight, "dp", axis=1, tiled=True),
        lax.all_gather(expand_weight, "dp", axis=0, tiled=True),
        lax.all_gather(shrink_weight, "dp", axis=1, tiled=True),
        lax.all_gather(biases, "dp", axis=1, tiled=True),
        lax.all_gather(gains, "dp", axis=1, tiled=True),
        lax.all_gather(expand_bias, "dp", axis=0, tiled=True),
    )
    query_key_value_proj, out_weight, widen_projection, shrink, bias_rows, gain_rows, exp_bias = (
        gathered
    )
    head_width = query_key_value_proj.shape[2]
    hidden_width = widen_projection.shape[1]
    out_heads = lax.dynamic_slice_in_dim(out_weight, my_rank * head_width, head_width, 0)
    bias_query = lax.dynamic_slice_in_dim(bias_rows[0], my_rank * head_width, head_width).astype(
        jnp.float32
    )
    bias_value = lax.dynamic_slice_in_dim(bias_rows[1], my_rank * head_width, head_width).astype(
        jnp.float32
    )
    bias_hidden = lax.dynamic_slice_in_dim(exp_bias, my_rank * hidden_width, hidden_width).astype(
        jnp.float32
    )
    bias_stack = jnp.stack([bias_query, jnp.zeros_like(bias_query), bias_value])
    gain_first = gain_rows[0].astype(jnp.float32)
    gain_second = gain_rows[1].astype(jnp.float32)
    full_shape = (per_group, tensor_size, quarter, model_width)
    token_all_rows = lax.all_gather(local_x, "tensor", axis=1, tiled=True).reshape(
        per_group, full_length, model_width
    )
    projected = (
        jnp.einsum(
            "jah,rhu->rjau",
            token_all_rows,
            query_key_value_proj,
            preferred_element_type=jnp.float32,
        )
        + bias_stack[:, None, None, :]
    ).astype(jnp.bfloat16)
    attended, log_totals = lax.map(attend, (projected[0], projected[1], projected[2], my_lengths))
    attn_terms = jnp.einsum(
        "sle,em->slm", attended, out_heads, preferred_element_type=jnp.float32
    ).reshape(full_shape)
    attn_sum = lax.psum_scatter(attn_terms, "tensor", scatter_dimension=1, tiled=True)
    hidden_in = local_x.astype(jnp.float32) + (attn_sum + bias_rows[2].astype(jnp.float32))
    normed, normed_scaled, normed_inv = normalize(
        hidden_in, gain_first, bias_rows[3].astype(jnp.float32)
    )
    normalized_all_rows = lax.all_gather(
        normed.astype(jnp.bfloat16), "tensor", axis=1, tiled=True
    ).reshape(per_group, full_length, model_width)
    pre_act = (
        jnp.einsum(
            "uqj,jt->uqt", normalized_all_rows, widen_projection, preferred_element_type=jnp.float32
        )
        + bias_hidden
    )
    hidden = gelu_exact(pre_act).astype(jnp.bfloat16)
    ffn_terms = jnp.einsum(
        "slf,fm->slm", hidden, shrink, preferred_element_type=jnp.float32
    ).reshape(full_shape)
    ffn_sum = lax.psum_scatter(
        ffn_terms.astype(jnp.bfloat16), "tensor", scatter_dimension=1, tiled=True
    ).astype(jnp.float32)
    total_rows = normed + (ffn_sum + bias_rows[4].astype(jnp.float32))
    output, out_scaled, out_inv = normalize(
        total_rows, gain_second, bias_rows[5].astype(jnp.float32)
    )
    positions = my_rank * quarter + jnp.arange(quarter)
    valid = (positions[None, :] < my_lengths[:, None]).astype(jnp.float32)
    grad_out = local_dy.astype(jnp.float32) * valid[:, None, :, None]
    row_axes = (0, 1, 2)
    gain_grad_second = jnp.sum(grad_out * out_scaled, axis=row_axes)
    shift_grad_second = jnp.sum(grad_out, axis=row_axes)
    grad_total = normalize_back(grad_out, out_scaled, out_inv, gain_second)
    branch_bias_grad = jnp.sum(grad_total, axis=row_axes)
    grad_branch = lax.all_gather(
        grad_total.astype(jnp.bfloat16), "tensor", axis=1, tiled=True
    ).reshape(per_group, full_length, model_width)
    shrink_grad = jnp.einsum("slf,slm->fm", hidden, grad_branch, preferred_element_type=jnp.float32)
    grad_hidden = jnp.einsum("slm,fm->slf", grad_branch, shrink, preferred_element_type=jnp.float32)
    preactivation_grad = (grad_hidden * gelu_slope(pre_act)).astype(jnp.bfloat16)
    hidden_bias_grad = jnp.sum(preactivation_grad, axis=(0, 1), dtype=jnp.float32)
    expand_grad = jnp.einsum(
        "mgc,mga->ca", normalized_all_rows, preactivation_grad, preferred_element_type=jnp.float32
    )
    normed_terms = jnp.einsum(
        "cpk,rk->cpr", preactivation_grad, widen_projection, preferred_element_type=jnp.float32
    ).reshape(full_shape)
    grad_normed = grad_total + lax.psum_scatter(
        normed_terms.astype(jnp.bfloat16), "tensor", scatter_dimension=1, tiled=True
    ).astype(jnp.float32)
    first_norm_gain_grad = jnp.sum(grad_normed * normed_scaled, axis=row_axes)
    shift_grad_first = jnp.sum(grad_normed, axis=row_axes)
    grad_hidden_in = normalize_back(grad_normed, normed_scaled, normed_inv, gain_first)
    out_bias_grad = jnp.sum(grad_hidden_in, axis=row_axes)
    grad_attn = lax.all_gather(
        grad_hidden_in.astype(jnp.bfloat16), "tensor", axis=1, tiled=True
    ).reshape(per_group, full_length, model_width)
    output_grad = jnp.einsum("sle,slm->em", attended, grad_attn, preferred_element_type=jnp.float32)
    grad_blended = jnp.einsum(
        "slm,em->sle", grad_attn, out_heads, preferred_element_type=jnp.float32
    ).astype(jnp.bfloat16)
    grad_query, grad_key, grad_value = lax.map(
        attend_back,
        (projected[0], projected[1], projected[2], grad_blended, log_totals, my_lengths),
    )
    projection_output_grad = jnp.stack([grad_query, grad_key, grad_value])
    query_bias_grad = jnp.sum(grad_query, axis=(0, 1), dtype=jnp.float32)
    value_bias_grad = jnp.sum(grad_value, axis=(0, 1), dtype=jnp.float32)
    triple_grad = jnp.einsum(
        "xyt,vxyu->vtu", token_all_rows, projection_output_grad, preferred_element_type=jnp.float32
    )
    token_terms = jnp.einsum(
        "atpi,aki->tpk",
        projection_output_grad,
        query_key_value_proj,
        preferred_element_type=jnp.float32,
    ).reshape(full_shape)
    grad_tokens = grad_hidden_in + lax.psum_scatter(
        token_terms.astype(jnp.bfloat16), "tensor", scatter_dimension=1, tiled=True
    ).astype(jnp.float32)
    zero_row = jnp.zeros((model_width,), jnp.float32)
    query_full = lax.dynamic_update_slice_in_dim(zero_row, query_bias_grad, my_rank * head_width, 0)
    value_full = lax.dynamic_update_slice_in_dim(zero_row, value_bias_grad, my_rank * head_width, 0)
    bias_grad = jnp.stack(
        [
            query_full,
            value_full,
            out_bias_grad,
            shift_grad_first,
            branch_bias_grad,
            shift_grad_second,
        ]
    )
    gain_grad = jnp.stack([first_norm_gain_grad, gain_grad_second])
    hidden_full = lax.dynamic_update_slice_in_dim(
        jnp.zeros((exp_bias.shape[0],), jnp.float32), hidden_bias_grad, my_rank * hidden_width, 0
    )
    bias_grad, gain_grad, hidden_full = (
        lax.psum(bias_grad.astype(jnp.bfloat16), "tensor").astype(jnp.float32),
        lax.psum(gain_grad.astype(jnp.bfloat16), "tensor").astype(jnp.float32),
        lax.psum(hidden_full.astype(jnp.bfloat16), "tensor").astype(jnp.float32),
    )
    shards = (
        lax.psum_scatter(triple_grad, "dp", scatter_dimension=1, tiled=True),
        lax.psum_scatter(output_grad, "dp", scatter_dimension=1, tiled=True),
        lax.psum_scatter(expand_grad, "dp", scatter_dimension=0, tiled=True),
        lax.psum_scatter(shrink_grad, "dp", scatter_dimension=1, tiled=True),
        lax.psum_scatter(bias_grad, "dp", scatter_dimension=1, tiled=True),
        lax.psum_scatter(gain_grad, "dp", scatter_dimension=1, tiled=True),
        lax.psum_scatter(hidden_full, "dp", scatter_dimension=0, tiled=True),
    )
    mixed_rows, back_rows = (
        lax.all_to_all(output.astype(jnp.bfloat16), "dp", split_axis=2, concat_axis=0, tiled=True),
        lax.all_to_all(
            grad_tokens.astype(jnp.bfloat16), "dp", split_axis=2, concat_axis=0, tiled=True
        ),
    )
    return (
        mixed_rows,
        back_rows[order],
        shards[0],
        shards[1],
        shards[2],
        shards[3],
        shards[4],
        shards[5],
        shards[6],
    )


BF = jnp.bfloat16
F32 = jnp.float32
MESH = pl.DeviceIdType.MESH
LOG2E = math.log2(math.e)
N_SEM = 147
PACK, W3, WO, WE, WS = range(5)
GS, GE, G3, GO = range(10, 14)
TX, TU, TZ, TH, R1, R2, R3, R4 = range(20, 28)
TOK, COT, MIX, BACK, SMALL, SMALL_T = range(30, 36)
RIGHT, LEFT, OVER_Y, OVER_Z, FAR, NEAR, NEAR_ON = range(40, 47)
VMEM_BYTES = 64 * 1024 * 1024


def mm(a, b):
    return lax.dot_general(a, b, (((1,), (0,)), ((), ())), preferred_element_type=F32)


def mm_t(a, b):
    return lax.dot_general(a, b, (((1,), (1,)), ((), ())), preferred_element_type=F32)


def t_mm(a, b):
    return lax.dot_general(a, b, (((0,), (0,)), ((), ())), preferred_element_type=F32)


class Links:
    def __init__(self, send_sems, recv_sems, local_sems):
        self.send_sems = send_sems
        self.recv_sems = recv_sems
        self.local_sems = local_sems
        self.slots = {}
        self.flying = {}
        self.local_count = 0

    def slot(self, name):
        if TX <= name[0] <= TH:
            name = (TX,) + name[1:]
        if R1 <= name[0] <= R4:
            name = (R1,) + name[1:]
        return self.slots.setdefault(name, len(self.slots))

    def send(self, name, src, dst, where):
        i = self.slot(name)
        if i in self.flying:
            self.sent(name)
        copy = pltpu.make_async_remote_copy(
            src_ref=src,
            dst_ref=dst,
            send_sem=self.send_sems.at[i],
            recv_sem=self.recv_sems.at[i],
            device_id=where,
            device_id_type=MESH,
        )
        copy.start()
        self.flying[i] = copy

    def sent(self, name):
        self.flying.pop(self.slot(name)).wait_send()

    def arrived(self, name, dst, where):
        i = self.slot(name)
        pltpu.make_async_remote_copy(
            src_ref=dst,
            dst_ref=dst,
            send_sem=self.send_sems.at[i],
            recv_sem=self.recv_sems.at[i],
            device_id=where,
            device_id_type=MESH,
        ).wait_recv()

    def drain(self):
        for copy in self.flying.values():
            copy.wait_send()

    def local(self, src, dst):
        copy = pltpu.make_async_copy(src, dst, self.local_sems.at[self.local_count])
        self.local_count += 1
        copy.start()
        return copy


def layer_kernel(g, *refs):
    (order_s, lengths_s, tok, cot, w3, wo, we, ws, bias_in, gain_in, hidden_in) = refs[:11]
    (out_mixed, back_recv, out_g3, out_go, out_ge, out_gs, out_small) = refs[11:18]
    s = types.SimpleNamespace(**dict(zip(g.scratch_names, refs[18:])))
    n_seq, quarter, width = g.n_seq, g.quarter, g.width
    n_dp, n_y, n_t = g.n_dp, g.n_y, g.n_t
    n_z = n_dp // n_y
    full = n_t * quarter
    half = full // 2
    rows = quarter // n_dp
    hw, fw = g.head_width, g.hidden_width
    heads = hw // HEAD_DIM
    dw = width // n_dp
    tile = 256
    ebias_rows = g.ebias_rows
    owners = n_dp // n_t

    d = lax.axis_index("dp")
    t = lax.axis_index("tensor")
    z, y = d // n_y, d % n_y
    x, c = t // 2, t % 2
    t_core = x * 2 + (1 - c)
    t_far = (1 - x) * 2 + c
    t_diag = (1 - x) * 2 + (1 - c)

    def dp_to(o):
        return (d + o) % n_dp

    def dp_from(o):
        return (d + n_dp - o) % n_dp

    def z_to(k):
        return ((z + k) % n_z) * n_y + y

    def z_from(k):
        return ((z + n_z - k) % n_z) * n_y + y

    y_peer = z * n_y + (1 - y)
    ring = (1 - y) * z + y * (n_dp - 1 - z)

    def ring_at(k):
        r = (ring + n_dp + k) % n_dp
        back = r // n_z
        return ((1 - back) * r + back * (n_dp - 1 - r)) * n_y + back

    link = Links(s.send_sems, s.recv_sems, s.local_sems)

    barrier = pltpu.get_barrier_semaphore()
    for o in range(1, n_dp):
        pl.semaphore_signal(barrier, inc=1, device_id={"dp": dp_to(o)}, device_id_type=MESH)
    for peer in (t_core, t_far, t_diag):
        pl.semaphore_signal(barrier, inc=1, device_id={"tensor": peer}, device_id_type=MESH)

    stage, x_all, cots = s.stage, s.x_all, s.cots
    w3_all, wo_all, we_all, ws_all = s.w3_all, s.wo_all, s.we_all, s.ws_all
    pack_own, vec, ebias = s.pack_own, s.vec, s.ebias
    qkv, att, lse, part = s.qkv, s.att, s.lse, s.part
    r_a, r_b, r_x = s.r_a, s.r_b, s.r_x
    n1, inv1, u_all, hid, slope = s.n1, s.inv1, s.u_all, s.hid, s.slope
    dz, dh, dy, dqkv = s.dz, s.dh, s.dy, s.dqkv
    acc, hacc, qacc = s.acc, s.hacc, s.qacc
    kt, ot, dk_acc, dv_acc, da = s.kt, s.ot, s.dk_acc, s.dv_acc, s.da
    mixed_send, back_send = s.mixed_send, s.back_send

    def al(v, m):
        return pl.multiple_of(v, m)

    def seq_rows(j, start, n):
        return pl.ds(al(j * full + start, 16), n)

    def mine(j):
        return seq_rows(j, t * quarter, quarter)


    def permute(k, carry):
        arrival = jnp.int32(0)
        for i in range(n_dp * n_seq):
            arrival = jnp.where(order_s[i] == k, i, arrival)
        stage[k] = tok[arrival]
        return carry

    lax.fori_loop(0, n_dp * n_seq, permute, 0)
    pack_own[0:6, :] = bias_in[...].astype(F32)
    pack_own[6:8, :] = gain_in[...].astype(F32)
    pack_own[8 : 8 + ebias_rows, :] = hidden_in[...].astype(F32)
    pack_own[8 + ebias_rows :, :] = jnp.zeros((16 - 8 - ebias_rows, dw), F32)
    acc[...] = jnp.zeros_like(acc)
    hacc[...] = jnp.zeros_like(hacc)
    qacc[...] = jnp.zeros_like(qacc)
    pl.semaphore_wait(barrier, n_dp - 1 + 3)

    def x_block(j, src):
        return x_all.at[seq_rows(j, t * quarter + src * rows, rows)]

    def tokens_start(j):
        for o in range(1, n_dp):
            e = dp_to(o)
            link.send((TOK, j, o), stage.at[e * n_seq + j], x_block(j, d), {"dp": e})
        x_all[seq_rows(j, t * quarter + d * rows, rows), :] = stage[d * n_seq + j]

    def tokens_finish(j):
        for o in range(1, n_dp):
            link.arrived((TOK, j, o), x_block(j, dp_from(o)), {"dp": dp_from(o)})

    def cot_block(src):
        return cots.at[:, pl.ds(al(src * rows, 16), rows), :]

    own_copies = {}

    def cot_start():
        for o in range(1, n_dp):
            e = dp_to(o)
            link.send((COT, o), cot.at[pl.ds(e * n_seq, n_seq)], cot_block(d), {"dp": e})
        own_copies[COT] = link.local(cot.at[pl.ds(d * n_seq, n_seq)], cot_block(d))

    def cot_finish():
        own_copies.pop(COT).wait()
        for o in range(1, n_dp):
            link.arrived((COT, o), cot_block(dp_from(o)), {"dp": dp_from(o)})

    def cols(ref, e):
        return ref.at[:, pl.ds(al(e * dw, 128), dw)]

    def row_block(ref, e):
        return ref.at[pl.ds(al(e * dw, 16), dw), :]

    def w3_block(e):
        return w3_all.at[:, pl.ds(al(e * dw, 16), dw), :]

    gathers = {
        PACK: (pack_own, lambda e: cols(vec, e), n_dp // 2),
        W3: (w3, w3_block, n_dp // 2),
        WO: (
            wo.at[pl.ds(al(t * hw, 16), hw), :],
            lambda e: cols(wo_all, e),
            n_dp // 2 - 1,
        ),
        WE: (we, lambda e: row_block(we_all, e), n_dp // 2),
        WS: (ws, lambda e: cols(ws_all, e), n_dp // 2 - 1),
    }

    def gather_start(name):
        src, block, _ = gathers[name]
        link.send((name, RIGHT, 1), src, block(d), {"dp": ring_at(1)})
        link.send((name, LEFT, 1), src, block(d), {"dp": ring_at(-1)})
        own_copies[name] = link.local(src, block(d))

    def gather_step(name, way, k):
        _, block, right = gathers[name]
        steps, sign = (right, -1) if way == RIGHT else (n_dp - 1 - right, 1)
        got = block(ring_at(sign * k))
        link.arrived((name, way, k), got, {"dp": ring_at(sign)})
        if k < steps:
            link.send((name, way, k + 1), got, got, {"dp": ring_at(-sign)})

    def gather_ready(name):
        own_copies.pop(name).wait()


    def t_rows(j, who):
        return seq_rows(j, who * quarter, quarter)

    def ag_start(buf, tag, j):
        own = buf.at[t_rows(j, t)]
        link.send((tag, FAR, j), own, own, {"tensor": t_far})
        link.send((tag, NEAR, j), own, own, {"tensor": t_core})

    def ag_forward(buf, tag, j):
        got = buf.at[t_rows(j, t_far)]
        link.arrived((tag, FAR, j), got, {"tensor": t_far})
        link.send((tag, NEAR_ON, j), got, got, {"tensor": t_core})

    def ag_finish(buf, tag, j):
        link.arrived((tag, NEAR, j), buf.at[t_rows(j, t_core)], {"tensor": t_core})
        link.arrived((tag, NEAR_ON, j), buf.at[t_rows(j, t_diag)], {"tensor": t_core})

    def q_rows(j):
        return pl.ds(j * quarter, quarter)

    def rs_start_far(tag, j):
        link.send((tag, NEAR_ON, j), part.at[t_rows(j, t_diag)], r_b.at[q_rows(j)], {"tensor": t_core})

    def rs_start_near(tag, j):
        link.send((tag, NEAR, j), part.at[t_rows(j, t_core)], r_a.at[q_rows(j)], {"tensor": t_core})

    def rs_forward(tag, j):
        link.arrived((tag, NEAR_ON, j), r_b.at[q_rows(j)], {"tensor": t_core})
        far = t_rows(j, t_far)
        both = part[far, :].astype(F32) + r_b[q_rows(j), :].astype(F32)
        part[far, :] = both.astype(BF)
        link.send((tag, FAR, j), part.at[far], r_x.at[q_rows(j)], {"tensor": t_far})

    def rs_finish(tag, j):
        link.arrived((tag, NEAR, j), r_a.at[q_rows(j)], {"tensor": t_core})
        link.arrived((tag, FAR, j), r_x.at[q_rows(j)], {"tensor": t_far})

    chunk = 32

    def row_loop(fn):
        lax.fori_loop(0, quarter // chunk, lambda i, carry: fn(i * chunk) or carry, 0)

    def summed(j, r):
        loc = seq_rows(j, t * quarter + r, chunk)
        buf = pl.ds(al(j * quarter + r, 16), chunk)
        return (
            part[loc, :].astype(F32)
            + r_a[buf, :].astype(F32)
            + r_x[buf, :].astype(F32)
        )

    def add_sum(row, value):
        acc[row : row + 1, :] += jnp.sum(value, axis=0, keepdims=True)

    def two_halves(tag, j, fn):
        if tag > R1:
            for what in (NEAR_ON, NEAR, FAR):
                link.sent((tag - 1, what, j))
        fn(al(j * full + (1 - x) * half, 16))
        rs_start_far(tag, j)
        fn(al(j * full + x * half, 16))
        rs_start_near(tag, j)

    def by_tiles(n, fn):
        lax.fori_loop(0, n // tile, lambda i, carry: fn(al(i * tile, tile)) or carry, 0)


    def spread_vectors():
        for i in range(owners):
            e = t * owners + i
            for r in range(ebias_rows):
                ebias[0:1, (i * ebias_rows + r) * dw : (i * ebias_rows + r + 1) * dw] = vec[
                    8 + r : 9 + r, pl.ds(al(e * dw, 128), dw)
                ]


    def project(j):
        at = pl.ds(j * full, full)
        for w in range(3):
            span = slice(w * hw, (w + 1) * hw)
            value = mm(x_all[at, :], w3_all[w])
            if w == 0:
                value = value + vec[0:1, pl.ds(al(t * hw, 128), hw)]
            if w == 2:
                value = value + vec[1:2, pl.ds(al(t * hw, 128), hw)]
            qkv[at, span] = value.astype(BF)

    lane_head = lax.broadcasted_iota(jnp.int32, (full, hw), 1) // HEAD_DIM
    scale2 = LOG2E / math.sqrt(HEAD_DIM)

    def head_scores(j, h, at):
        q_head = jnp.where(lane_head == h, qkv[at, 0:hw], jnp.zeros((), BF))
        raw = mm_t(qkv[at, hw : 2 * hw], q_head)
        key_row = lax.broadcasted_iota(jnp.int32, (full, 1), 0)
        visible = key_row < lengths_s[d * n_seq + j]
        return q_head, jnp.where(visible, raw * scale2, MASKED)

    def attention(j):
        at = pl.ds(j * full, full)
        kt[...] = jnp.transpose(qkv[at, 2 * hw : 3 * hw])

        def head(h, carry):
            span = pl.ds(al(h * HEAD_DIM, HEAD_DIM), HEAD_DIM)
            _, scores = head_scores(j, h, at)
            top = jnp.max(scores, axis=0, keepdims=True)
            e = jnp.exp2(scores - top)
            total = jnp.sum(e, axis=0, keepdims=True)
            o = mm(kt[span, :], e.astype(BF))
            ot[span, :] = o * (1.0 / total)
            lse[j, pl.ds(h, 1), :] = top + jnp.log2(total)
            return carry

        lax.fori_loop(0, heads, head, 0)
        att[at, :] = jnp.transpose(ot[...]).astype(BF)

    def project_out(j):
        def part_rows(start):
            def go(n):
                part[pl.ds(start, half), pl.ds(n, tile)] = mm(
                    att[pl.ds(start, half), :], wo_all[:, pl.ds(n, tile)]
                ).astype(BF)

            by_tiles(width, go)

        two_halves(R1, j, part_rows)

    def norm_first(j):
        def go(r):
            loc = seq_rows(j, t * quarter + r, chunk)
            buf = pl.ds(al(j * quarter + r, 16), chunk)
            h = x_all[loc, :].astype(F32) + (summed(j, r) + vec[2:3, :])
            center = h - jnp.mean(h, axis=-1, keepdims=True)
            inv = lax.rsqrt(jnp.mean(center * center, axis=-1, keepdims=True) + EPSILON)
            scaled = center * inv
            n1[buf, :] = scaled
            inv1[buf, :] = jnp.broadcast_to(inv, (chunk, 128))
            u_all[loc, :] = (scaled * vec[6:7, :] + vec[3:4, :]).astype(BF)

        row_loop(go)

    def widen(j):
        at = pl.ds(j * full, full)

        def go(n):
            f = mm(u_all[at, :], we_all[:, pl.ds(n, tile)]) + ebias[0:1, pl.ds(n, tile)]
            cdf = 0.5 + 0.5 * lax.erf(f * (1.0 / math.sqrt(2.0)))
            hid[at, pl.ds(n, tile)] = (f * cdf).astype(BF)
            bell = jnp.exp2((f * f) * (-0.5 * LOG2E)) * (1.0 / math.sqrt(2.0 * math.pi))
            slope[at, pl.ds(n, tile)] = (cdf + f * bell).astype(BF)

        by_tiles(fw, go)

    def shrink_rows(j):
        def part_rows(start):
            def go(n):
                part[pl.ds(start, half), pl.ds(n, tile)] = mm(
                    hid[pl.ds(start, half), :], ws_all[:, pl.ds(n, tile)]
                ).astype(BF)

            by_tiles(width, go)

        two_halves(R2, j, part_rows)

    def norm_second(j):
        length = lengths_s[d * n_seq + j]

        def go(r):
            loc = seq_rows(j, t * quarter + r, chunk)
            buf = pl.ds(al(j * quarter + r, 16), chunk)
            u = n1[buf, :] * vec[6:7, :] + vec[3:4, :]
            total = u + (summed(j, r) + vec[4:5, :])
            center = total - jnp.mean(total, axis=-1, keepdims=True)
            inv = lax.rsqrt(jnp.mean(center * center, axis=-1, keepdims=True) + EPSILON)
            scaled = center * inv
            mixed_send[j, pl.ds(al(r, 16), chunk), :] = (scaled * vec[7:8, :] + vec[5:6, :]).astype(BF)
            place = t * quarter + r + lax.broadcasted_iota(jnp.int32, (chunk, 1), 0)
            valid = (place < length).astype(F32)
            e = cots[j, pl.ds(al(r, 16), chunk), :].astype(F32) * valid
            add_sum(5, e)
            add_sum(7, e * scaled)
            pushed = e * vec[7:8, :]
            first = jnp.mean(pushed, axis=-1, keepdims=True)
            second = jnp.mean(pushed * scaled, axis=-1, keepdims=True)
            grad = inv * (pushed - first - scaled * second)
            add_sum(4, grad)
            dy[buf, :] = grad
            dz[loc, :] = grad.astype(BF)

        row_loop(go)

    def rows_out(tag, j, count, src, dst):
        for o in range(1, n_dp):
            e = dp_to(o)
            link.send(
                (tag, j, o),
                src.at[pl.ds(j, count), pl.ds(al(e * rows, 16), rows)],
                dst.at[pl.ds(d * n_seq + j, count)],
                {"dp": e},
            )
        own_copies[tag, j] = link.local(
            src.at[pl.ds(j, count), pl.ds(al(d * rows, 16), rows)],
            dst.at[pl.ds(d * n_seq + j, count)],
        )

    def rows_in(tag, j, count, dst):
        own_copies.pop((tag, j)).wait()
        for o in range(1, n_dp):
            e = dp_from(o)
            link.arrived((tag, j, o), dst.at[pl.ds(e * n_seq + j, count)], {"dp": e})


    def widen_back(j):
        at = pl.ds(j * full, full)

        def go(n):
            spread = mm_t(dz[at, :], ws_all[pl.ds(n, tile), :])
            grad = (spread * slope[at, pl.ds(n, tile)].astype(F32)).astype(BF)
            slope[at, pl.ds(n, tile)] = grad
            hacc[0:1, pl.ds(n, tile)] += jnp.sum(grad.astype(F32), axis=0, keepdims=True)

        by_tiles(fw, go)

    def normed_rows(j):
        def part_rows(start):
            def go(n):
                part[pl.ds(start, half), pl.ds(n, tile)] = mm_t(
                    slope[pl.ds(start, half), :], we_all[pl.ds(n, tile), :]
                ).astype(BF)

            by_tiles(width, go)

        two_halves(R3, j, part_rows)

    def norm_first_back(j):
        def go(r):
            loc = seq_rows(j, t * quarter + r, chunk)
            buf = pl.ds(al(j * quarter + r, 16), chunk)
            du = dy[buf, :] + summed(j, r)
            scaled = n1[buf, :]
            add_sum(3, du)
            add_sum(6, du * scaled)
            pushed = du * vec[6:7, :]
            first = jnp.mean(pushed, axis=-1, keepdims=True)
            second = jnp.mean(pushed * scaled, axis=-1, keepdims=True)
            grad = inv1[buf, 0:1] * (pushed - first - scaled * second)
            add_sum(2, grad)
            dy[buf, :] = grad
            dh[loc, :] = grad.astype(BF)

        row_loop(go)

    def attention_back(j, between=None):
        at = pl.ds(j * full, full)
        da[...] = mm_t(dh[at, :], wo_all[...]).astype(BF)
        kt[...] = jnp.transpose(qkv[at, hw : 2 * hw])
        dk_acc[...] = jnp.zeros_like(dk_acc)
        dv_acc[...] = jnp.zeros_like(dv_acc)

        def head(h, carry):
            span = pl.ds(al(h * HEAD_DIM, HEAD_DIM), HEAD_DIM)
            q_head, scores = head_scores(j, h, at)
            da_head = jnp.where(lane_head == h, da[...], jnp.zeros((), BF))
            p = jnp.exp2(scores - lse[j, pl.ds(h, 1), :])
            dp = mm_t(qkv[at, 2 * hw : 3 * hw], da_head)
            inner = jnp.sum(p * dp, axis=0, keepdims=True)
            ds = (p * (dp - inner)).astype(BF)
            dv_acc[...] += mm(p.astype(BF), da_head)
            dk_acc[...] += mm(ds, q_head)
            ot[span, :] = mm(kt[span, :], ds)
            return carry

        lax.fori_loop(0, heads, head, 0)
        scale = 1.0 / math.sqrt(HEAD_DIM)
        grad_q = (jnp.transpose(ot[...]) * scale).astype(BF)
        grad_k = (dk_acc[...] * scale).astype(BF)
        grad_v = dv_acc[...].astype(BF)
        dqkv[at, 0:hw] = grad_q
        dqkv[at, hw : 2 * hw] = grad_k
        dqkv[at, 2 * hw : 3 * hw] = grad_v
        qacc[0:1, :] += jnp.sum(grad_q.astype(F32), axis=0, keepdims=True)
        qacc[1:2, :] += jnp.sum(grad_v.astype(F32), axis=0, keepdims=True)

    def token_rows(j):
        def part_rows(start):
            def go(n):
                total = None
                for w in range(3):
                    term = mm_t(
                        dqkv[pl.ds(start, half), w * hw : (w + 1) * hw],
                        w3_all[w, pl.ds(n, tile), :],
                    )
                    total = term if total is None else total + term
                part[pl.ds(start, half), pl.ds(n, tile)] = total.astype(BF)

            by_tiles(width, go)

        two_halves(R4, j, part_rows)

    def finish_rows(j):
        def go(r):
            buf = pl.ds(al(j * quarter + r, 16), chunk)
            back_send[j, pl.ds(al(r, 16), chunk), :] = (dy[buf, :] + summed(j, r)).astype(BF)

        row_loop(go)


    grads = {
        GS: (dz, hid, s.gs, s.gs_y, s.gs_z, out_gs),
        GE: (u_all, slope, s.ge, s.ge_y, s.ge_z, out_ge),
        GO: (dh, att, s.go, s.go_y, s.go_z, out_go),
        G3: (x_all, dqkv, s.g3, s.g3_y, s.g3_z, out_g3),
    }

    def owned(i):
        return pl.ds(al(i * dw, 16), dw)

    def grad_tile(name, k):
        left, right, whole, from_y, _, _ = grads[name]
        first = ((z + k) % n_z) * n_y
        both = pl.ds(al(first * dw, n_y * dw), n_y * dw)
        whole[both, :] = t_mm(left[:, both], right[...]).astype(BF)
        link.send(
            (name, OVER_Y, k),
            whole.at[owned(first + (1 - y))],
            from_y.at[owned(k)],
            {"dp": y_peer},
        )

    def grad_forward(name, k):
        _, _, whole, from_y, from_z, out = grads[name]
        mid = from_y.at[owned(k)]
        link.arrived((name, OVER_Y, k), mid, {"dp": y_peer})
        owner = ((z + k) % n_z) * n_y + y
        total = whole[owned(owner), :].astype(F32) + from_y[owned(k), :].astype(F32)
        if k < n_z - 1:
            link.arrived((name, OVER_Z, k + 1), from_z.at[owned(k)], {"dp": z_from(1)})
            total = total + from_z[owned(k), :].astype(F32)
        if k:
            from_y[owned(k), :] = total.astype(BF)
            link.send((name, OVER_Z, k), mid, from_z.at[owned(k - 1)], {"dp": z_to(1)})
        else:
            out[...] = total

    small_send, small_recv, small_t = s.small_send, s.small_recv, s.small_t

    def small_start():
        small_send[...] = jnp.zeros_like(small_send)
        for e in range(n_dp):
            small_send[e, 2:8, :] = acc[2:8, e * dw : (e + 1) * dw]
        for i in range(owners):
            e = t * owners + i
            small_send[e, 0:2, :] = qacc[0:2, i * dw : (i + 1) * dw]
            for r in range(ebias_rows):
                at = (i * ebias_rows + r) * dw
                small_send[e, 8 + r : 9 + r, :] = hacc[0:1, at : at + dw]
        for o in range(1, n_dp):
            e = dp_to(o)
            link.send((SMALL, o), small_send.at[e], small_recv.at[o], {"dp": e})

    def small_forward():
        total = small_send[d]
        for o in range(1, n_dp):
            link.arrived((SMALL, o), small_recv.at[o], {"dp": dp_from(o)})
            total = total + small_recv[o]
        small_t[t] = total
        for what, peer in ((NEAR, t_core), (FAR, t_far), (NEAR_ON, t_diag)):
            link.send((SMALL_T, what), small_t.at[t], small_t.at[t], {"tensor": peer})

    def small_finish():
        for what, peer in ((NEAR, t_core), (FAR, t_far), (NEAR_ON, t_diag)):
            link.arrived((SMALL_T, what), small_t.at[peer], {"tensor": peer})
        total = small_t[0]
        for i in range(1, n_t):
            total = total + small_t[i]
        out_small[...] = total


    tokens_start(0)
    tokens_start(1)
    tokens_start(2)
    gather_start(W3)
    gather_start(WO)
    gather_start(PACK)
    gather_step(W3, RIGHT, 1)
    gather_step(WO, LEFT, 1)
    tokens_finish(0)
    ag_start(x_all, TX, 0)
    tokens_finish(1)
    ag_start(x_all, TX, 1)
    gather_step(PACK, LEFT, 1)
    gather_step(W3, LEFT, 1)
    gather_step(PACK, RIGHT, 1)
    gather_step(PACK, LEFT, 2)
    gather_step(WO, RIGHT, 1)
    gather_step(PACK, RIGHT, 2)
    gather_step(W3, RIGHT, 2)
    gather_step(WO, LEFT, 2)
    gather_step(PACK, RIGHT, 3)
    gather_step(W3, LEFT, 2)
    gather_step(WO, LEFT, 3)
    gather_step(WO, RIGHT, 2)
    gather_step(W3, RIGHT, 3)
    ag_forward(x_all, TX, 1)
    gather_step(WO, RIGHT, 3)
    gather_start(WE)
    gather_step(PACK, RIGHT, 4)
    ag_forward(x_all, TX, 0)
    tokens_finish(2)
    ag_start(x_all, TX, 2)
    gather_step(PACK, LEFT, 3)
    gather_step(W3, LEFT, 3)
    gather_step(W3, RIGHT, 4)
    gather_step(WO, LEFT, 4)
    ag_finish(x_all, TX, 1)
    gather_ready(PACK)
    ag_finish(x_all, TX, 0)
    gather_ready(W3)
    spread_vectors()
    gather_start(WS)
    project(1)
    gather_ready(WO)
    attention(1)
    ag_forward(x_all, TX, 2)
    project_out(1)
    project(0)
    gather_step(WE, RIGHT, 1)
    gather_step(WE, LEFT, 1)
    ag_finish(x_all, TX, 2)
    rs_forward(R1, 1)
    attention(0)
    project_out(0)
    rs_forward(R1, 0)
    gather_step(WS, LEFT, 1)
    project(2)
    gather_step(WE, RIGHT, 2)
    gather_step(WE, LEFT, 2)
    attention(2)
    gather_step(WS, RIGHT, 1)
    rs_finish(R1, 1)
    norm_first(1)
    ag_start(u_all, TU, 1)
    project_out(2)
    rs_forward(R1, 2)
    gather_step(WS, LEFT, 2)
    gather_step(WE, RIGHT, 3)
    gather_step(WE, LEFT, 3)
    rs_finish(R1, 0)
    norm_first(0)
    ag_start(u_all, TU, 0)
    ag_forward(u_all, TU, 1)
    gather_step(WS, LEFT, 3)
    gather_step(WS, RIGHT, 2)
    ag_finish(u_all, TU, 1)
    gather_step(WE, RIGHT, 4)
    rs_finish(R1, 2)
    norm_first(2)
    ag_start(u_all, TU, 2)
    gather_ready(WE)
    widen(1)
    ag_forward(u_all, TU, 0)
    gather_step(WS, LEFT, 4)
    cot_start()
    gather_step(WS, RIGHT, 3)
    gather_ready(WS)
    shrink_rows(1)
    ag_finish(u_all, TU, 0)
    rs_forward(R2, 1)
    widen(0)
    ag_forward(u_all, TU, 2)
    shrink_rows(0)
    rs_forward(R2, 0)
    ag_finish(u_all, TU, 2)
    widen(2)
    shrink_rows(2)
    rs_forward(R2, 2)
    cot_finish()
    rs_finish(R2, 1)
    norm_second(1)
    ag_start(dz, TZ, 1)
    rs_finish(R2, 2)
    norm_second(2)
    ag_start(dz, TZ, 2)
    ag_forward(dz, TZ, 1)
    rs_finish(R2, 0)
    norm_second(0)
    ag_start(dz, TZ, 0)
    rows_out(MIX, 0, n_seq, mixed_send, out_mixed)
    ag_finish(dz, TZ, 1)
    widen_back(1)
    ag_forward(dz, TZ, 2)
    normed_rows(1)
    rs_forward(R3, 1)
    ag_finish(dz, TZ, 2)
    ag_forward(dz, TZ, 0)
    widen_back(2)
    ag_finish(dz, TZ, 0)
    grad_tile(GS, 3)
    widen_back(0)
    rs_finish(R3, 1)
    norm_first_back(1)
    ag_start(dh, TH, 1)
    grad_tile(GE, 3)
    normed_rows(0)
    grad_tile(GS, 2)
    rs_forward(R3, 0)
    grad_forward(GS, 3)
    normed_rows(2)
    ag_forward(dh, TH, 1)
    grad_tile(GE, 2)
    grad_tile(GS, 1)
    rs_forward(R3, 2)
    ag_finish(dh, TH, 1)
    grad_forward(GE, 3)
    attention_back(1)
    grad_forward(GS, 2)
    rs_finish(R3, 0)
    norm_first_back(0)
    ag_start(dh, TH, 0)
    grad_tile(GE, 1)
    token_rows(1)
    grad_forward(GE, 2)
    grad_tile(GS, 0)
    rs_finish(R3, 2)
    norm_first_back(2)
    ag_start(dh, TH, 2)
    ag_forward(dh, TH, 0)
    grad_tile(GE, 0)
    ag_finish(dh, TH, 0)
    rs_forward(R4, 1)
    grad_forward(GS, 1)
    attention_back(0)
    grad_forward(GE, 1)
    ag_forward(dh, TH, 2)
    token_rows(0)
    ag_finish(dh, TH, 2)
    grad_tile(GO, 3)
    rs_finish(R4, 1)
    finish_rows(1)
    rows_out(BACK, 1, 1, back_send, back_recv)
    rs_forward(R4, 0)
    attention_back(2)
    grad_tile(G3, 3)
    rows_in(MIX, 0, n_seq, out_mixed)
    grad_forward(GS, 0)
    grad_forward(GO, 3)
    small_start()
    grad_tile(GO, 2)
    rs_finish(R4, 0)
    finish_rows(0)
    rows_out(BACK, 0, 1, back_send, back_recv)
    token_rows(2)
    rs_forward(R4, 2)
    grad_forward(GO, 2)
    small_forward()
    grad_forward(G3, 3)
    grad_tile(G3, 2)
    rs_finish(R4, 2)
    finish_rows(2)
    rows_out(BACK, 2, 1, back_send, back_recv)
    grad_forward(G3, 2)
    grad_tile(GO, 1)
    rows_in(BACK, 0, 1, back_recv)
    grad_tile(G3, 1)
    rows_in(BACK, 2, 1, back_recv)
    grad_tile(G3, 0)
    grad_forward(GO, 1)
    small_finish()
    grad_forward(GE, 0)
    grad_forward(G3, 1)
    grad_tile(GO, 0)
    grad_forward(GO, 0)
    grad_forward(G3, 0)
    rows_in(BACK, 1, 1, back_recv)
    link.drain()


def finish_kernel(
    ebias_rows,
    order_s,
    mixed,
    back,
    g3,
    go,
    ge,
    gs,
    small,
    out_mixed,
    out_back,
    out_g3,
    out_go,
    out_ge,
    out_gs,
    out_biases,
    out_gains,
    out_hidden,
):
    def move(k, carry):
        out_back[k] = back[order_s[k]]
        return carry

    lax.fori_loop(0, out_back.shape[0], move, 0)
    out_mixed[...] = mixed[...]
    width = out_g3.shape[2]
    for w in range(3):
        out_g3[w] = g3[:, w * width : (w + 1) * width]
    out_go[...] = jnp.transpose(go[...])
    out_gs[...] = jnp.transpose(gs[...])
    out_ge[...] = ge[...]
    out_biases[...] = small[0:6]
    out_gains[...] = small[6:8]
    out_hidden[...] = small[8 : 8 + ebias_rows]


def body(
    tokens,
    cotangent,
    lengths,
    order,
    triple_weight,
    output_weight,
    expand_weight,
    shrink_weight,
    biases,
    gains,
    expand_bias,
):
    n_dp, n_t = lax.axis_size("dp"), lax.axis_size("tensor")
    slots, _, rows, width = tokens.shape
    n_seq = slots // n_dp
    quarter = rows * n_dp
    full = quarter * n_t
    dw = triple_weight.shape[1]
    hw = triple_weight.shape[2]
    fw = expand_weight.shape[1]
    fits = (
        n_t == 4
        and n_dp % 4 == 0
        and rows % 16 == 0
        and dw % 128 == 0
        and hw % 128 == 0
        and n_seq == 3
        and expand_bias.shape[0] % dw == 0
        and n_dp % n_t == 0
    )
    if not fits:
        return plain_body(
            tokens,
            cotangent,
            lengths,
            order,
            triple_weight,
            output_weight,
            expand_weight,
            shrink_weight,
            biases,
            gains,
            expand_bias,
        )
    n_y = 2
    n_z = n_dp // n_y
    ebias_rows = expand_bias.shape[0] // dw
    all_rows = n_seq * full
    own_rows = n_seq * quarter
    vm = pltpu.VMEM
    scratch = dict(
        stage=vm((slots, rows, width), BF),
        x_all=vm((all_rows, width), BF),
        cots=vm((n_seq, quarter, width), BF),
        w3_all=vm((3, width, hw), BF),
        wo_all=vm((hw, width), BF),
        we_all=vm((width, fw), BF),
        ws_all=vm((fw, width), BF),
        pack_own=vm((16, dw), F32),
        vec=vm((16, width), F32),
        ebias=vm((8, fw), F32),
        qkv=vm((all_rows, 3 * hw), BF),
        att=vm((all_rows, hw), BF),
        lse=vm((n_seq, 8, full), F32),
        part=vm((all_rows, width), BF),
        r_a=vm((own_rows, width), BF),
        r_b=vm((own_rows, width), BF),
        r_x=vm((own_rows, width), BF),
        n1=vm((own_rows, width), F32),
        inv1=vm((own_rows, 128), F32),
        u_all=vm((all_rows, width), BF),
        hid=vm((all_rows, fw), BF),
        slope=vm((all_rows, fw), BF),
        dz=vm((all_rows, width), BF),
        dh=vm((all_rows, width), BF),
        dy=vm((own_rows, width), F32),
        dqkv=vm((all_rows, 3 * hw), BF),
        acc=vm((8, width), F32),
        hacc=vm((8, fw), F32),
        qacc=vm((8, hw), F32),
        kt=vm((hw, full), BF),
        ot=vm((hw, full), F32),
        dk_acc=vm((full, hw), F32),
        dv_acc=vm((full, hw), F32),
        da=vm((full, hw), BF),
        mixed_send=vm((n_seq, quarter, width), BF),
        back_send=vm((n_seq, quarter, width), BF),
        gs=vm((width, fw), BF),
        gs_y=vm((n_z * dw, fw), BF),
        gs_z=vm(((n_z - 1) * dw, fw), BF),
        ge=vm((width, fw), BF),
        ge_y=vm((n_z * dw, fw), BF),
        ge_z=vm(((n_z - 1) * dw, fw), BF),
        go=vm((width, hw), BF),
        go_y=vm((n_z * dw, hw), BF),
        go_z=vm(((n_z - 1) * dw, hw), BF),
        g3=vm((width, 3 * hw), BF),
        g3_y=vm((n_z * dw, 3 * hw), BF),
        g3_z=vm(((n_z - 1) * dw, 3 * hw), BF),
        small_send=vm((n_dp, 16, dw), F32),
        small_recv=vm((n_dp, 16, dw), F32),
        small_t=vm((n_t, 16, dw), F32),
        send_sems=pltpu.SemaphoreType.DMA((N_SEM,)),
        recv_sems=pltpu.SemaphoreType.DMA((N_SEM,)),
        local_sems=pltpu.SemaphoreType.DMA((24,)),
    )
    g = types.SimpleNamespace(
        n_seq=n_seq,
        quarter=quarter,
        width=width,
        n_dp=n_dp,
        n_y=n_y,
        n_t=n_t,
        head_width=hw,
        hidden_width=fw,
        ebias_rows=ebias_rows,
        scratch_names=tuple(scratch),
    )
    smem = pl.BlockSpec(memory_space=pltpu.SMEM)
    vmem = pl.BlockSpec(memory_space=pltpu.VMEM)
    anywhere = pl.BlockSpec(memory_space=pl.ANY)
    sds = jax.ShapeDtypeStruct
    flops = 2 * all_rows * (3 * width * 3 * hw + 3 * width * hw + 6 * width * fw + 7 * full * hw)
    mixed, back, g3, go, ge, gs, small = pl.pallas_call(
        functools.partial(layer_kernel, g),
        out_shape=(
            sds(tokens.shape[:1] + (rows, width), BF),
            sds(tokens.shape[:1] + (rows, width), BF),
            sds((dw, 3 * hw), F32),
            sds((dw, hw), F32),
            sds((dw, fw), F32),
            sds((dw, fw), F32),
            sds((16, dw), F32),
        ),
        in_specs=[smem] * 2 + [vmem] + [anywhere] * 5 + [vmem] * 3,
        out_specs=[anywhere] * 2 + [vmem] * 5,
        scratch_shapes=list(scratch.values()),
        compiler_params=pltpu.CompilerParams(
            collective_id=0,
            has_side_effects=True,
            vmem_limit_bytes=VMEM_BYTES,
        ),
        cost_estimate=pl.CostEstimate(flops=flops, bytes_accessed=1 << 24, transcendentals=0),
    )(
        order,
        lengths,
        tokens.reshape(slots, rows, width),
        cotangent.reshape(slots, rows, width),
        triple_weight,
        output_weight,
        expand_weight,
        shrink_weight,
        biases,
        gains,
        expand_bias.reshape(ebias_rows, dw),
    )
    finals = pl.pallas_call(
        functools.partial(finish_kernel, ebias_rows),
        out_shape=(
            sds(mixed.shape, BF),
            sds(back.shape, BF),
            sds((3, dw, hw), F32),
            sds((hw, dw), F32),
            sds((dw, fw), F32),
            sds((fw, dw), F32),
            sds((6, dw), F32),
            sds((2, dw), F32),
            sds((ebias_rows, dw), F32),
        ),
        in_specs=[smem] + [vmem] * 7,
        out_specs=[vmem] * 9,
        compiler_params=pltpu.CompilerParams(vmem_limit_bytes=VMEM_BYTES),
    )(order, mixed, back, g3, go, ge, gs, small)
    return (
        finals[0].reshape(tokens.shape),
        finals[1].reshape(tokens.shape),
        *finals[2:8],
        finals[8].reshape(expand_bias.shape),
    )


def solution(mesh):
    return jax.shard_map(
        body,
        mesh=mesh,
        in_specs=(
            P(None, "tensor", "dp", None),
            P(None, "tensor", "dp", None),
            P(),
            P(),
            P(None, "dp", "tensor"),
            P(None, "dp"),
            P("dp", "tensor"),
            P("tensor", "dp"),
            P(None, "dp"),
            P(None, "dp"),
            P("dp"),
        ),
        out_specs=(
            P(None, "tensor", "dp", None),
            P(None, "tensor", "dp", None),
            P(None, "dp", "tensor"),
            P("tensor", "dp"),
            P("dp", "tensor"),
            P("tensor", "dp"),
            P(None, "dp"),
            P(None, "dp"),
            P("dp"),
        ),
        check_vma=False,
    )
```

```python
import functools
import math
import types

import jax
import jax.numpy as jnp
from jax import lax
from jax.experimental import pallas as pl
from jax.experimental.pallas import tpu as pltpu
from jax.sharding import PartitionSpec as P

HEAD_DIM = 64


EPSILON = 1e-12
MASKED = -1e30


def normalize(values, gain, shift):
    center = values - jnp.mean(values, axis=-1, keepdims=True)
    spread = jnp.mean(center * center, axis=-1, keepdims=True)
    inv_std = lax.rsqrt(spread + EPSILON)
    scaled = center * inv_std
    return (scaled * gain + shift, scaled, inv_std)


def normalize_back(grad_rows, scaled, inv_std, gain):
    pushed = grad_rows * gain
    first = jnp.mean(pushed, axis=-1, keepdims=True)
    second = jnp.mean(pushed * scaled, axis=-1, keepdims=True)
    return inv_std * (pushed - first - scaled * second)


def gelu_exact(values):
    return 0.5 * values * (1.0 + jax.scipy.special.erf(values / math.sqrt(2.0)))


def gelu_slope(values):
    return 0.5 * (1.0 + jax.scipy.special.erf(values / math.sqrt(2.0))) + values * jnp.exp(
        -0.5 * values * values
    ) / math.sqrt(2.0 * math.pi)


def split_heads(rows):
    return rows.reshape(rows.shape[0], rows.shape[1] // HEAD_DIM, HEAD_DIM)


def score_block(queries, key_rows, seq_length):
    raw_scores = jnp.einsum("qhe,khe->hqk", queries, key_rows, preferred_element_type=jnp.float32)
    scores = raw_scores * (1.0 / math.sqrt(HEAD_DIM))
    visible = jnp.arange(key_rows.shape[0]) < seq_length
    return jnp.where(visible[None, None, :], scores, MASKED)


def attend(seq_item):
    queries, key_rows, value_rows, seq_length = seq_item
    queries = split_heads(queries)
    key_rows = split_heads(key_rows)
    value_rows = split_heads(value_rows)
    masked = score_block(queries, key_rows, seq_length)
    highest = jnp.max(masked, axis=-1, keepdims=True)
    totals = jnp.sum(jnp.exp(masked - highest), axis=-1, keepdims=True)
    log_totals = highest + jnp.log(totals)
    probs = jnp.exp(masked - log_totals).astype(jnp.bfloat16)
    blended = jnp.einsum("hqk,khe->qhe", probs, value_rows, preferred_element_type=jnp.float32)
    return (blended.astype(jnp.bfloat16).reshape(queries.shape[0], -1), log_totals[..., 0])


def attend_back(seq_item):
    queries, key_rows, value_rows, grad_rows, log_totals, seq_length = seq_item
    queries = split_heads(queries)
    key_rows = split_heads(key_rows)
    value_rows = split_heads(value_rows)
    grad_heads = split_heads(grad_rows)
    masked = score_block(queries, key_rows, seq_length)
    probs = jnp.exp(masked - log_totals[..., None])
    grad_probs = jnp.einsum(
        "qhe,khe->hqk", grad_heads, value_rows, preferred_element_type=jnp.float32
    )
    inner = jnp.sum(probs * grad_probs, axis=-1, keepdims=True)
    grad_scores = (probs * (grad_probs - inner)).astype(jnp.bfloat16)
    score_scale = 1.0 / math.sqrt(HEAD_DIM)
    grad_query = (
        jnp.einsum("hqk,khe->qhe", grad_scores, key_rows, preferred_element_type=jnp.float32)
        * score_scale
    )
    grad_key = (
        jnp.einsum("hqk,qhe->khe", grad_scores, queries, preferred_element_type=jnp.float32)
        * score_scale
    )
    grad_value = jnp.einsum(
        "hqk,qhe->khe", probs.astype(jnp.bfloat16), grad_heads, preferred_element_type=jnp.float32
    )
    row_count = queries.shape[0]
    return (
        grad_query.astype(jnp.bfloat16).reshape(row_count, -1),
        grad_key.astype(jnp.bfloat16).reshape(row_count, -1),
        grad_value.astype(jnp.bfloat16).reshape(row_count, -1),
    )


def plain_body(
    tokens,
    cotangent,
    lengths,
    order,
    triple_weight,
    output_weight,
    expand_weight,
    shrink_weight,
    biases,
    gains,
    expand_bias,
):
    seq_count = order.shape[0]
    per_group = seq_count // lax.axis_size("dp")
    tensor_size = lax.axis_size("tensor")
    member = lax.axis_index("dp")
    my_rank = lax.axis_index("tensor")
    slot_ids = jnp.arange(seq_count, dtype=jnp.int32)
    inverse = jnp.zeros((seq_count,), jnp.int32).at[order].set(slot_ids)
    local_x, local_dy = (
        lax.all_to_all(tokens[inverse], "dp", split_axis=0, concat_axis=2, tiled=True),
        lax.all_to_all(cotangent, "dp", split_axis=0, concat_axis=2, tiled=True),
    )
    quarter = local_x.shape[2]
    model_width = local_x.shape[3]
    full_length = quarter * tensor_size
    my_lengths = lax.dynamic_slice_in_dim(lengths, member * per_group, per_group)
    gathered = (
        lax.all_gather(triple_weight, "dp", axis=1, tiled=True),
        lax.all_gather(output_weight, "dp", axis=1, tiled=True),
        lax.all_gather(expand_weight, "dp", axis=0, tiled=True),
        lax.all_gather(shrink_weight, "dp", axis=1, tiled=True),
        lax.all_gather(biases, "dp", axis=1, tiled=True),
        lax.all_gather(gains, "dp", axis=1, tiled=True),
        lax.all_gather(expand_bias, "dp", axis=0, tiled=True),
    )
    query_key_value_proj, out_weight, widen_projection, shrink, bias_rows, gain_rows, exp_bias = (
        gathered
    )
    head_width = query_key_value_proj.shape[2]
    hidden_width = widen_projection.shape[1]
    out_heads = lax.dynamic_slice_in_dim(out_weight, my_rank * head_width, head_width, 0)
    bias_query = lax.dynamic_slice_in_dim(bias_rows[0], my_rank * head_width, head_width).astype(
        jnp.float32
    )
    bias_value = lax.dynamic_slice_in_dim(bias_rows[1], my_rank * head_width, head_width).astype(
        jnp.float32
    )
    bias_hidden = lax.dynamic_slice_in_dim(exp_bias, my_rank * hidden_width, hidden_width).astype(
        jnp.float32
    )
    bias_stack = jnp.stack([bias_query, jnp.zeros_like(bias_query), bias_value])
    gain_first = gain_rows[0].astype(jnp.float32)
    gain_second = gain_rows[1].astype(jnp.float32)
    full_shape = (per_group, tensor_size, quarter, model_width)
    token_all_rows = lax.all_gather(local_x, "tensor", axis=1, tiled=True).reshape(
        per_group, full_length, model_width
    )
    projected = (
        jnp.einsum(
            "jah,rhu->rjau",
            token_all_rows,
            query_key_value_proj,
            preferred_element_type=jnp.float32,
        )
        + bias_stack[:, None, None, :]
    ).astype(jnp.bfloat16)
    attended, log_totals = lax.map(attend, (projected[0], projected[1], projected[2], my_lengths))
    attn_terms = jnp.einsum(
        "sle,em->slm", attended, out_heads, preferred_element_type=jnp.float32
    ).reshape(full_shape)
    attn_sum = lax.psum_scatter(attn_terms, "tensor", scatter_dimension=1, tiled=True)
    hidden_in = local_x.astype(jnp.float32) + (attn_sum + bias_rows[2].astype(jnp.float32))
    normed, normed_scaled, normed_inv = normalize(
        hidden_in, gain_first, bias_rows[3].astype(jnp.float32)
    )
    normalized_all_rows = lax.all_gather(
        normed.astype(jnp.bfloat16), "tensor", axis=1, tiled=True
    ).reshape(per_group, full_length, model_width)
    pre_act = (
        jnp.einsum(
            "uqj,jt->uqt", normalized_all_rows, widen_projection, preferred_element_type=jnp.float32
        )
        + bias_hidden
    )
    hidden = gelu_exact(pre_act).astype(jnp.bfloat16)
    ffn_terms = jnp.einsum(
        "slf,fm->slm", hidden, shrink, preferred_element_type=jnp.float32
    ).reshape(full_shape)
    ffn_sum = lax.psum_scatter(
        ffn_terms.astype(jnp.bfloat16), "tensor", scatter_dimension=1, tiled=True
    ).astype(jnp.float32)
    total_rows = normed + (ffn_sum + bias_rows[4].astype(jnp.float32))
    output, out_scaled, out_inv = normalize(
        total_rows, gain_second, bias_rows[5].astype(jnp.float32)
    )
    positions = my_rank * quarter + jnp.arange(quarter)
    valid = (positions[None, :] < my_lengths[:, None]).astype(jnp.float32)
    grad_out = local_dy.astype(jnp.float32) * valid[:, None, :, None]
    row_axes = (0, 1, 2)
    gain_grad_second = jnp.sum(grad_out * out_scaled, axis=row_axes)
    shift_grad_second = jnp.sum(grad_out, axis=row_axes)
    grad_total = normalize_back(grad_out, out_scaled, out_inv, gain_second)
    branch_bias_grad = jnp.sum(grad_total, axis=row_axes)
    grad_branch = lax.all_gather(
        grad_total.astype(jnp.bfloat16), "tensor", axis=1, tiled=True
    ).reshape(per_group, full_length, model_width)
    shrink_grad = jnp.einsum("slf,slm->fm", hidden, grad_branch, preferred_element_type=jnp.float32)
    grad_hidden = jnp.einsum("slm,fm->slf", grad_branch, shrink, preferred_element_type=jnp.float32)
    preactivation_grad = (grad_hidden * gelu_slope(pre_act)).astype(jnp.bfloat16)
    hidden_bias_grad = jnp.sum(preactivation_grad, axis=(0, 1), dtype=jnp.float32)
    expand_grad = jnp.einsum(
        "mgc,mga->ca", normalized_all_rows, preactivation_grad, preferred_element_type=jnp.float32
    )
    normed_terms = jnp.einsum(
        "cpk,rk->cpr", preactivation_grad, widen_projection, preferred_element_type=jnp.float32
    ).reshape(full_shape)
    grad_normed = grad_total + lax.psum_scatter(
        normed_terms.astype(jnp.bfloat16), "tensor", scatter_dimension=1, tiled=True
    ).astype(jnp.float32)
    first_norm_gain_grad = jnp.sum(grad_normed * normed_scaled, axis=row_axes)
    shift_grad_first = jnp.sum(grad_normed, axis=row_axes)
    grad_hidden_in = normalize_back(grad_normed, normed_scaled, normed_inv, gain_first)
    out_bias_grad = jnp.sum(grad_hidden_in, axis=row_axes)
    grad_attn = lax.all_gather(
        grad_hidden_in.astype(jnp.bfloat16), "tensor", axis=1, tiled=True
    ).reshape(per_group, full_length, model_width)
    output_grad = jnp.einsum("sle,slm->em", attended, grad_attn, preferred_element_type=jnp.float32)
    grad_blended = jnp.einsum(
        "slm,em->sle", grad_attn, out_heads, preferred_element_type=jnp.float32
    ).astype(jnp.bfloat16)
    grad_query, grad_key, grad_value = lax.map(
        attend_back,
        (projected[0], projected[1], projected[2], grad_blended, log_totals, my_lengths),
    )
    projection_output_grad = jnp.stack([grad_query, grad_key, grad_value])
    query_bias_grad = jnp.sum(grad_query, axis=(0, 1), dtype=jnp.float32)
    value_bias_grad = jnp.sum(grad_value, axis=(0, 1), dtype=jnp.float32)
    triple_grad = jnp.einsum(
        "xyt,vxyu->vtu", token_all_rows, projection_output_grad, preferred_element_type=jnp.float32
    )
    token_terms = jnp.einsum(
        "atpi,aki->tpk",
        projection_output_grad,
        query_key_value_proj,
        preferred_element_type=jnp.float32,
    ).reshape(full_shape)
    grad_tokens = grad_hidden_in + lax.psum_scatter(
        token_terms.astype(jnp.bfloat16), "tensor", scatter_dimension=1, tiled=True
    ).astype(jnp.float32)
    zero_row = jnp.zeros((model_width,), jnp.float32)
    query_full = lax.dynamic_update_slice_in_dim(zero_row, query_bias_grad, my_rank * head_width, 0)
    value_full = lax.dynamic_update_slice_in_dim(zero_row, value_bias_grad, my_rank * head_width, 0)
    bias_grad = jnp.stack(
        [
            query_full,
            value_full,
            out_bias_grad,
            shift_grad_first,
            branch_bias_grad,
            shift_grad_second,
        ]
    )
    gain_grad = jnp.stack([first_norm_gain_grad, gain_grad_second])
    hidden_full = lax.dynamic_update_slice_in_dim(
        jnp.zeros((exp_bias.shape[0],), jnp.float32), hidden_bias_grad, my_rank * hidden_width, 0
    )
    bias_grad, gain_grad, hidden_full = (
        lax.psum(bias_grad.astype(jnp.bfloat16), "tensor").astype(jnp.float32),
        lax.psum(gain_grad.astype(jnp.bfloat16), "tensor").astype(jnp.float32),
        lax.psum(hidden_full.astype(jnp.bfloat16), "tensor").astype(jnp.float32),
    )
    shards = (
        lax.psum_scatter(triple_grad, "dp", scatter_dimension=1, tiled=True),
        lax.psum_scatter(output_grad, "dp", scatter_dimension=1, tiled=True),
        lax.psum_scatter(expand_grad, "dp", scatter_dimension=0, tiled=True),
        lax.psum_scatter(shrink_grad, "dp", scatter_dimension=1, tiled=True),
        lax.psum_scatter(bias_grad, "dp", scatter_dimension=1, tiled=True),
        lax.psum_scatter(gain_grad, "dp", scatter_dimension=1, tiled=True),
        lax.psum_scatter(hidden_full, "dp", scatter_dimension=0, tiled=True),
    )
    mixed_rows, back_rows = (
        lax.all_to_all(output.astype(jnp.bfloat16), "dp", split_axis=2, concat_axis=0, tiled=True),
        lax.all_to_all(
            grad_tokens.astype(jnp.bfloat16), "dp", split_axis=2, concat_axis=0, tiled=True
        ),
    )
    return (
        mixed_rows,
        back_rows[order],
        shards[0],
        shards[1],
        shards[2],
        shards[3],
        shards[4],
        shards[5],
        shards[6],
    )


BF = jnp.bfloat16
F32 = jnp.float32
MESH = pl.DeviceIdType.MESH
LOG2E = math.log2(math.e)
N_SEM = 147
PACK, W3, WO, WE, WS = range(5)
GS, GE, G3, GO = range(10, 14)
TX, TU, TZ, TH, R1, R2, R3, R4 = range(20, 28)
TOK, COT, MIX, BACK, SMALL, SMALL_T = range(30, 36)
RIGHT, LEFT, OVER_Y, OVER_Z, FAR, NEAR, NEAR_ON = range(40, 47)
VMEM_BYTES = 64 * 1024 * 1024


def mm(a, b):
    return lax.dot_general(a, b, (((1,), (0,)), ((), ())), preferred_element_type=F32)


def mm_t(a, b):
    return lax.dot_general(a, b, (((1,), (1,)), ((), ())), preferred_element_type=F32)


def t_mm(a, b):
    return lax.dot_general(a, b, (((0,), (0,)), ((), ())), preferred_element_type=F32)


class Links:
    def __init__(self, send_sems, recv_sems, local_sems):
        self.send_sems = send_sems
        self.recv_sems = recv_sems
        self.local_sems = local_sems
        self.slots = {}
        self.flying = {}
        self.local_count = 0

    def slot(self, name):
        if TX <= name[0] <= TH:
            name = (TX,) + name[1:]
        if R1 <= name[0] <= R4:
            name = (R1,) + name[1:]
        return self.slots.setdefault(name, len(self.slots))

    def send(self, name, src, dst, where):
        i = self.slot(name)
        if i in self.flying:
            self.sent(name)
        copy = pltpu.make_async_remote_copy(
            src_ref=src,
            dst_ref=dst,
            send_sem=self.send_sems.at[i],
            recv_sem=self.recv_sems.at[i],
            device_id=where,
            device_id_type=MESH,
        )
        copy.start()
        self.flying[i] = copy

    def sent(self, name):
        self.flying.pop(self.slot(name)).wait_send()

    def arrived(self, name, dst, where):
        i = self.slot(name)
        pltpu.make_async_remote_copy(
            src_ref=dst,
            dst_ref=dst,
            send_sem=self.send_sems.at[i],
            recv_sem=self.recv_sems.at[i],
            device_id=where,
            device_id_type=MESH,
        ).wait_recv()

    def drain(self):
        for copy in self.flying.values():
            copy.wait_send()

    def local(self, src, dst):
        copy = pltpu.make_async_copy(src, dst, self.local_sems.at[self.local_count])
        self.local_count += 1
        copy.start()
        return copy


def layer_kernel(g, *refs):
    (order_s, lengths_s, tok, cot, w3, wo, we, ws, bias_in, gain_in, hidden_in) = refs[:11]
    (out_mixed, back_recv, out_g3, out_go, out_ge, out_gs, out_small) = refs[11:18]
    s = types.SimpleNamespace(**dict(zip(g.scratch_names, refs[18:])))
    n_seq, quarter, width = g.n_seq, g.quarter, g.width
    n_dp, n_y, n_t = g.n_dp, g.n_y, g.n_t
    n_z = n_dp // n_y
    full = n_t * quarter
    half = full // 2
    rows = quarter // n_dp
    hw, fw = g.head_width, g.hidden_width
    heads = hw // HEAD_DIM
    dw = width // n_dp
    tile = 256
    ebias_rows = g.ebias_rows
    owners = n_dp // n_t

    d = lax.axis_index("dp")
    t = lax.axis_index("tensor")
    z, y = d // n_y, d % n_y
    x, c = t // 2, t % 2
    t_core = x * 2 + (1 - c)
    t_far = (1 - x) * 2 + c
    t_diag = (1 - x) * 2 + (1 - c)

    def dp_to(o):
        return (d + o) % n_dp

    def dp_from(o):
        return (d + n_dp - o) % n_dp

    def z_to(k):
        return ((z + k) % n_z) * n_y + y

    def z_from(k):
        return ((z + n_z - k) % n_z) * n_y + y

    y_peer = z * n_y + (1 - y)
    ring = (1 - y) * z + y * (n_dp - 1 - z)

    def ring_at(k):
        r = (ring + n_dp + k) % n_dp
        back = r // n_z
        return ((1 - back) * r + back * (n_dp - 1 - r)) * n_y + back

    link = Links(s.send_sems, s.recv_sems, s.local_sems)

    barrier = pltpu.get_barrier_semaphore()
    for o in range(1, n_dp):
        pl.semaphore_signal(barrier, inc=1, device_id={"dp": dp_to(o)}, device_id_type=MESH)
    for peer in (t_core, t_far, t_diag):
        pl.semaphore_signal(barrier, inc=1, device_id={"tensor": peer}, device_id_type=MESH)

    stage, x_all, cots = s.stage, s.x_all, s.cots
    w3_all, wo_all, we_all, ws_all = s.w3_all, s.wo_all, s.we_all, s.ws_all
    pack_own, vec, ebias = s.pack_own, s.vec, s.ebias
    qkv, att, lse, part = s.qkv, s.att, s.lse, s.part
    r_a, r_b, r_x = s.r_a, s.r_b, s.r_x
    n1, inv1, u_all, hid, slope = s.n1, s.inv1, s.u_all, s.hid, s.slope
    dz, dh, dy, dqkv = s.dz, s.dh, s.dy, s.dqkv
    acc, hacc, qacc = s.acc, s.hacc, s.qacc
    kt, ot, dk_acc, dv_acc, da = s.kt, s.ot, s.dk_acc, s.dv_acc, s.da
    mixed_send, back_send = s.mixed_send, s.back_send

    def al(v, m):
        return pl.multiple_of(v, m)

    def seq_rows(j, start, n):
        return pl.ds(al(j * full + start, 16), n)

    def mine(j):
        return seq_rows(j, t * quarter, quarter)


    def permute(k, carry):
        arrival = jnp.int32(0)
        for i in range(n_dp * n_seq):
            arrival = jnp.where(order_s[i] == k, i, arrival)
        stage[k] = tok[arrival]
        return carry

    lax.fori_loop(0, n_dp * n_seq, permute, 0)
    pack_own[0:6, :] = bias_in[...].astype(F32)
    pack_own[6:8, :] = gain_in[...].astype(F32)
    pack_own[8 : 8 + ebias_rows, :] = hidden_in[...].astype(F32)
    pack_own[8 + ebias_rows :, :] = jnp.zeros((16 - 8 - ebias_rows, dw), F32)
    acc[...] = jnp.zeros_like(acc)
    hacc[...] = jnp.zeros_like(hacc)
    qacc[...] = jnp.zeros_like(qacc)
    pl.semaphore_wait(barrier, n_dp - 1 + 3)

    def x_block(j, src):
        return x_all.at[seq_rows(j, t * quarter + src * rows, rows)]

    def tokens_start(j):
        for o in range(1, n_dp):
            e = dp_to(o)
            link.send((TOK, j, o), stage.at[e * n_seq + j], x_block(j, d), {"dp": e})
        x_all[seq_rows(j, t * quarter + d * rows, rows), :] = stage[d * n_seq + j]

    def tokens_finish(j):
        for o in range(1, n_dp):
            link.arrived((TOK, j, o), x_block(j, dp_from(o)), {"dp": dp_from(o)})

    def cot_block(src):
        return cots.at[:, pl.ds(al(src * rows, 16), rows), :]

    own_copies = {}

    def cot_start():
        for o in range(1, n_dp):
            e = dp_to(o)
            link.send((COT, o), cot.at[pl.ds(e * n_seq, n_seq)], cot_block(d), {"dp": e})
        own_copies[COT] = link.local(cot.at[pl.ds(d * n_seq, n_seq)], cot_block(d))

    def cot_finish():
        own_copies.pop(COT).wait()
        for o in range(1, n_dp):
            link.arrived((COT, o), cot_block(dp_from(o)), {"dp": dp_from(o)})

    def cols(ref, e):
        return ref.at[:, pl.ds(al(e * dw, 128), dw)]

    def row_block(ref, e):
        return ref.at[pl.ds(al(e * dw, 16), dw), :]

    def w3_block(e):
        return w3_all.at[:, pl.ds(al(e * dw, 16), dw), :]

    gathers = {
        PACK: (pack_own, lambda e: cols(vec, e), n_dp // 2),
        W3: (w3, w3_block, n_dp // 2),
        WO: (
            wo.at[pl.ds(al(t * hw, 16), hw), :],
            lambda e: cols(wo_all, e),
            n_dp // 2 - 1,
        ),
        WE: (we, lambda e: row_block(we_all, e), n_dp // 2),
        WS: (ws, lambda e: cols(ws_all, e), n_dp // 2 - 1),
    }

    def gather_start(name):
        src, block, _ = gathers[name]
        link.send((name, RIGHT, 1), src, block(d), {"dp": ring_at(1)})
        link.send((name, LEFT, 1), src, block(d), {"dp": ring_at(-1)})
        own_copies[name] = link.local(src, block(d))

    def gather_step(name, way, k):
        _, block, right = gathers[name]
        steps, sign = (right, -1) if way == RIGHT else (n_dp - 1 - right, 1)
        got = block(ring_at(sign * k))
        link.arrived((name, way, k), got, {"dp": ring_at(sign)})
        if k < steps:
            link.send((name, way, k + 1), got, got, {"dp": ring_at(-sign)})

    def gather_ready(name):
        own_copies.pop(name).wait()


    def t_rows(j, who):
        return seq_rows(j, who * quarter, quarter)

    def ag_start(buf, tag, j):
        own = buf.at[t_rows(j, t)]
        link.send((tag, FAR, j), own, own, {"tensor": t_far})
        link.send((tag, NEAR, j), own, own, {"tensor": t_core})

    def ag_forward(buf, tag, j):
        got = buf.at[t_rows(j, t_far)]
        link.arrived((tag, FAR, j), got, {"tensor": t_far})
        link.send((tag, NEAR_ON, j), got, got, {"tensor": t_core})

    def ag_finish(buf, tag, j):
        link.arrived((tag, NEAR, j), buf.at[t_rows(j, t_core)], {"tensor": t_core})
        link.arrived((tag, NEAR_ON, j), buf.at[t_rows(j, t_diag)], {"tensor": t_core})

    def q_rows(j):
        return pl.ds(j * quarter, quarter)

    def rs_start_far(tag, j):
        link.send((tag, NEAR_ON, j), part.at[t_rows(j, t_diag)], r_b.at[q_rows(j)], {"tensor": t_core})

    def rs_start_near(tag, j):
        link.send((tag, NEAR, j), part.at[t_rows(j, t_core)], r_a.at[q_rows(j)], {"tensor": t_core})

    def rs_forward(tag, j):
        link.arrived((tag, NEAR_ON, j), r_b.at[q_rows(j)], {"tensor": t_core})
        far = t_rows(j, t_far)
        both = part[far, :].astype(F32) + r_b[q_rows(j), :].astype(F32)
        part[far, :] = both.astype(BF)
        link.send((tag, FAR, j), part.at[far], r_x.at[q_rows(j)], {"tensor": t_far})

    def rs_finish(tag, j):
        link.arrived((tag, NEAR, j), r_a.at[q_rows(j)], {"tensor": t_core})
        link.arrived((tag, FAR, j), r_x.at[q_rows(j)], {"tensor": t_far})

    chunk = 32

    def row_loop(fn):
        lax.fori_loop(0, quarter // chunk, lambda i, carry: fn(i * chunk) or carry, 0)

    def summed(j, r):
        loc = seq_rows(j, t * quarter + r, chunk)
        buf = pl.ds(al(j * quarter + r, 16), chunk)
        return (
            part[loc, :].astype(F32)
            + r_a[buf, :].astype(F32)
            + r_x[buf, :].astype(F32)
        )

    def add_sum(row, value):
        acc[row : row + 1, :] += jnp.sum(value, axis=0, keepdims=True)

    def two_halves(tag, j, fn):
        if tag > R1:
            for what in (NEAR_ON, NEAR, FAR):
                link.sent((tag - 1, what, j))
        fn(al(j * full + (1 - x) * half, 16))
        rs_start_far(tag, j)
        fn(al(j * full + x * half, 16))
        rs_start_near(tag, j)

    def by_tiles(n, fn):
        lax.fori_loop(0, n // tile, lambda i, carry: fn(al(i * tile, tile)) or carry, 0)


    def spread_vectors():
        for i in range(owners):
            e = t * owners + i
            for r in range(ebias_rows):
                ebias[0:1, (i * ebias_rows + r) * dw : (i * ebias_rows + r + 1) * dw] = vec[
                    8 + r : 9 + r, pl.ds(al(e * dw, 128), dw)
                ]


    def project(j):
        at = pl.ds(j * full, full)
        for w in range(3):
            span = slice(w * hw, (w + 1) * hw)
            value = mm(x_all[at, :], w3_all[w])
            if w == 0:
                value = value + vec[0:1, pl.ds(al(t * hw, 128), hw)]
            if w == 2:
                value = value + vec[1:2, pl.ds(al(t * hw, 128), hw)]
            qkv[at, span] = value.astype(BF)

    lane_head = lax.broadcasted_iota(jnp.int32, (full, hw), 1) // HEAD_DIM
    scale2 = LOG2E / math.sqrt(HEAD_DIM)

    def head_scores(j, h, at):
        q_head = jnp.where(lane_head == h, qkv[at, 0:hw], jnp.zeros((), BF))
        raw = mm_t(qkv[at, hw : 2 * hw], q_head)
        key_row = lax.broadcasted_iota(jnp.int32, (full, 1), 0)
        visible = key_row < lengths_s[d * n_seq + j]
        return q_head, jnp.where(visible, raw * scale2, MASKED)

    def attention(j):
        at = pl.ds(j * full, full)
        kt[...] = jnp.transpose(qkv[at, 2 * hw : 3 * hw])

        def head(h, carry):
            span = pl.ds(al(h * HEAD_DIM, HEAD_DIM), HEAD_DIM)
            _, scores = head_scores(j, h, at)
            top = jnp.max(scores, axis=0, keepdims=True)
            e = jnp.exp2(scores - top)
            total = jnp.sum(e, axis=0, keepdims=True)
            o = mm(kt[span, :], e.astype(BF))
            ot[span, :] = o * (1.0 / total)
            lse[j, pl.ds(h, 1), :] = top + jnp.log2(total)
            return carry

        lax.fori_loop(0, heads, head, 0)
        att[at, :] = jnp.transpose(ot[...]).astype(BF)

    def project_out(j):
        def part_rows(start):
            def go(n):
                part[pl.ds(start, half), pl.ds(n, tile)] = mm(
                    att[pl.ds(start, half), :], wo_all[:, pl.ds(n, tile)]
                ).astype(BF)

            by_tiles(width, go)

        two_halves(R1, j, part_rows)

    def norm_first(j):
        def go(r):
            loc = seq_rows(j, t * quarter + r, chunk)
            buf = pl.ds(al(j * quarter + r, 16), chunk)
            h = x_all[loc, :].astype(F32) + (summed(j, r) + vec[2:3, :])
            center = h - jnp.mean(h, axis=-1, keepdims=True)
            inv = lax.rsqrt(jnp.mean(center * center, axis=-1, keepdims=True) + EPSILON)
            scaled = center * inv
            n1[buf, :] = scaled
            inv1[buf, :] = jnp.broadcast_to(inv, (chunk, 128))
            u_all[loc, :] = (scaled * vec[6:7, :] + vec[3:4, :]).astype(BF)

        row_loop(go)

    def widen(j):
        at = pl.ds(j * full, full)

        def go(n):
            f = mm(u_all[at, :], we_all[:, pl.ds(n, tile)]) + ebias[0:1, pl.ds(n, tile)]
            cdf = 0.5 + 0.5 * lax.erf(f * (1.0 / math.sqrt(2.0)))
            hid[at, pl.ds(n, tile)] = (f * cdf).astype(BF)
            bell = jnp.exp2((f * f) * (-0.5 * LOG2E)) * (1.0 / math.sqrt(2.0 * math.pi))
            slope[at, pl.ds(n, tile)] = (cdf + f * bell).astype(BF)

        by_tiles(fw, go)

    def shrink_rows(j):
        def part_rows(start):
            def go(n):
                part[pl.ds(start, half), pl.ds(n, tile)] = mm(
                    hid[pl.ds(start, half), :], ws_all[:, pl.ds(n, tile)]
                ).astype(BF)

            by_tiles(width, go)

        two_halves(R2, j, part_rows)

    def norm_second(j):
        length = lengths_s[d * n_seq + j]

        def go(r):
            loc = seq_rows(j, t * quarter + r, chunk)
            buf = pl.ds(al(j * quarter + r, 16), chunk)
            u = n1[buf, :] * vec[6:7, :] + vec[3:4, :]
            total = u + (summed(j, r) + vec[4:5, :])
            center = total - jnp.mean(total, axis=-1, keepdims=True)
            inv = lax.rsqrt(jnp.mean(center * center, axis=-1, keepdims=True) + EPSILON)
            scaled = center * inv
            mixed_send[j, pl.ds(al(r, 16), chunk), :] = (scaled * vec[7:8, :] + vec[5:6, :]).astype(BF)
            place = t * quarter + r + lax.broadcasted_iota(jnp.int32, (chunk, 1), 0)
            valid = (place < length).astype(F32)
            e = cots[j, pl.ds(al(r, 16), chunk), :].astype(F32) * valid
            add_sum(5, e)
            add_sum(7, e * scaled)
            pushed = e * vec[7:8, :]
            first = jnp.mean(pushed, axis=-1, keepdims=True)
            second = jnp.mean(pushed * scaled, axis=-1, keepdims=True)
            grad = inv * (pushed - first - scaled * second)
            add_sum(4, grad)
            dy[buf, :] = grad
            dz[loc, :] = grad.astype(BF)

        row_loop(go)

    def rows_out(tag, j, count, src, dst):
        for o in range(1, n_dp):
            e = dp_to(o)
            link.send(
                (tag, j, o),
                src.at[pl.ds(j, count), pl.ds(al(e * rows, 16), rows)],
                dst.at[pl.ds(d * n_seq + j, count)],
                {"dp": e},
            )
        own_copies[tag, j] = link.local(
            src.at[pl.ds(j, count), pl.ds(al(d * rows, 16), rows)],
            dst.at[pl.ds(d * n_seq + j, count)],
        )

    def rows_in(tag, j, count, dst):
        own_copies.pop((tag, j)).wait()
        for o in range(1, n_dp):
            e = dp_from(o)
            link.arrived((tag, j, o), dst.at[pl.ds(e * n_seq + j, count)], {"dp": e})


    def widen_back(j):
        at = pl.ds(j * full, full)

        def go(n):
            spread = mm_t(dz[at, :], ws_all[pl.ds(n, tile), :])
            grad = (spread * slope[at, pl.ds(n, tile)].astype(F32)).astype(BF)
            slope[at, pl.ds(n, tile)] = grad
            hacc[0:1, pl.ds(n, tile)] += jnp.sum(grad.astype(F32), axis=0, keepdims=True)

        by_tiles(fw, go)

    def normed_rows(j):
        def part_rows(start):
            def go(n):
                part[pl.ds(start, half), pl.ds(n, tile)] = mm_t(
                    slope[pl.ds(start, half), :], we_all[pl.ds(n, tile), :]
                ).astype(BF)

            by_tiles(width, go)

        two_halves(R3, j, part_rows)

    def norm_first_back(j):
        def go(r):
            loc = seq_rows(j, t * quarter + r, chunk)
            buf = pl.ds(al(j * quarter + r, 16), chunk)
            du = dy[buf, :] + summed(j, r)
            scaled = n1[buf, :]
            add_sum(3, du)
            add_sum(6, du * scaled)
            pushed = du * vec[6:7, :]
            first = jnp.mean(pushed, axis=-1, keepdims=True)
            second = jnp.mean(pushed * scaled, axis=-1, keepdims=True)
            grad = inv1[buf, 0:1] * (pushed - first - scaled * second)
            add_sum(2, grad)
            dy[buf, :] = grad
            dh[loc, :] = grad.astype(BF)

        row_loop(go)

    def attention_back(j, between=None):
        at = pl.ds(j * full, full)
        da[...] = mm_t(dh[at, :], wo_all[...]).astype(BF)
        kt[...] = jnp.transpose(qkv[at, hw : 2 * hw])
        dk_acc[...] = jnp.zeros_like(dk_acc)
        dv_acc[...] = jnp.zeros_like(dv_acc)

        def head(h, carry):
            span = pl.ds(al(h * HEAD_DIM, HEAD_DIM), HEAD_DIM)
            q_head, scores = head_scores(j, h, at)
            da_head = jnp.where(lane_head == h, da[...], jnp.zeros((), BF))
            p = jnp.exp2(scores - lse[j, pl.ds(h, 1), :])
            dp = mm_t(qkv[at, 2 * hw : 3 * hw], da_head)
            inner = jnp.sum(p * dp, axis=0, keepdims=True)
            ds = (p * (dp - inner)).astype(BF)
            dv_acc[...] += mm(p.astype(BF), da_head)
            dk_acc[...] += mm(ds, q_head)
            ot[span, :] = mm(kt[span, :], ds)
            return carry

        lax.fori_loop(0, heads, head, 0)
        scale = 1.0 / math.sqrt(HEAD_DIM)
        grad_q = (jnp.transpose(ot[...]) * scale).astype(BF)
        grad_k = (dk_acc[...] * scale).astype(BF)
        grad_v = dv_acc[...].astype(BF)
        dqkv[at, 0:hw] = grad_q
        dqkv[at, hw : 2 * hw] = grad_k
        dqkv[at, 2 * hw : 3 * hw] = grad_v
        qacc[0:1, :] += jnp.sum(grad_q.astype(F32), axis=0, keepdims=True)
        qacc[1:2, :] += jnp.sum(grad_v.astype(F32), axis=0, keepdims=True)

    def token_rows(j):
        def part_rows(start):
            def go(n):
                total = None
                for w in range(3):
                    term = mm_t(
                        dqkv[pl.ds(start, half), w * hw : (w + 1) * hw],
                        w3_all[w, pl.ds(n, tile), :],
                    )
                    total = term if total is None else total + term
                part[pl.ds(start, half), pl.ds(n, tile)] = total.astype(BF)

            by_tiles(width, go)

        two_halves(R4, j, part_rows)

    def finish_rows(j):
        def go(r):
            buf = pl.ds(al(j * quarter + r, 16), chunk)
            back_send[j, pl.ds(al(r, 16), chunk), :] = (dy[buf, :] + summed(j, r)).astype(BF)

        row_loop(go)


    grads = {
        GS: (dz, hid, s.gs, s.gs_y, s.gs_z, out_gs),
        GE: (u_all, slope, s.ge, s.ge_y, s.ge_z, out_ge),
        GO: (dh, att, s.go, s.go_y, s.go_z, out_go),
        G3: (x_all, dqkv, s.g3, s.g3_y, s.g3_z, out_g3),
    }

    def owned(i):
        return pl.ds(al(i * dw, 16), dw)

    def grad_tile(name, k):
        left, right, whole, from_y, _, _ = grads[name]
        first = ((z + k) % n_z) * n_y
        both = pl.ds(al(first * dw, n_y * dw), n_y * dw)
        whole[both, :] = t_mm(left[:, both], right[...]).astype(BF)
        link.send(
            (name, OVER_Y, k),
            whole.at[owned(first + (1 - y))],
            from_y.at[owned(k)],
            {"dp": y_peer},
        )

    def grad_forward(name, k):
        _, _, whole, from_y, from_z, out = grads[name]
        mid = from_y.at[owned(k)]
        link.arrived((name, OVER_Y, k), mid, {"dp": y_peer})
        owner = ((z + k) % n_z) * n_y + y
        total = whole[owned(owner), :].astype(F32) + from_y[owned(k), :].astype(F32)
        if k < n_z - 1:
            link.arrived((name, OVER_Z, k + 1), from_z.at[owned(k)], {"dp": z_from(1)})
            total = total + from_z[owned(k), :].astype(F32)
        if k:
            from_y[owned(k), :] = total.astype(BF)
            link.send((name, OVER_Z, k), mid, from_z.at[owned(k - 1)], {"dp": z_to(1)})
        else:
            out[...] = total

    small_send, small_recv, small_t = s.small_send, s.small_recv, s.small_t

    def small_start():
        small_send[...] = jnp.zeros_like(small_send)
        for e in range(n_dp):
            small_send[e, 2:8, :] = acc[2:8, e * dw : (e + 1) * dw]
        for i in range(owners):
            e = t * owners + i
            small_send[e, 0:2, :] = qacc[0:2, i * dw : (i + 1) * dw]
            for r in range(ebias_rows):
                at = (i * ebias_rows + r) * dw
                small_send[e, 8 + r : 9 + r, :] = hacc[0:1, at : at + dw]
        for o in range(1, n_dp):
            e = dp_to(o)
            link.send((SMALL, o), small_send.at[e], small_recv.at[o], {"dp": e})

    def small_forward():
        total = small_send[d]
        for o in range(1, n_dp):
            link.arrived((SMALL, o), small_recv.at[o], {"dp": dp_from(o)})
            total = total + small_recv[o]
        small_t[t] = total
        for what, peer in ((NEAR, t_core), (FAR, t_far), (NEAR_ON, t_diag)):
            link.send((SMALL_T, what), small_t.at[t], small_t.at[t], {"tensor": peer})

    def small_finish():
        for what, peer in ((NEAR, t_core), (FAR, t_far), (NEAR_ON, t_diag)):
            link.arrived((SMALL_T, what), small_t.at[peer], {"tensor": peer})
        total = small_t[0]
        for i in range(1, n_t):
            total = total + small_t[i]
        out_small[...] = total


    tokens_start(0)
    gather_start(W3)
    gather_start(PACK)
    gather_start(WO)
    gather_step(W3, RIGHT, 1)
    gather_step(PACK, LEFT, 1)
    gather_step(WO, LEFT, 1)
    gather_step(PACK, LEFT, 2)
    tokens_finish(0)
    ag_start(x_all, TX, 0)
    gather_step(W3, LEFT, 1)
    gather_step(PACK, RIGHT, 1)
    gather_step(PACK, RIGHT, 2)
    gather_step(WO, RIGHT, 1)
    gather_step(WO, LEFT, 2)
    gather_step(PACK, RIGHT, 3)
    gather_step(W3, RIGHT, 2)
    tokens_start(1)
    gather_step(PACK, LEFT, 3)
    gather_step(W3, LEFT, 2)
    ag_forward(x_all, TX, 0)
    gather_step(PACK, RIGHT, 4)
    gather_step(W3, RIGHT, 3)
    gather_step(WO, RIGHT, 2)
    gather_ready(PACK)
    gather_step(WO, LEFT, 3)
    tokens_finish(1)
    ag_start(x_all, TX, 1)
    gather_step(W3, LEFT, 3)
    tokens_start(2)
    gather_step(W3, RIGHT, 4)
    gather_ready(W3)
    gather_step(WO, RIGHT, 3)
    ag_forward(x_all, TX, 1)
    ag_finish(x_all, TX, 0)
    gather_start(WE)
    spread_vectors()
    gather_step(WO, LEFT, 4)
    gather_ready(WO)
    ag_finish(x_all, TX, 1)
    project(0)
    tokens_finish(2)
    ag_start(x_all, TX, 2)
    project(1)
    gather_start(WS)
    attention(1)
    project_out(1)
    rs_forward(R1, 1)
    gather_step(WE, RIGHT, 1)
    ag_forward(x_all, TX, 2)
    gather_step(WE, LEFT, 1)
    attention(0)
    project_out(0)
    gather_step(WS, LEFT, 1)
    ag_finish(x_all, TX, 2)
    gather_step(WS, RIGHT, 1)
    rs_forward(R1, 0)
    gather_step(WE, RIGHT, 2)
    gather_step(WE, LEFT, 2)
    rs_finish(R1, 1)
    norm_first(1)
    ag_start(u_all, TU, 1)
    project(2)
    attention(2)
    project_out(2)
    gather_step(WS, LEFT, 2)
    rs_forward(R1, 2)
    gather_step(WE, RIGHT, 3)
    ag_forward(u_all, TU, 1)
    rs_finish(R1, 0)
    norm_first(0)
    ag_start(u_all, TU, 0)
    gather_step(WS, LEFT, 3)
    gather_step(WS, RIGHT, 2)
    gather_step(WE, RIGHT, 4)
    gather_step(WE, LEFT, 3)
    ag_finish(u_all, TU, 1)
    gather_ready(WE)
    rs_finish(R1, 2)
    norm_first(2)
    ag_start(u_all, TU, 2)
    widen(1)
    ag_forward(u_all, TU, 0)
    gather_step(WS, LEFT, 4)
    gather_step(WS, RIGHT, 3)
    gather_ready(WS)
    cot_start()
    shrink_rows(1)
    rs_forward(R2, 1)
    ag_finish(u_all, TU, 0)
    widen(0)
    ag_forward(u_all, TU, 2)
    shrink_rows(0)
    ag_finish(u_all, TU, 2)
    rs_forward(R2, 0)
    widen(2)
    shrink_rows(2)
    rs_forward(R2, 2)
    cot_finish()
    rs_finish(R2, 0)
    norm_second(0)
    ag_start(dz, TZ, 0)
    rs_finish(R2, 2)
    norm_second(2)
    ag_start(dz, TZ, 2)
    ag_forward(dz, TZ, 0)
    rs_finish(R2, 1)
    norm_second(1)
    ag_start(dz, TZ, 1)
    ag_finish(dz, TZ, 0)
    rows_out(MIX, 0, n_seq, mixed_send, out_mixed)
    widen_back(0)
    ag_forward(dz, TZ, 2)
    normed_rows(0)
    rs_forward(R3, 0)
    ag_forward(dz, TZ, 1)
    ag_finish(dz, TZ, 2)
    widen_back(2)
    ag_finish(dz, TZ, 1)
    grad_tile(GS, 3)
    widen_back(1)
    rs_finish(R3, 0)
    norm_first_back(0)
    ag_start(dh, TH, 0)
    grad_tile(GE, 3)
    normed_rows(1)
    rs_forward(R3, 1)
    grad_forward(GS, 3)
    grad_tile(GS, 2)
    normed_rows(2)
    ag_forward(dh, TH, 0)
    rs_forward(R3, 2)
    grad_forward(GE, 3)
    grad_tile(GE, 2)
    ag_finish(dh, TH, 0)
    attention_back(0)
    rs_finish(R3, 1)
    norm_first_back(1)
    ag_start(dh, TH, 1)
    grad_forward(GS, 2)
    grad_tile(GS, 1)
    grad_forward(GE, 2)
    rs_finish(R3, 2)
    norm_first_back(2)
    ag_start(dh, TH, 2)
    rows_in(MIX, 0, n_seq, out_mixed)
    grad_tile(GE, 1)
    token_rows(0)
    ag_forward(dh, TH, 1)
    grad_forward(GS, 1)
    grad_tile(GS, 0)
    rs_forward(R4, 0)
    ag_forward(dh, TH, 2)
    ag_finish(dh, TH, 1)
    grad_forward(GE, 1)
    ag_finish(dh, TH, 2)
    grad_tile(GO, 3)
    attention_back(2)
    rs_finish(R4, 0)
    finish_rows(0)
    rows_out(BACK, 0, 1, back_send, back_recv)
    grad_forward(GO, 3)
    grad_tile(GO, 2)
    attention_back(1)
    grad_tile(G3, 3)
    token_rows(1)
    grad_forward(GO, 2)
    small_start()
    rs_forward(R4, 1)
    grad_tile(GO, 1)
    grad_tile(G3, 2)
    grad_forward(G3, 3)
    token_rows(2)
    grad_tile(G3, 1)
    grad_forward(GO, 1)
    rs_finish(R4, 1)
    finish_rows(1)
    rows_out(BACK, 1, 1, back_send, back_recv)
    grad_forward(G3, 2)
    grad_tile(GE, 0)
    rows_in(BACK, 0, 1, back_recv)
    rs_forward(R4, 2)
    small_forward()
    grad_tile(GO, 0)
    grad_tile(G3, 0)
    rs_finish(R4, 2)
    finish_rows(2)
    rows_out(BACK, 2, 1, back_send, back_recv)
    grad_forward(GS, 0)
    grad_forward(G3, 1)
    grad_forward(GO, 0)
    small_finish()
    grad_forward(GE, 0)
    rows_in(BACK, 1, 1, back_recv)
    grad_forward(G3, 0)
    rows_in(BACK, 2, 1, back_recv)
    link.drain()


def finish_kernel(
    ebias_rows,
    order_s,
    mixed,
    back,
    g3,
    go,
    ge,
    gs,
    small,
    out_mixed,
    out_back,
    out_g3,
    out_go,
    out_ge,
    out_gs,
    out_biases,
    out_gains,
    out_hidden,
):
    def move(k, carry):
        out_back[k] = back[order_s[k]]
        return carry

    lax.fori_loop(0, out_back.shape[0], move, 0)
    out_mixed[...] = mixed[...]
    width = out_g3.shape[2]
    for w in range(3):
        out_g3[w] = g3[:, w * width : (w + 1) * width]
    out_go[...] = jnp.transpose(go[...])
    out_gs[...] = jnp.transpose(gs[...])
    out_ge[...] = ge[...]
    out_biases[...] = small[0:6]
    out_gains[...] = small[6:8]
    out_hidden[...] = small[8 : 8 + ebias_rows]


def body(
    tokens,
    cotangent,
    lengths,
    order,
    triple_weight,
    output_weight,
    expand_weight,
    shrink_weight,
    biases,
    gains,
    expand_bias,
):
    n_dp, n_t = lax.axis_size("dp"), lax.axis_size("tensor")
    slots, _, rows, width = tokens.shape
    n_seq = slots // n_dp
    quarter = rows * n_dp
    full = quarter * n_t
    dw = triple_weight.shape[1]
    hw = triple_weight.shape[2]
    fw = expand_weight.shape[1]
    fits = (
        n_t == 4
        and n_dp % 4 == 0
        and rows % 16 == 0
        and dw % 128 == 0
        and hw % 128 == 0
        and n_seq == 3
        and expand_bias.shape[0] % dw == 0
        and n_dp % n_t == 0
    )
    if not fits:
        return plain_body(
            tokens,
            cotangent,
            lengths,
            order,
            triple_weight,
            output_weight,
            expand_weight,
            shrink_weight,
            biases,
            gains,
            expand_bias,
        )
    n_y = 2
    n_z = n_dp // n_y
    ebias_rows = expand_bias.shape[0] // dw
    all_rows = n_seq * full
    own_rows = n_seq * quarter
    vm = pltpu.VMEM
    scratch = dict(
        stage=vm((slots, rows, width), BF),
        x_all=vm((all_rows, width), BF),
        cots=vm((n_seq, quarter, width), BF),
        w3_all=vm((3, width, hw), BF),
        wo_all=vm((hw, width), BF),
        we_all=vm((width, fw), BF),
        ws_all=vm((fw, width), BF),
        pack_own=vm((16, dw), F32),
        vec=vm((16, width), F32),
        ebias=vm((8, fw), F32),
        qkv=vm((all_rows, 3 * hw), BF),
        att=vm((all_rows, hw), BF),
        lse=vm((n_seq, 8, full), F32),
        part=vm((all_rows, width), BF),
        r_a=vm((own_rows, width), BF),
        r_b=vm((own_rows, width), BF),
        r_x=vm((own_rows, width), BF),
        n1=vm((own_rows, width), F32),
        inv1=vm((own_rows, 128), F32),
        u_all=vm((all_rows, width), BF),
        hid=vm((all_rows, fw), BF),
        slope=vm((all_rows, fw), BF),
        dz=vm((all_rows, width), BF),
        dh=vm((all_rows, width), BF),
        dy=vm((own_rows, width), F32),
        dqkv=vm((all_rows, 3 * hw), BF),
        acc=vm((8, width), F32),
        hacc=vm((8, fw), F32),
        qacc=vm((8, hw), F32),
        kt=vm((hw, full), BF),
        ot=vm((hw, full), F32),
        dk_acc=vm((full, hw), F32),
        dv_acc=vm((full, hw), F32),
        da=vm((full, hw), BF),
        mixed_send=vm((n_seq, quarter, width), BF),
        back_send=vm((n_seq, quarter, width), BF),
        gs=vm((width, fw), BF),
        gs_y=vm((n_z * dw, fw), BF),
        gs_z=vm(((n_z - 1) * dw, fw), BF),
        ge=vm((width, fw), BF),
        ge_y=vm((n_z * dw, fw), BF),
        ge_z=vm(((n_z - 1) * dw, fw), BF),
        go=vm((width, hw), BF),
        go_y=vm((n_z * dw, hw), BF),
        go_z=vm(((n_z - 1) * dw, hw), BF),
        g3=vm((width, 3 * hw), BF),
        g3_y=vm((n_z * dw, 3 * hw), BF),
        g3_z=vm(((n_z - 1) * dw, 3 * hw), BF),
        small_send=vm((n_dp, 16, dw), F32),
        small_recv=vm((n_dp, 16, dw), F32),
        small_t=vm((n_t, 16, dw), F32),
        send_sems=pltpu.SemaphoreType.DMA((N_SEM,)),
        recv_sems=pltpu.SemaphoreType.DMA((N_SEM,)),
        local_sems=pltpu.SemaphoreType.DMA((24,)),
    )
    g = types.SimpleNamespace(
        n_seq=n_seq,
        quarter=quarter,
        width=width,
        n_dp=n_dp,
        n_y=n_y,
        n_t=n_t,
        head_width=hw,
        hidden_width=fw,
        ebias_rows=ebias_rows,
        scratch_names=tuple(scratch),
    )
    smem = pl.BlockSpec(memory_space=pltpu.SMEM)
    vmem = pl.BlockSpec(memory_space=pltpu.VMEM)
    anywhere = pl.BlockSpec(memory_space=pl.ANY)
    sds = jax.ShapeDtypeStruct
    flops = 2 * all_rows * (3 * width * 3 * hw + 3 * width * hw + 6 * width * fw + 7 * full * hw)
    mixed, back, g3, go, ge, gs, small = pl.pallas_call(
        functools.partial(layer_kernel, g),
        out_shape=(
            sds(tokens.shape[:1] + (rows, width), BF),
            sds(tokens.shape[:1] + (rows, width), BF),
            sds((dw, 3 * hw), F32),
            sds((dw, hw), F32),
            sds((dw, fw), F32),
            sds((dw, fw), F32),
            sds((16, dw), F32),
        ),
        in_specs=[smem] * 2 + [vmem] + [anywhere] * 5 + [vmem] * 3,
        out_specs=[anywhere] * 2 + [vmem] * 5,
        scratch_shapes=list(scratch.values()),
        compiler_params=pltpu.CompilerParams(
            collective_id=0,
            has_side_effects=True,
            vmem_limit_bytes=VMEM_BYTES,
        ),
        cost_estimate=pl.CostEstimate(flops=flops, bytes_accessed=1 << 24, transcendentals=0),
    )(
        order,
        lengths,
        tokens.reshape(slots, rows, width),
        cotangent.reshape(slots, rows, width),
        triple_weight,
        output_weight,
        expand_weight,
        shrink_weight,
        biases,
        gains,
        expand_bias.reshape(ebias_rows, dw),
    )
    finals = pl.pallas_call(
        functools.partial(finish_kernel, ebias_rows),
        out_shape=(
            sds(mixed.shape, BF),
            sds(back.shape, BF),
            sds((3, dw, hw), F32),
            sds((hw, dw), F32),
            sds((dw, fw), F32),
            sds((fw, dw), F32),
            sds((6, dw), F32),
            sds((2, dw), F32),
            sds((ebias_rows, dw), F32),
        ),
        in_specs=[smem] + [vmem] * 7,
        out_specs=[vmem] * 9,
        compiler_params=pltpu.CompilerParams(vmem_limit_bytes=VMEM_BYTES),
    )(order, mixed, back, g3, go, ge, gs, small)
    return (
        finals[0].reshape(tokens.shape),
        finals[1].reshape(tokens.shape),
        *finals[2:8],
        finals[8].reshape(expand_bias.shape),
    )


def solution(mesh):
    return jax.shard_map(
        body,
        mesh=mesh,
        in_specs=(
            P(None, "tensor", "dp", None),
            P(None, "tensor", "dp", None),
            P(),
            P(),
            P(None, "dp", "tensor"),
            P(None, "dp"),
            P("dp", "tensor"),
            P("tensor", "dp"),
            P(None, "dp"),
            P(None, "dp"),
            P("dp"),
        ),
        out_specs=(
            P(None, "tensor", "dp", None),
            P(None, "tensor", "dp", None),
            P(None, "dp", "tensor"),
            P("tensor", "dp"),
            P("dp", "tensor"),
            P("tensor", "dp"),
            P(None, "dp"),
            P(None, "dp"),
            P("dp"),
        ),
        check_vma=False,
    )
```

```python
import functools
import math
import types

import jax
import jax.numpy as jnp
from jax import lax
from jax.experimental import pallas as pl
from jax.experimental.pallas import tpu as pltpu
from jax.sharding import PartitionSpec as P

HEAD_DIM = 64


EPSILON = 1e-12
MASKED = -1e30


def normalize(values, gain, shift):
    center = values - jnp.mean(values, axis=-1, keepdims=True)
    spread = jnp.mean(center * center, axis=-1, keepdims=True)
    inv_std = lax.rsqrt(spread + EPSILON)
    scaled = center * inv_std
    return (scaled * gain + shift, scaled, inv_std)


def normalize_back(grad_rows, scaled, inv_std, gain):
    pushed = grad_rows * gain
    first = jnp.mean(pushed, axis=-1, keepdims=True)
    second = jnp.mean(pushed * scaled, axis=-1, keepdims=True)
    return inv_std * (pushed - first - scaled * second)


def gelu_exact(values):
    return 0.5 * values * (1.0 + jax.scipy.special.erf(values / math.sqrt(2.0)))


def gelu_slope(values):
    return 0.5 * (1.0 + jax.scipy.special.erf(values / math.sqrt(2.0))) + values * jnp.exp(
        -0.5 * values * values
    ) / math.sqrt(2.0 * math.pi)


def split_heads(rows):
    return rows.reshape(rows.shape[0], rows.shape[1] // HEAD_DIM, HEAD_DIM)


def score_block(queries, key_rows, seq_length):
    raw_scores = jnp.einsum("qhe,khe->hqk", queries, key_rows, preferred_element_type=jnp.float32)
    scores = raw_scores * (1.0 / math.sqrt(HEAD_DIM))
    visible = jnp.arange(key_rows.shape[0]) < seq_length
    return jnp.where(visible[None, None, :], scores, MASKED)


def attend(seq_item):
    queries, key_rows, value_rows, seq_length = seq_item
    queries = split_heads(queries)
    key_rows = split_heads(key_rows)
    value_rows = split_heads(value_rows)
    masked = score_block(queries, key_rows, seq_length)
    highest = jnp.max(masked, axis=-1, keepdims=True)
    totals = jnp.sum(jnp.exp(masked - highest), axis=-1, keepdims=True)
    log_totals = highest + jnp.log(totals)
    probs = jnp.exp(masked - log_totals).astype(jnp.bfloat16)
    blended = jnp.einsum("hqk,khe->qhe", probs, value_rows, preferred_element_type=jnp.float32)
    return (blended.astype(jnp.bfloat16).reshape(queries.shape[0], -1), log_totals[..., 0])


def attend_back(seq_item):
    queries, key_rows, value_rows, grad_rows, log_totals, seq_length = seq_item
    queries = split_heads(queries)
    key_rows = split_heads(key_rows)
    value_rows = split_heads(value_rows)
    grad_heads = split_heads(grad_rows)
    masked = score_block(queries, key_rows, seq_length)
    probs = jnp.exp(masked - log_totals[..., None])
    grad_probs = jnp.einsum(
        "qhe,khe->hqk", grad_heads, value_rows, preferred_element_type=jnp.float32
    )
    inner = jnp.sum(probs * grad_probs, axis=-1, keepdims=True)
    grad_scores = (probs * (grad_probs - inner)).astype(jnp.bfloat16)
    score_scale = 1.0 / math.sqrt(HEAD_DIM)
    grad_query = (
        jnp.einsum("hqk,khe->qhe", grad_scores, key_rows, preferred_element_type=jnp.float32)
        * score_scale
    )
    grad_key = (
        jnp.einsum("hqk,qhe->khe", grad_scores, queries, preferred_element_type=jnp.float32)
        * score_scale
    )
    grad_value = jnp.einsum(
        "hqk,qhe->khe", probs.astype(jnp.bfloat16), grad_heads, preferred_element_type=jnp.float32
    )
    row_count = queries.shape[0]
    return (
        grad_query.astype(jnp.bfloat16).reshape(row_count, -1),
        grad_key.astype(jnp.bfloat16).reshape(row_count, -1),
        grad_value.astype(jnp.bfloat16).reshape(row_count, -1),
    )


def plain_body(
    tokens,
    cotangent,
    lengths,
    order,
    triple_weight,
    output_weight,
    expand_weight,
    shrink_weight,
    biases,
    gains,
    expand_bias,
):
    seq_count = order.shape[0]
    per_group = seq_count // lax.axis_size("dp")
    tensor_size = lax.axis_size("tensor")
    member = lax.axis_index("dp")
    my_rank = lax.axis_index("tensor")
    slot_ids = jnp.arange(seq_count, dtype=jnp.int32)
    inverse = jnp.zeros((seq_count,), jnp.int32).at[order].set(slot_ids)
    local_x, local_dy = (
        lax.all_to_all(tokens[inverse], "dp", split_axis=0, concat_axis=2, tiled=True),
        lax.all_to_all(cotangent, "dp", split_axis=0, concat_axis=2, tiled=True),
    )
    quarter = local_x.shape[2]
    model_width = local_x.shape[3]
    full_length = quarter * tensor_size
    my_lengths = lax.dynamic_slice_in_dim(lengths, member * per_group, per_group)
    gathered = (
        lax.all_gather(triple_weight, "dp", axis=1, tiled=True),
        lax.all_gather(output_weight, "dp", axis=1, tiled=True),
        lax.all_gather(expand_weight, "dp", axis=0, tiled=True),
        lax.all_gather(shrink_weight, "dp", axis=1, tiled=True),
        lax.all_gather(biases, "dp", axis=1, tiled=True),
        lax.all_gather(gains, "dp", axis=1, tiled=True),
        lax.all_gather(expand_bias, "dp", axis=0, tiled=True),
    )
    query_key_value_proj, out_weight, widen_projection, shrink, bias_rows, gain_rows, exp_bias = (
        gathered
    )
    head_width = query_key_value_proj.shape[2]
    hidden_width = widen_projection.shape[1]
    out_heads = lax.dynamic_slice_in_dim(out_weight, my_rank * head_width, head_width, 0)
    bias_query = lax.dynamic_slice_in_dim(bias_rows[0], my_rank * head_width, head_width).astype(
        jnp.float32
    )
    bias_value = lax.dynamic_slice_in_dim(bias_rows[1], my_rank * head_width, head_width).astype(
        jnp.float32
    )
    bias_hidden = lax.dynamic_slice_in_dim(exp_bias, my_rank * hidden_width, hidden_width).astype(
        jnp.float32
    )
    bias_stack = jnp.stack([bias_query, jnp.zeros_like(bias_query), bias_value])
    gain_first = gain_rows[0].astype(jnp.float32)
    gain_second = gain_rows[1].astype(jnp.float32)
    full_shape = (per_group, tensor_size, quarter, model_width)
    token_all_rows = lax.all_gather(local_x, "tensor", axis=1, tiled=True).reshape(
        per_group, full_length, model_width
    )
    projected = (
        jnp.einsum(
            "jah,rhu->rjau",
            token_all_rows,
            query_key_value_proj,
            preferred_element_type=jnp.float32,
        )
        + bias_stack[:, None, None, :]
    ).astype(jnp.bfloat16)
    attended, log_totals = lax.map(attend, (projected[0], projected[1], projected[2], my_lengths))
    attn_terms = jnp.einsum(
        "sle,em->slm", attended, out_heads, preferred_element_type=jnp.float32
    ).reshape(full_shape)
    attn_sum = lax.psum_scatter(attn_terms, "tensor", scatter_dimension=1, tiled=True)
    hidden_in = local_x.astype(jnp.float32) + (attn_sum + bias_rows[2].astype(jnp.float32))
    normed, normed_scaled, normed_inv = normalize(
        hidden_in, gain_first, bias_rows[3].astype(jnp.float32)
    )
    normalized_all_rows = lax.all_gather(
        normed.astype(jnp.bfloat16), "tensor", axis=1, tiled=True
    ).reshape(per_group, full_length, model_width)
    pre_act = (
        jnp.einsum(
            "uqj,jt->uqt", normalized_all_rows, widen_projection, preferred_element_type=jnp.float32
        )
        + bias_hidden
    )
    hidden = gelu_exact(pre_act).astype(jnp.bfloat16)
    ffn_terms = jnp.einsum(
        "slf,fm->slm", hidden, shrink, preferred_element_type=jnp.float32
    ).reshape(full_shape)
    ffn_sum = lax.psum_scatter(
        ffn_terms.astype(jnp.bfloat16), "tensor", scatter_dimension=1, tiled=True
    ).astype(jnp.float32)
    total_rows = normed + (ffn_sum + bias_rows[4].astype(jnp.float32))
    output, out_scaled, out_inv = normalize(
        total_rows, gain_second, bias_rows[5].astype(jnp.float32)
    )
    positions = my_rank * quarter + jnp.arange(quarter)
    valid = (positions[None, :] < my_lengths[:, None]).astype(jnp.float32)
    grad_out = local_dy.astype(jnp.float32) * valid[:, None, :, None]
    row_axes = (0, 1, 2)
    gain_grad_second = jnp.sum(grad_out * out_scaled, axis=row_axes)
    shift_grad_second = jnp.sum(grad_out, axis=row_axes)
    grad_total = normalize_back(grad_out, out_scaled, out_inv, gain_second)
    branch_bias_grad = jnp.sum(grad_total, axis=row_axes)
    grad_branch = lax.all_gather(
        grad_total.astype(jnp.bfloat16), "tensor", axis=1, tiled=True
    ).reshape(per_group, full_length, model_width)
    shrink_grad = jnp.einsum("slf,slm->fm", hidden, grad_branch, preferred_element_type=jnp.float32)
    grad_hidden = jnp.einsum("slm,fm->slf", grad_branch, shrink, preferred_element_type=jnp.float32)
    preactivation_grad = (grad_hidden * gelu_slope(pre_act)).astype(jnp.bfloat16)
    hidden_bias_grad = jnp.sum(preactivation_grad, axis=(0, 1), dtype=jnp.float32)
    expand_grad = jnp.einsum(
        "mgc,mga->ca", normalized_all_rows, preactivation_grad, preferred_element_type=jnp.float32
    )
    normed_terms = jnp.einsum(
        "cpk,rk->cpr", preactivation_grad, widen_projection, preferred_element_type=jnp.float32
    ).reshape(full_shape)
    grad_normed = grad_total + lax.psum_scatter(
        normed_terms.astype(jnp.bfloat16), "tensor", scatter_dimension=1, tiled=True
    ).astype(jnp.float32)
    first_norm_gain_grad = jnp.sum(grad_normed * normed_scaled, axis=row_axes)
    shift_grad_first = jnp.sum(grad_normed, axis=row_axes)
    grad_hidden_in = normalize_back(grad_normed, normed_scaled, normed_inv, gain_first)
    out_bias_grad = jnp.sum(grad_hidden_in, axis=row_axes)
    grad_attn = lax.all_gather(
        grad_hidden_in.astype(jnp.bfloat16), "tensor", axis=1, tiled=True
    ).reshape(per_group, full_length, model_width)
    output_grad = jnp.einsum("sle,slm->em", attended, grad_attn, preferred_element_type=jnp.float32)
    grad_blended = jnp.einsum(
        "slm,em->sle", grad_attn, out_heads, preferred_element_type=jnp.float32
    ).astype(jnp.bfloat16)
    grad_query, grad_key, grad_value = lax.map(
        attend_back,
        (projected[0], projected[1], projected[2], grad_blended, log_totals, my_lengths),
    )
    projection_output_grad = jnp.stack([grad_query, grad_key, grad_value])
    query_bias_grad = jnp.sum(grad_query, axis=(0, 1), dtype=jnp.float32)
    value_bias_grad = jnp.sum(grad_value, axis=(0, 1), dtype=jnp.float32)
    triple_grad = jnp.einsum(
        "xyt,vxyu->vtu", token_all_rows, projection_output_grad, preferred_element_type=jnp.float32
    )
    token_terms = jnp.einsum(
        "atpi,aki->tpk",
        projection_output_grad,
        query_key_value_proj,
        preferred_element_type=jnp.float32,
    ).reshape(full_shape)
    grad_tokens = grad_hidden_in + lax.psum_scatter(
        token_terms.astype(jnp.bfloat16), "tensor", scatter_dimension=1, tiled=True
    ).astype(jnp.float32)
    zero_row = jnp.zeros((model_width,), jnp.float32)
    query_full = lax.dynamic_update_slice_in_dim(zero_row, query_bias_grad, my_rank * head_width, 0)
    value_full = lax.dynamic_update_slice_in_dim(zero_row, value_bias_grad, my_rank * head_width, 0)
    bias_grad = jnp.stack(
        [
            query_full,
            value_full,
            out_bias_grad,
            shift_grad_first,
            branch_bias_grad,
            shift_grad_second,
        ]
    )
    gain_grad = jnp.stack([first_norm_gain_grad, gain_grad_second])
    hidden_full = lax.dynamic_update_slice_in_dim(
        jnp.zeros((exp_bias.shape[0],), jnp.float32), hidden_bias_grad, my_rank * hidden_width, 0
    )
    bias_grad, gain_grad, hidden_full = (
        lax.psum(bias_grad.astype(jnp.bfloat16), "tensor").astype(jnp.float32),
        lax.psum(gain_grad.astype(jnp.bfloat16), "tensor").astype(jnp.float32),
        lax.psum(hidden_full.astype(jnp.bfloat16), "tensor").astype(jnp.float32),
    )
    shards = (
        lax.psum_scatter(triple_grad, "dp", scatter_dimension=1, tiled=True),
        lax.psum_scatter(output_grad, "dp", scatter_dimension=1, tiled=True),
        lax.psum_scatter(expand_grad, "dp", scatter_dimension=0, tiled=True),
        lax.psum_scatter(shrink_grad, "dp", scatter_dimension=1, tiled=True),
        lax.psum_scatter(bias_grad, "dp", scatter_dimension=1, tiled=True),
        lax.psum_scatter(gain_grad, "dp", scatter_dimension=1, tiled=True),
        lax.psum_scatter(hidden_full, "dp", scatter_dimension=0, tiled=True),
    )
    mixed_rows, back_rows = (
        lax.all_to_all(output.astype(jnp.bfloat16), "dp", split_axis=2, concat_axis=0, tiled=True),
        lax.all_to_all(
            grad_tokens.astype(jnp.bfloat16), "dp", split_axis=2, concat_axis=0, tiled=True
        ),
    )
    return (
        mixed_rows,
        back_rows[order],
        shards[0],
        shards[1],
        shards[2],
        shards[3],
        shards[4],
        shards[5],
        shards[6],
    )


BF = jnp.bfloat16
F32 = jnp.float32
MESH = pl.DeviceIdType.MESH
LOG2E = math.log2(math.e)
N_SEM = 175
PACK, WQ, WK, WV, WO, WE0, WE1, WS0, WS1 = range(9)
GS, GE, G3, GO = range(10, 14)
TX, TU, TZ, TH, R1, R2, R3, R4 = range(20, 28)
TOK, COT, MIX, BACK, SMALL, SMALL_T = range(30, 36)
RIGHT, LEFT, OVER_Y, OVER_Z, FAR, NEAR, NEAR_ON = range(40, 47)
VMEM_BYTES = 64 * 1024 * 1024


def mm(a, b):
    return lax.dot_general(a, b, (((1,), (0,)), ((), ())), preferred_element_type=F32)


def mm_t(a, b):
    return lax.dot_general(a, b, (((1,), (1,)), ((), ())), preferred_element_type=F32)


def t_mm(a, b):
    return lax.dot_general(a, b, (((0,), (0,)), ((), ())), preferred_element_type=F32)


class Links:
    def __init__(self, send_sems, recv_sems, local_sems):
        self.send_sems = send_sems
        self.recv_sems = recv_sems
        self.local_sems = local_sems
        self.slots = {}
        self.flying = {}
        self.local_count = 0

    def slot(self, name):
        if TX <= name[0] <= TH:
            name = (TX,) + name[1:]
        if R1 <= name[0] <= R4:
            name = (R1,) + name[1:]
        return self.slots.setdefault(name, len(self.slots))

    def send(self, name, src, dst, where):
        i = self.slot(name)
        if i in self.flying:
            self.sent(name)
        copy = pltpu.make_async_remote_copy(
            src_ref=src,
            dst_ref=dst,
            send_sem=self.send_sems.at[i],
            recv_sem=self.recv_sems.at[i],
            device_id=where,
            device_id_type=MESH,
        )
        copy.start()
        self.flying[i] = copy

    def sent(self, name):
        self.flying.pop(self.slot(name)).wait_send()

    def arrived(self, name, dst, where):
        i = self.slot(name)
        pltpu.make_async_remote_copy(
            src_ref=dst,
            dst_ref=dst,
            send_sem=self.send_sems.at[i],
            recv_sem=self.recv_sems.at[i],
            device_id=where,
            device_id_type=MESH,
        ).wait_recv()

    def drain(self):
        for copy in self.flying.values():
            copy.wait_send()

    def local(self, src, dst):
        copy = pltpu.make_async_copy(src, dst, self.local_sems.at[self.local_count])
        self.local_count += 1
        copy.start()
        return copy


def layer_kernel(g, *refs):
    (order_s, lengths_s, tok, cot, w3, wo, we, ws, bias_in, gain_in, hidden_in) = refs[:11]
    (out_mixed, back_recv, out_g3, out_go, out_ge, out_gs, out_small) = refs[11:18]
    s = types.SimpleNamespace(**dict(zip(g.scratch_names, refs[18:])))
    n_seq, quarter, width = g.n_seq, g.quarter, g.width
    n_dp, n_y, n_t = g.n_dp, g.n_y, g.n_t
    n_z = n_dp // n_y
    full = n_t * quarter
    half = full // 2
    rows = quarter // n_dp
    hw, fw = g.head_width, g.hidden_width
    heads = hw // HEAD_DIM
    dw = width // n_dp
    tile = 256
    ebias_rows = g.ebias_rows
    owners = n_dp // n_t

    d = lax.axis_index("dp")
    t = lax.axis_index("tensor")
    z, y = d // n_y, d % n_y
    x, c = t // 2, t % 2
    t_core = x * 2 + (1 - c)
    t_far = (1 - x) * 2 + c
    t_diag = (1 - x) * 2 + (1 - c)

    def dp_to(o):
        return (d + o) % n_dp

    def dp_from(o):
        return (d + n_dp - o) % n_dp

    def z_to(k):
        return ((z + k) % n_z) * n_y + y

    def z_from(k):
        return ((z + n_z - k) % n_z) * n_y + y

    y_peer = z * n_y + (1 - y)
    ring = (1 - y) * z + y * (n_dp - 1 - z)

    def ring_at(k):
        r = (ring + n_dp + k) % n_dp
        back = r // n_z
        return ((1 - back) * r + back * (n_dp - 1 - r)) * n_y + back

    link = Links(s.send_sems, s.recv_sems, s.local_sems)

    barrier = pltpu.get_barrier_semaphore()
    for o in range(1, n_dp):
        pl.semaphore_signal(barrier, inc=1, device_id={"dp": dp_to(o)}, device_id_type=MESH)
    for peer in (t_core, t_far, t_diag):
        pl.semaphore_signal(barrier, inc=1, device_id={"tensor": peer}, device_id_type=MESH)

    stage, x_all, cots = s.stage, s.x_all, s.cots
    w3_all, wo_all, we_all, ws_all = s.w3_all, s.wo_all, s.we_all, s.ws_all
    pack_own, vec, ebias = s.pack_own, s.vec, s.ebias
    qkv, att, lse, part = s.qkv, s.att, s.lse, s.part
    r_a, r_b, r_x = s.r_a, s.r_b, s.r_x
    n1, inv1, u_all, hid, slope = s.n1, s.inv1, s.u_all, s.hid, s.slope
    dz, dh, dy, dqkv = s.dz, s.dh, s.dy, s.dqkv
    acc, hacc, qacc = s.acc, s.hacc, s.qacc
    kt, ot, dk_acc, dv_acc, da = s.kt, s.ot, s.dk_acc, s.dv_acc, s.da
    mixed_send, back_send = s.mixed_send, s.back_send

    def al(v, m):
        return pl.multiple_of(v, m)

    def seq_rows(j, start, n):
        return pl.ds(al(j * full + start, 16), n)

    def mine(j):
        return seq_rows(j, t * quarter, quarter)


    def permute(k, carry):
        arrival = jnp.int32(0)
        for i in range(n_dp * n_seq):
            arrival = jnp.where(order_s[i] == k, i, arrival)
        stage[k] = tok[arrival]
        return carry

    lax.fori_loop(0, n_dp * n_seq, permute, 0)
    pack_own[0:6, :] = bias_in[...].astype(F32)
    pack_own[6:8, :] = gain_in[...].astype(F32)
    pack_own[8 : 8 + ebias_rows, :] = hidden_in[...].astype(F32)
    pack_own[8 + ebias_rows :, :] = jnp.zeros((16 - 8 - ebias_rows, dw), F32)
    acc[...] = jnp.zeros_like(acc)
    hacc[...] = jnp.zeros_like(hacc)
    qacc[...] = jnp.zeros_like(qacc)
    pl.semaphore_wait(barrier, n_dp - 1 + 3)

    def x_block(j, src):
        return x_all.at[seq_rows(j, t * quarter + src * rows, rows)]

    def tokens_start(j):
        for o in range(1, n_dp):
            e = dp_to(o)
            link.send((TOK, j, o), stage.at[e * n_seq + j], x_block(j, d), {"dp": e})
        x_all[seq_rows(j, t * quarter + d * rows, rows), :] = stage[d * n_seq + j]

    def tokens_finish(j):
        for o in range(1, n_dp):
            link.arrived((TOK, j, o), x_block(j, dp_from(o)), {"dp": dp_from(o)})

    def cot_block(src):
        return cots.at[:, pl.ds(al(src * rows, 16), rows), :]

    own_copies = {}

    def cot_start():
        for o in range(1, n_dp):
            e = dp_to(o)
            link.send((COT, o), cot.at[pl.ds(e * n_seq, n_seq)], cot_block(d), {"dp": e})
        own_copies[COT] = link.local(cot.at[pl.ds(d * n_seq, n_seq)], cot_block(d))

    def cot_finish():
        own_copies.pop(COT).wait()
        for o in range(1, n_dp):
            link.arrived((COT, o), cot_block(dp_from(o)), {"dp": dp_from(o)})

    def cols(ref, e):
        return ref.at[:, pl.ds(al(e * dw, 128), dw)]

    def w3_part(w, steps):
        return (w3.at[w], lambda e: w3_all.at[w, pl.ds(al(e * dw, 16), dw), :], steps)

    def we_part(i, steps):
        span = pl.ds(i * (fw // 2), fw // 2)
        return (we.at[:, span], lambda e: we_all.at[pl.ds(al(e * dw, 16), dw), span], steps)

    def ws_part(i, steps):
        span = pl.ds(i * (fw // 2), fw // 2)
        return (ws.at[span, :], lambda e: ws_all.at[span, pl.ds(al(e * dw, 128), dw)], steps)

    more, less = n_dp // 2, n_dp // 2 - 1
    gathers = {
        PACK: (pack_own, lambda e: cols(vec, e), n_dp // 2),
        WQ: w3_part(0, more),
        WK: w3_part(1, less),
        WV: w3_part(2, more),
        WO: (
            wo.at[pl.ds(al(t * hw, 16), hw), :],
            lambda e: cols(wo_all, e),
            n_dp // 2 - 1,
        ),
        WE0: we_part(0, more),
        WE1: we_part(1, less),
        WS0: ws_part(0, more),
        WS1: ws_part(1, less),
    }

    def gather_start(name):
        src, block, _ = gathers[name]
        link.send((name, RIGHT, 1), src, block(d), {"dp": ring_at(1)})
        link.send((name, LEFT, 1), src, block(d), {"dp": ring_at(-1)})
        own_copies[name] = link.local(src, block(d))

    def gather_step(name, way, k):
        _, block, right = gathers[name]
        steps, sign = (right, -1) if way == RIGHT else (n_dp - 1 - right, 1)
        got = block(ring_at(sign * k))
        link.arrived((name, way, k), got, {"dp": ring_at(sign)})
        if k < steps:
            link.send((name, way, k + 1), got, got, {"dp": ring_at(-sign)})

    def gather_ready(name):
        own_copies.pop(name).wait()


    def t_rows(j, who):
        return seq_rows(j, who * quarter, quarter)

    def ag_start(buf, tag, j):
        own = buf.at[t_rows(j, t)]
        link.send((tag, FAR, j), own, own, {"tensor": t_far})
        link.send((tag, NEAR, j), own, own, {"tensor": t_core})

    def ag_forward(buf, tag, j):
        got = buf.at[t_rows(j, t_far)]
        link.arrived((tag, FAR, j), got, {"tensor": t_far})
        link.send((tag, NEAR_ON, j), got, got, {"tensor": t_core})

    def ag_finish(buf, tag, j):
        link.arrived((tag, NEAR, j), buf.at[t_rows(j, t_core)], {"tensor": t_core})
        link.arrived((tag, NEAR_ON, j), buf.at[t_rows(j, t_diag)], {"tensor": t_core})

    def q_rows(j):
        return pl.ds(j * quarter, quarter)

    def rs_start_far(tag, j):
        link.send((tag, NEAR_ON, j), part.at[t_rows(j, t_diag)], r_b.at[q_rows(j)], {"tensor": t_core})

    def rs_start_near(tag, j):
        link.send((tag, NEAR, j), part.at[t_rows(j, t_core)], r_a.at[q_rows(j)], {"tensor": t_core})

    def rs_forward(tag, j):
        link.arrived((tag, NEAR_ON, j), r_b.at[q_rows(j)], {"tensor": t_core})
        far = t_rows(j, t_far)
        both = part[far, :].astype(F32) + r_b[q_rows(j), :].astype(F32)
        part[far, :] = both.astype(BF)
        link.send((tag, FAR, j), part.at[far], r_x.at[q_rows(j)], {"tensor": t_far})

    def rs_finish(tag, j):
        link.arrived((tag, NEAR, j), r_a.at[q_rows(j)], {"tensor": t_core})
        link.arrived((tag, FAR, j), r_x.at[q_rows(j)], {"tensor": t_far})

    chunk = 32

    def row_loop(fn):
        lax.fori_loop(0, quarter // chunk, lambda i, carry: fn(i * chunk) or carry, 0)

    def summed(j, r):
        loc = seq_rows(j, t * quarter + r, chunk)
        buf = pl.ds(al(j * quarter + r, 16), chunk)
        return (
            part[loc, :].astype(F32)
            + r_a[buf, :].astype(F32)
            + r_x[buf, :].astype(F32)
        )

    def add_sum(row, value):
        acc[row : row + 1, :] += jnp.sum(value, axis=0, keepdims=True)

    def two_halves(tag, j, fn):
        if tag > R1:
            for what in (NEAR_ON, NEAR, FAR):
                link.sent((tag - 1, what, j))
        fn(al(j * full + (1 - x) * half, 16))
        rs_start_far(tag, j)
        fn(al(j * full + x * half, 16))
        rs_start_near(tag, j)

    def by_tiles(n, fn):
        lax.fori_loop(0, n // tile, lambda i, carry: fn(al(i * tile, tile)) or carry, 0)


    def spread_vectors():
        for i in range(owners):
            e = t * owners + i
            for r in range(ebias_rows):
                ebias[0:1, (i * ebias_rows + r) * dw : (i * ebias_rows + r + 1) * dw] = vec[
                    8 + r : 9 + r, pl.ds(al(e * dw, 128), dw)
                ]


    def project(j):
        at = pl.ds(j * full, full)
        for w in range(3):
            span = slice(w * hw, (w + 1) * hw)
            value = mm(x_all[at, :], w3_all[w])
            if w == 0:
                value = value + vec[0:1, pl.ds(al(t * hw, 128), hw)]
            if w == 2:
                value = value + vec[1:2, pl.ds(al(t * hw, 128), hw)]
            qkv[at, span] = value.astype(BF)

    lane_head = lax.broadcasted_iota(jnp.int32, (full, hw), 1) // HEAD_DIM
    scale2 = LOG2E / math.sqrt(HEAD_DIM)

    def head_scores(j, h, at):
        q_head = jnp.where(lane_head == h, qkv[at, 0:hw], jnp.zeros((), BF))
        raw = mm_t(qkv[at, hw : 2 * hw], q_head)
        key_row = lax.broadcasted_iota(jnp.int32, (full, 1), 0)
        visible = key_row < lengths_s[d * n_seq + j]
        return q_head, jnp.where(visible, raw * scale2, MASKED)

    def attention(j):
        at = pl.ds(j * full, full)
        kt[...] = jnp.transpose(qkv[at, 2 * hw : 3 * hw])

        def head(h, carry):
            span = pl.ds(al(h * HEAD_DIM, HEAD_DIM), HEAD_DIM)
            _, scores = head_scores(j, h, at)
            top = jnp.max(scores, axis=0, keepdims=True)
            e = jnp.exp2(scores - top)
            total = jnp.sum(e, axis=0, keepdims=True)
            o = mm(kt[span, :], e.astype(BF))
            ot[span, :] = o * (1.0 / total)
            lse[j, pl.ds(h, 1), :] = top + jnp.log2(total)
            return carry

        lax.fori_loop(0, heads, head, 0)
        att[at, :] = jnp.transpose(ot[...]).astype(BF)

    def project_out(j):
        def part_rows(start):
            def go(n):
                part[pl.ds(start, half), pl.ds(n, tile)] = mm(
                    att[pl.ds(start, half), :], wo_all[:, pl.ds(n, tile)]
                ).astype(BF)

            by_tiles(width, go)

        two_halves(R1, j, part_rows)

    def norm_first(j):
        def go(r):
            loc = seq_rows(j, t * quarter + r, chunk)
            buf = pl.ds(al(j * quarter + r, 16), chunk)
            h = x_all[loc, :].astype(F32) + (summed(j, r) + vec[2:3, :])
            center = h - jnp.mean(h, axis=-1, keepdims=True)
            inv = lax.rsqrt(jnp.mean(center * center, axis=-1, keepdims=True) + EPSILON)
            scaled = center * inv
            n1[buf, :] = scaled
            inv1[buf, :] = jnp.broadcast_to(inv, (chunk, 128))
            u_all[loc, :] = (scaled * vec[6:7, :] + vec[3:4, :]).astype(BF)

        row_loop(go)

    def widen(j):
        at = pl.ds(j * full, full)

        def go(n):
            f = mm(u_all[at, :], we_all[:, pl.ds(n, tile)]) + ebias[0:1, pl.ds(n, tile)]
            cdf = 0.5 + 0.5 * lax.erf(f * (1.0 / math.sqrt(2.0)))
            hid[at, pl.ds(n, tile)] = (f * cdf).astype(BF)
            bell = jnp.exp2((f * f) * (-0.5 * LOG2E)) * (1.0 / math.sqrt(2.0 * math.pi))
            slope[at, pl.ds(n, tile)] = (cdf + f * bell).astype(BF)

        by_tiles(fw, go)

    def shrink_rows(j):
        def part_rows(start):
            def go(n):
                part[pl.ds(start, half), pl.ds(n, tile)] = mm(
                    hid[pl.ds(start, half), :], ws_all[:, pl.ds(n, tile)]
                ).astype(BF)

            by_tiles(width, go)

        two_halves(R2, j, part_rows)

    def norm_second(j):
        length = lengths_s[d * n_seq + j]

        def go(r):
            loc = seq_rows(j, t * quarter + r, chunk)
            buf = pl.ds(al(j * quarter + r, 16), chunk)
            u = n1[buf, :] * vec[6:7, :] + vec[3:4, :]
            total = u + (summed(j, r) + vec[4:5, :])
            center = total - jnp.mean(total, axis=-1, keepdims=True)
            inv = lax.rsqrt(jnp.mean(center * center, axis=-1, keepdims=True) + EPSILON)
            scaled = center * inv
            mixed_send[j, pl.ds(al(r, 16), chunk), :] = (scaled * vec[7:8, :] + vec[5:6, :]).astype(BF)
            place = t * quarter + r + lax.broadcasted_iota(jnp.int32, (chunk, 1), 0)
            valid = (place < length).astype(F32)
            e = cots[j, pl.ds(al(r, 16), chunk), :].astype(F32) * valid
            add_sum(5, e)
            add_sum(7, e * scaled)
            pushed = e * vec[7:8, :]
            first = jnp.mean(pushed, axis=-1, keepdims=True)
            second = jnp.mean(pushed * scaled, axis=-1, keepdims=True)
            grad = inv * (pushed - first - scaled * second)
            add_sum(4, grad)
            dy[buf, :] = grad
            dz[loc, :] = grad.astype(BF)

        row_loop(go)

    def rows_out(tag, j, count, src, dst):
        for o in range(1, n_dp):
            e = dp_to(o)
            link.send(
                (tag, j, o),
                src.at[pl.ds(j, count), pl.ds(al(e * rows, 16), rows)],
                dst.at[pl.ds(d * n_seq + j, count)],
                {"dp": e},
            )
        own_copies[tag, j] = link.local(
            src.at[pl.ds(j, count), pl.ds(al(d * rows, 16), rows)],
            dst.at[pl.ds(d * n_seq + j, count)],
        )

    def rows_in(tag, j, count, dst):
        own_copies.pop((tag, j)).wait()
        for o in range(1, n_dp):
            e = dp_from(o)
            link.arrived((tag, j, o), dst.at[pl.ds(e * n_seq + j, count)], {"dp": e})


    def widen_back(j):
        at = pl.ds(j * full, full)

        def go(n):
            spread = mm_t(dz[at, :], ws_all[pl.ds(n, tile), :])
            grad = (spread * slope[at, pl.ds(n, tile)].astype(F32)).astype(BF)
            slope[at, pl.ds(n, tile)] = grad
            hacc[0:1, pl.ds(n, tile)] += jnp.sum(grad.astype(F32), axis=0, keepdims=True)

        by_tiles(fw, go)

    def normed_rows(j):
        def part_rows(start):
            def go(n):
                part[pl.ds(start, half), pl.ds(n, tile)] = mm_t(
                    slope[pl.ds(start, half), :], we_all[pl.ds(n, tile), :]
                ).astype(BF)

            by_tiles(width, go)

        two_halves(R3, j, part_rows)

    def norm_first_back(j):
        def go(r):
            loc = seq_rows(j, t * quarter + r, chunk)
            buf = pl.ds(al(j * quarter + r, 16), chunk)
            du = dy[buf, :] + summed(j, r)
            scaled = n1[buf, :]
            add_sum(3, du)
            add_sum(6, du * scaled)
            pushed = du * vec[6:7, :]
            first = jnp.mean(pushed, axis=-1, keepdims=True)
            second = jnp.mean(pushed * scaled, axis=-1, keepdims=True)
            grad = inv1[buf, 0:1] * (pushed - first - scaled * second)
            add_sum(2, grad)
            dy[buf, :] = grad
            dh[loc, :] = grad.astype(BF)

        row_loop(go)

    def attention_back(j, between=None):
        at = pl.ds(j * full, full)
        da[...] = mm_t(dh[at, :], wo_all[...]).astype(BF)
        kt[...] = jnp.transpose(qkv[at, hw : 2 * hw])
        dk_acc[...] = jnp.zeros_like(dk_acc)
        dv_acc[...] = jnp.zeros_like(dv_acc)

        def head(h, carry):
            span = pl.ds(al(h * HEAD_DIM, HEAD_DIM), HEAD_DIM)
            q_head, scores = head_scores(j, h, at)
            da_head = jnp.where(lane_head == h, da[...], jnp.zeros((), BF))
            p = jnp.exp2(scores - lse[j, pl.ds(h, 1), :])
            dp = mm_t(qkv[at, 2 * hw : 3 * hw], da_head)
            inner = jnp.sum(p * dp, axis=0, keepdims=True)
            ds = (p * (dp - inner)).astype(BF)
            dv_acc[...] += mm(p.astype(BF), da_head)
            dk_acc[...] += mm(ds, q_head)
            ot[span, :] = mm(kt[span, :], ds)
            return carry

        lax.fori_loop(0, heads, head, 0)
        scale = 1.0 / math.sqrt(HEAD_DIM)
        grad_q = (jnp.transpose(ot[...]) * scale).astype(BF)
        grad_k = (dk_acc[...] * scale).astype(BF)
        grad_v = dv_acc[...].astype(BF)
        dqkv[at, 0:hw] = grad_q
        dqkv[at, hw : 2 * hw] = grad_k
        dqkv[at, 2 * hw : 3 * hw] = grad_v
        qacc[0:1, :] += jnp.sum(grad_q.astype(F32), axis=0, keepdims=True)
        qacc[1:2, :] += jnp.sum(grad_v.astype(F32), axis=0, keepdims=True)

    def token_rows(j):
        def part_rows(start):
            def go(n):
                total = None
                for w in range(3):
                    term = mm_t(
                        dqkv[pl.ds(start, half), w * hw : (w + 1) * hw],
                        w3_all[w, pl.ds(n, tile), :],
                    )
                    total = term if total is None else total + term
                part[pl.ds(start, half), pl.ds(n, tile)] = total.astype(BF)

            by_tiles(width, go)

        two_halves(R4, j, part_rows)

    def finish_rows(j):
        def go(r):
            buf = pl.ds(al(j * quarter + r, 16), chunk)
            back_send[j, pl.ds(al(r, 16), chunk), :] = (dy[buf, :] + summed(j, r)).astype(BF)

        row_loop(go)


    grads = {
        GS: (dz, hid, s.gs, s.gs_y, s.gs_z, out_gs),
        GE: (u_all, slope, s.ge, s.ge_y, s.ge_z, out_ge),
        GO: (dh, att, s.go, s.go_y, s.go_z, out_go),
        G3: (x_all, dqkv, s.g3, s.g3_y, s.g3_z, out_g3),
    }

    def owned(i):
        return pl.ds(al(i * dw, 16), dw)

    def grad_tile(name, k):
        left, right, whole, from_y, _, _ = grads[name]
        first = ((z + k) % n_z) * n_y
        both = pl.ds(al(first * dw, n_y * dw), n_y * dw)
        whole[both, :] = t_mm(left[:, both], right[...]).astype(BF)
        link.send(
            (name, OVER_Y, k),
            whole.at[owned(first + (1 - y))],
            from_y.at[owned(k)],
            {"dp": y_peer},
        )

    def grad_forward(name, k):
        _, _, whole, from_y, from_z, out = grads[name]
        mid = from_y.at[owned(k)]
        link.arrived((name, OVER_Y, k), mid, {"dp": y_peer})
        owner = ((z + k) % n_z) * n_y + y
        total = whole[owned(owner), :].astype(F32) + from_y[owned(k), :].astype(F32)
        if k < n_z - 1:
            link.arrived((name, OVER_Z, k + 1), from_z.at[owned(k)], {"dp": z_from(1)})
            total = total + from_z[owned(k), :].astype(F32)
        if k:
            from_y[owned(k), :] = total.astype(BF)
            link.send((name, OVER_Z, k), mid, from_z.at[owned(k - 1)], {"dp": z_to(1)})
        else:
            out[...] = total

    small_send, small_recv, small_t = s.small_send, s.small_recv, s.small_t

    def small_start():
        small_send[...] = jnp.zeros_like(small_send)
        for e in range(n_dp):
            small_send[e, 2:8, :] = acc[2:8, e * dw : (e + 1) * dw]
        for i in range(owners):
            e = t * owners + i
            small_send[e, 0:2, :] = qacc[0:2, i * dw : (i + 1) * dw]
            for r in range(ebias_rows):
                at = (i * ebias_rows + r) * dw
                small_send[e, 8 + r : 9 + r, :] = hacc[0:1, at : at + dw]
        for o in range(1, n_dp):
            e = dp_to(o)
            link.send((SMALL, o), small_send.at[e], small_recv.at[o], {"dp": e})

    def small_forward():
        total = small_send[d]
        for o in range(1, n_dp):
            link.arrived((SMALL, o), small_recv.at[o], {"dp": dp_from(o)})
            total = total + small_recv[o]
        small_t[t] = total
        for what, peer in ((NEAR, t_core), (FAR, t_far), (NEAR_ON, t_diag)):
            link.send((SMALL_T, what), small_t.at[t], small_t.at[t], {"tensor": peer})

    def small_finish():
        for what, peer in ((NEAR, t_core), (FAR, t_far), (NEAR_ON, t_diag)):
            link.arrived((SMALL_T, what), small_t.at[peer], {"tensor": peer})
        total = small_t[0]
        for i in range(1, n_t):
            total = total + small_t[i]
        out_small[...] = total


    tokens_start(0)
    gather_start(WV)
    gather_start(WK)
    gather_step(WV, RIGHT, 1)
    gather_start(WQ)
    gather_start(WO)
    gather_step(WK, LEFT, 1)
    gather_step(WV, RIGHT, 2)
    gather_step(WV, LEFT, 1)
    gather_step(WQ, RIGHT, 1)
    gather_step(WO, LEFT, 1)
    gather_start(PACK)
    tokens_start(1)
    gather_step(WQ, LEFT, 1)
    gather_step(WK, LEFT, 2)
    gather_step(WV, RIGHT, 3)
    gather_step(WK, RIGHT, 1)
    gather_step(WQ, LEFT, 2)
    gather_step(WO, LEFT, 2)
    gather_step(WO, RIGHT, 1)
    tokens_finish(0)
    ag_start(x_all, TX, 0)
    gather_step(WV, RIGHT, 4)
    tokens_start(2)
    gather_step(WQ, RIGHT, 2)
    gather_step(PACK, LEFT, 1)
    tokens_finish(1)
    ag_start(x_all, TX, 1)
    gather_step(WQ, LEFT, 3)
    ag_forward(x_all, TX, 0)
    gather_step(PACK, RIGHT, 1)
    gather_step(WO, LEFT, 3)
    gather_step(WO, RIGHT, 2)
    gather_step(WK, RIGHT, 2)
    gather_step(WK, LEFT, 3)
    gather_step(PACK, RIGHT, 2)
    gather_step(WV, LEFT, 2)
    ag_finish(x_all, TX, 0)
    gather_step(WQ, RIGHT, 3)
    gather_step(PACK, RIGHT, 3)
    gather_step(WO, LEFT, 4)
    gather_step(PACK, LEFT, 2)
    gather_start(WE0)
    tokens_finish(2)
    ag_start(x_all, TX, 2)
    gather_step(WO, RIGHT, 3)
    ag_forward(x_all, TX, 1)
    gather_ready(WO)
    gather_start(WE1)
    gather_start(WS1)
    gather_step(WK, LEFT, 4)
    gather_step(PACK, RIGHT, 4)
    gather_step(PACK, LEFT, 3)
    gather_ready(PACK)
    gather_step(WV, LEFT, 3)
    gather_step(WK, RIGHT, 3)
    gather_ready(WK)
    spread_vectors()
    gather_step(WQ, RIGHT, 4)
    gather_ready(WV)
    gather_ready(WQ)
    project(0)
    attention(0)
    project_out(0)
    ag_forward(x_all, TX, 2)
    ag_finish(x_all, TX, 1)
    gather_start(WS0)
    rs_forward(R1, 0)
    project(1)
    gather_step(WE0, RIGHT, 1)
    gather_step(WE0, LEFT, 1)
    ag_finish(x_all, TX, 2)
    project(2)
    attention(2)
    gather_step(WE1, RIGHT, 1)
    gather_step(WS1, LEFT, 1)
    project_out(2)
    gather_step(WS1, RIGHT, 1)
    gather_step(WE1, LEFT, 1)
    rs_forward(R1, 2)
    attention(1)
    gather_step(WS0, RIGHT, 1)
    gather_step(WS0, LEFT, 1)
    project_out(1)
    gather_step(WE0, RIGHT, 2)
    rs_forward(R1, 1)
    gather_step(WE0, LEFT, 2)
    gather_step(WE1, LEFT, 2)
    rs_finish(R1, 2)
    norm_first(2)
    ag_start(u_all, TU, 2)
    gather_step(WS1, LEFT, 2)
    gather_step(WS1, RIGHT, 2)
    gather_step(WS0, RIGHT, 2)
    gather_step(WE1, LEFT, 3)
    gather_step(WE1, RIGHT, 2)
    gather_step(WS1, RIGHT, 3)
    gather_step(WE0, RIGHT, 3)
    rs_finish(R1, 0)
    norm_first(0)
    ag_start(u_all, TU, 0)
    gather_step(WS1, LEFT, 3)
    ag_forward(u_all, TU, 2)
    gather_step(WS0, LEFT, 2)
    gather_step(WS0, RIGHT, 3)
    gather_step(WE1, RIGHT, 3)
    gather_step(WE1, LEFT, 4)
    ag_finish(u_all, TU, 2)
    rs_finish(R1, 1)
    norm_first(1)
    ag_start(u_all, TU, 1)
    gather_step(WE0, LEFT, 3)
    gather_step(WS1, LEFT, 4)
    gather_step(WE0, RIGHT, 4)
    cot_start()
    gather_ready(WE1)
    gather_ready(WE0)
    widen(2)
    ag_forward(u_all, TU, 0)
    gather_step(WS0, LEFT, 3)
    gather_ready(WS1)
    gather_step(WS0, RIGHT, 4)
    gather_ready(WS0)
    shrink_rows(2)
    rs_forward(R2, 2)
    ag_finish(u_all, TU, 0)
    widen(0)
    ag_forward(u_all, TU, 1)
    shrink_rows(0)
    rs_forward(R2, 0)
    ag_finish(u_all, TU, 1)
    widen(1)
    shrink_rows(1)
    rs_forward(R2, 1)
    cot_finish()
    rs_finish(R2, 0)
    norm_second(0)
    ag_start(dz, TZ, 0)
    rs_finish(R2, 2)
    norm_second(2)
    ag_start(dz, TZ, 2)
    ag_forward(dz, TZ, 0)
    rs_finish(R2, 1)
    norm_second(1)
    ag_start(dz, TZ, 1)
    rows_out(MIX, 0, n_seq, mixed_send, out_mixed)
    ag_finish(dz, TZ, 0)
    widen_back(0)
    ag_forward(dz, TZ, 2)
    normed_rows(0)
    ag_finish(dz, TZ, 2)
    rs_forward(R3, 0)
    ag_forward(dz, TZ, 1)
    widen_back(2)
    ag_finish(dz, TZ, 1)
    grad_tile(GS, 3)
    normed_rows(2)
    rs_forward(R3, 2)
    widen_back(1)
    grad_tile(GE, 3)
    rs_finish(R3, 0)
    norm_first_back(0)
    ag_start(dh, TH, 0)
    grad_forward(GS, 3)
    grad_tile(GE, 2)
    grad_tile(GS, 2)
    grad_tile(GE, 1)
    normed_rows(1)
    rs_finish(R3, 2)
    norm_first_back(2)
    ag_start(dh, TH, 2)
    grad_forward(GE, 3)
    ag_forward(dh, TH, 0)
    rs_forward(R3, 1)
    ag_finish(dh, TH, 0)
    attention_back(0)
    grad_forward(GE, 2)
    token_rows(0)
    ag_forward(dh, TH, 2)
    grad_tile(GS, 1)
    grad_forward(GS, 2)
    rs_finish(R3, 1)
    norm_first_back(1)
    ag_start(dh, TH, 1)
    ag_finish(dh, TH, 2)
    attention_back(2)
    grad_forward(GE, 1)
    grad_tile(GE, 0)
    ag_forward(dh, TH, 1)
    grad_forward(GS, 1)
    rs_forward(R4, 0)
    ag_finish(dh, TH, 1)
    rows_in(MIX, 0, n_seq, out_mixed)
    grad_tile(GO, 3)
    grad_tile(GO, 2)
    attention_back(1)
    grad_forward(GO, 3)
    grad_tile(G3, 3)
    grad_forward(GE, 0)
    rs_finish(R4, 0)
    finish_rows(0)
    rows_out(BACK, 0, 1, back_send, back_recv)
    token_rows(2)
    rs_forward(R4, 2)
    grad_tile(G3, 2)
    small_start()
    grad_tile(GO, 1)
    grad_forward(G3, 3)
    token_rows(1)
    grad_tile(G3, 1)
    grad_forward(GO, 2)
    rs_finish(R4, 2)
    finish_rows(2)
    rows_out(BACK, 2, 1, back_send, back_recv)
    grad_forward(G3, 2)
    grad_tile(G3, 0)
    grad_tile(GS, 0)
    rows_in(BACK, 0, 1, back_recv)
    rs_forward(R4, 1)
    small_forward()
    grad_forward(GO, 1)
    grad_tile(GO, 0)
    rs_finish(R4, 1)
    finish_rows(1)
    rows_out(BACK, 1, 1, back_send, back_recv)
    small_finish()
    grad_forward(G3, 1)
    rows_in(BACK, 2, 1, back_recv)
    grad_forward(GO, 0)
    grad_forward(GS, 0)
    grad_forward(G3, 0)
    rows_in(BACK, 1, 1, back_recv)
    link.drain()


def finish_kernel(
    ebias_rows,
    order_s,
    mixed,
    back,
    g3,
    go,
    ge,
    gs,
    small,
    out_mixed,
    out_back,
    out_g3,
    out_go,
    out_ge,
    out_gs,
    out_biases,
    out_gains,
    out_hidden,
):
    def move(k, carry):
        out_back[k] = back[order_s[k]]
        return carry

    lax.fori_loop(0, out_back.shape[0], move, 0)
    out_mixed[...] = mixed[...]
    width = out_g3.shape[2]
    for w in range(3):
        out_g3[w] = g3[:, w * width : (w + 1) * width]
    out_go[...] = jnp.transpose(go[...])
    out_gs[...] = jnp.transpose(gs[...])
    out_ge[...] = ge[...]
    out_biases[...] = small[0:6]
    out_gains[...] = small[6:8]
    out_hidden[...] = small[8 : 8 + ebias_rows]


def body(
    tokens,
    cotangent,
    lengths,
    order,
    triple_weight,
    output_weight,
    expand_weight,
    shrink_weight,
    biases,
    gains,
    expand_bias,
):
    n_dp, n_t = lax.axis_size("dp"), lax.axis_size("tensor")
    slots, _, rows, width = tokens.shape
    n_seq = slots // n_dp
    quarter = rows * n_dp
    full = quarter * n_t
    dw = triple_weight.shape[1]
    hw = triple_weight.shape[2]
    fw = expand_weight.shape[1]
    fits = (
        n_t == 4
        and n_dp % 4 == 0
        and rows % 16 == 0
        and dw % 128 == 0
        and hw % 128 == 0
        and n_seq == 3
        and expand_bias.shape[0] % dw == 0
        and n_dp % n_t == 0
    )
    if not fits:
        return plain_body(
            tokens,
            cotangent,
            lengths,
            order,
            triple_weight,
            output_weight,
            expand_weight,
            shrink_weight,
            biases,
            gains,
            expand_bias,
        )
    n_y = 2
    n_z = n_dp // n_y
    ebias_rows = expand_bias.shape[0] // dw
    all_rows = n_seq * full
    own_rows = n_seq * quarter
    vm = pltpu.VMEM
    scratch = dict(
        stage=vm((slots, rows, width), BF),
        x_all=vm((all_rows, width), BF),
        cots=vm((n_seq, quarter, width), BF),
        w3_all=vm((3, width, hw), BF),
        wo_all=vm((hw, width), BF),
        we_all=vm((width, fw), BF),
        ws_all=vm((fw, width), BF),
        pack_own=vm((16, dw), F32),
        vec=vm((16, width), F32),
        ebias=vm((8, fw), F32),
        qkv=vm((all_rows, 3 * hw), BF),
        att=vm((all_rows, hw), BF),
        lse=vm((n_seq, 8, full), F32),
        part=vm((all_rows, width), BF),
        r_a=vm((own_rows, width), BF),
        r_b=vm((own_rows, width), BF),
        r_x=vm((own_rows, width), BF),
        n1=vm((own_rows, width), F32),
        inv1=vm((own_rows, 128), F32),
        u_all=vm((all_rows, width), BF),
        hid=vm((all_rows, fw), BF),
        slope=vm((all_rows, fw), BF),
        dz=vm((all_rows, width), BF),
        dh=vm((all_rows, width), BF),
        dy=vm((own_rows, width), F32),
        dqkv=vm((all_rows, 3 * hw), BF),
        acc=vm((8, width), F32),
        hacc=vm((8, fw), F32),
        qacc=vm((8, hw), F32),
        kt=vm((hw, full), BF),
        ot=vm((hw, full), F32),
        dk_acc=vm((full, hw), F32),
        dv_acc=vm((full, hw), F32),
        da=vm((full, hw), BF),
        mixed_send=vm((n_seq, quarter, width), BF),
        back_send=vm((n_seq, quarter, width), BF),
        gs=vm((width, fw), BF),
        gs_y=vm((n_z * dw, fw), BF),
        gs_z=vm(((n_z - 1) * dw, fw), BF),
        ge=vm((width, fw), BF),
        ge_y=vm((n_z * dw, fw), BF),
        ge_z=vm(((n_z - 1) * dw, fw), BF),
        go=vm((width, hw), BF),
        go_y=vm((n_z * dw, hw), BF),
        go_z=vm(((n_z - 1) * dw, hw), BF),
        g3=vm((width, 3 * hw), BF),
        g3_y=vm((n_z * dw, 3 * hw), BF),
        g3_z=vm(((n_z - 1) * dw, 3 * hw), BF),
        small_send=vm((n_dp, 16, dw), F32),
        small_recv=vm((n_dp, 16, dw), F32),
        small_t=vm((n_t, 16, dw), F32),
        send_sems=pltpu.SemaphoreType.DMA((N_SEM,)),
        recv_sems=pltpu.SemaphoreType.DMA((N_SEM,)),
        local_sems=pltpu.SemaphoreType.DMA((24,)),
    )
    g = types.SimpleNamespace(
        n_seq=n_seq,
        quarter=quarter,
        width=width,
        n_dp=n_dp,
        n_y=n_y,
        n_t=n_t,
        head_width=hw,
        hidden_width=fw,
        ebias_rows=ebias_rows,
        scratch_names=tuple(scratch),
    )
    smem = pl.BlockSpec(memory_space=pltpu.SMEM)
    vmem = pl.BlockSpec(memory_space=pltpu.VMEM)
    anywhere = pl.BlockSpec(memory_space=pl.ANY)
    sds = jax.ShapeDtypeStruct
    flops = 2 * all_rows * (3 * width * 3 * hw + 3 * width * hw + 6 * width * fw + 7 * full * hw)
    mixed, back, g3, go, ge, gs, small = pl.pallas_call(
        functools.partial(layer_kernel, g),
        out_shape=(
            sds(tokens.shape[:1] + (rows, width), BF),
            sds(tokens.shape[:1] + (rows, width), BF),
            sds((dw, 3 * hw), F32),
            sds((dw, hw), F32),
            sds((dw, fw), F32),
            sds((dw, fw), F32),
            sds((16, dw), F32),
        ),
        in_specs=[smem] * 2 + [vmem] + [anywhere] * 5 + [vmem] * 3,
        out_specs=[anywhere] * 2 + [vmem] * 5,
        scratch_shapes=list(scratch.values()),
        compiler_params=pltpu.CompilerParams(
            collective_id=0,
            has_side_effects=True,
            vmem_limit_bytes=VMEM_BYTES,
        ),
        cost_estimate=pl.CostEstimate(flops=flops, bytes_accessed=1 << 24, transcendentals=0),
    )(
        order,
        lengths,
        tokens.reshape(slots, rows, width),
        cotangent.reshape(slots, rows, width),
        triple_weight,
        output_weight,
        expand_weight,
        shrink_weight,
        biases,
        gains,
        expand_bias.reshape(ebias_rows, dw),
    )
    finals = pl.pallas_call(
        functools.partial(finish_kernel, ebias_rows),
        out_shape=(
            sds(mixed.shape, BF),
            sds(back.shape, BF),
            sds((3, dw, hw), F32),
            sds((hw, dw), F32),
            sds((dw, fw), F32),
            sds((fw, dw), F32),
            sds((6, dw), F32),
            sds((2, dw), F32),
            sds((ebias_rows, dw), F32),
        ),
        in_specs=[smem] + [vmem] * 7,
        out_specs=[vmem] * 9,
        compiler_params=pltpu.CompilerParams(vmem_limit_bytes=VMEM_BYTES),
    )(order, mixed, back, g3, go, ge, gs, small)
    return (
        finals[0].reshape(tokens.shape),
        finals[1].reshape(tokens.shape),
        *finals[2:8],
        finals[8].reshape(expand_bias.shape),
    )


def solution(mesh):
    return jax.shard_map(
        body,
        mesh=mesh,
        in_specs=(
            P(None, "tensor", "dp", None),
            P(None, "tensor", "dp", None),
            P(),
            P(),
            P(None, "dp", "tensor"),
            P(None, "dp"),
            P("dp", "tensor"),
            P("tensor", "dp"),
            P(None, "dp"),
            P(None, "dp"),
            P("dp"),
        ),
        out_specs=(
            P(None, "tensor", "dp", None),
            P(None, "tensor", "dp", None),
            P(None, "dp", "tensor"),
            P("tensor", "dp"),
            P("dp", "tensor"),
            P("tensor", "dp"),
            P(None, "dp"),
            P(None, "dp"),
            P("dp"),
        ),
        check_vma=False,
    )
```
